128 devices in a mesh: seq: 32 (over y, x_hi, z), head: 4 (over x_lo, core).
Axes of the slice: x: 4 (x_hi: 2, x_lo: 2; x = x_hi * 2 + x_lo), y: 4, z: 4, core: 2. Of those that a mesh axis runs over, the one named last changes fastest.
Arguments:
- hidden_in: bfloat16 [16384, 2048], P('seq'), may hold values from -6 to 6
- norm_gain_attn: bfloat16 [2048], P('seq'), may hold values from 0.099609375 to 1.8984375
- w_query: bfloat16 [2048, 2048], P('seq', 'head'), may hold values from -0.25 to 0.25
- w_key: bfloat16 [2048, 2048], P('seq', 'head'), may hold values from -0.125 to 0.125
- w_value: bfloat16 [2048, 2048], P('seq', 'head'), may hold values from -0.125 to 0.125
- w_out: bfloat16 [2048, 2048], P('head', 'seq'), may hold values from -0.5 to 0.5
- norm_gain_mlp: bfloat16 [2048], P('seq'), may hold values from 0.099609375 to 1.8984375
- w_gate: bfloat16 [2048, 5504], P('seq', 'head'), may hold values from -0.125 to 0.125
- w_up: bfloat16 [2048, 5504], P('seq', 'head'), may hold values from -0.125 to 0.125
- w_down: bfloat16 [5504, 2048], P('head', 'seq'), may hold values from -0.078125 to 0.078125
- lengths: int32 [3], replicated, may hold values from 1 to 15872, as said below
- cotangent: bfloat16 [16384, 2048], P('seq'), may hold values from -6 to 6
Outputs:
- output: bfloat16 [16384, 2048], P('seq')
- input_grad: bfloat16 [16384, 2048], P('seq')
- grad_gain_attn: float32 [2048], P('seq')
- grad_query: float32 [2048, 2048], P('seq', 'head')
- grad_key: float32 [2048, 2048], P('seq', 'head')
- grad_value: float32 [2048, 2048], P('seq', 'head')
- grad_out: float32 [2048, 2048], P('head', 'seq')
- grad_gain_mlp: float32 [2048], P('seq')
- grad_gate: float32 [2048, 5504], P('seq', 'head')
- grad_up: float32 [2048, 5504], P('seq', 'head')
- grad_down: float32 [5504, 2048], P('head', 'seq')
The draws below stay inside these ranges and needn't reach their ends.
Inputs may be any that keep to these rules, and one draw needn't show every extreme that they name: The lengths sum to 16384; the middle one is 15872 and the outer two add up to 512.
All inputs are finite; a program needn't handle non-finite values.
Results may differ from the reference program's by a relative error of at most 0.029.
Values may be sent and summed in bfloat16 or wider, within the bound.
A program may use at most 192 MiB of HBM per device.

```python
import jax
import jax.numpy as jnp
from jax import lax

D = 2048
HEADS = 16
HEAD_DIM = 128
FF = 5504
WINDOW = 64
TOK_DEV = 512
TOKENS = 16384


def draw_lengths(key, part):
    key = jax.random.fold_in(key, 7)
    first = jax.random.randint(key, (1,), 1, TOK_DEV).astype(jnp.int32)
    middle = jnp.full((1,), TOKENS - TOK_DEV, jnp.int32)
    return jnp.concatenate([first, middle, TOK_DEV - first]).astype(jnp.int32)


def with_spikes(values, stream_key, source, target, blocks, factor):
    def block_of(position):
        return (jnp.arange(values.shape[position]) // (values.shape[position] // blocks)).reshape((-1,) + (1,) * (values.ndim - 1 - position))

    one_side = jax.random.permutation(stream_key, blocks)[block_of(target)]
    second = (block_of(target) + blocks // 2) % blocks
    return jnp.where((block_of(source) == one_side) | (block_of(source) == second), factor * values, values)


def steps_of(rng, dims, split, low, largest):
    def one(dim, blocks):
        draws = jax.random.uniform(jax.random.fold_in(jax.random.fold_in(rng, 6), dim), (blocks,), jnp.float32, low / len(split), largest / len(split))
        return jnp.repeat(jnp.exp(draws), dims[dim] // blocks).reshape((-1,) + (1,) * (len(dims) - dim - 1))

    factor_of = one(*split[0])
    for cut in split[1:]:
        factor_of = factor_of * one(*cut)
    return factor_of


def scatter_about(stream_key, shape, spread, limit, cuts=(), kind=jnp.bfloat16):
    values = jax.random.normal(stream_key, shape, jnp.float32) * spread
    if len(cuts) > 0:
        values = steps_of(stream_key, shape, cuts, -0.22, 0.18) * values
    return jnp.clip(values, min=-limit, max=limit).astype(kind)


def noise_with(key, dims, scale, bound, split, heavy, held_as=jnp.bfloat16):
    values = scale * jax.random.normal(key, dims, jnp.float32)
    if split:
        values = values * steps_of(key, dims, split, -0.22, 0.18)
    return jnp.clip(with_spikes(values, jax.random.fold_in(key, 3), *heavy), -bound, bound).astype(held_as)


def setup_inputs(seed: int = 0) -> dict:
    arg_keys = jax.random.split(jax.random.key(seed), 13)
    return {
        "hidden_in": scatter_about(arg_keys[0], (TOKENS, D), 1.0, 6.0, ((0, 32),)),
        "norm_gain_attn": jnp.clip(1.0 + 0.18 * jax.random.normal(arg_keys[1], (D,), jnp.float32), 0.099609375, 1.8984375).astype(jnp.bfloat16),
        "w_query": scatter_about(arg_keys[2], (D, D), (D // 4) ** -0.5, 0.25, ((0, 32), (1, 4))),
        "w_key": scatter_about(arg_keys[3], (D, D), D ** -0.5, 0.125, ((0, 32), (1, 4))),
        "w_value": scatter_about(arg_keys[4], (D, D), D ** -0.5, 0.125, ((0, 32), (1, 4))),
        "w_out": scatter_about(arg_keys[5], (D, D), (D // 16) ** -0.5, 0.5, ((0, 4), (1, 32))),
        "norm_gain_mlp": jnp.clip(1.0 + 0.18 * jax.random.normal(arg_keys[6], (D,), jnp.float32), 0.099609375, 1.8984375).astype(jnp.bfloat16),
        "w_gate": scatter_about(arg_keys[7], (D, FF), D ** -0.5, 0.125, ((0, 32), (1, 4))),
        "w_up": scatter_about(arg_keys[8], (D, FF), D ** -0.5, 0.125, ((0, 32), (1, 4))),
        "w_down": scatter_about(arg_keys[9], (FF, D), FF ** -0.5, 0.078125, ((0, 4), (1, 32))),
        "lengths": draw_lengths(jax.random.fold_in(arg_keys[12], 71), 0),
        "cotangent": noise_with(arg_keys[11], (TOKENS, D), 1.0, 6.0, ((0, 32),), (0, 1, 32, 2.75)),
    }


epsilon = 1e-05
masked_score = -1e+30

@jax.custom_vjp
def low(v):
    return lax.optimization_barrier(v.astype(jnp.bfloat16)).astype(jnp.float32)

@jax.custom_vjp
def low_back(v):
    return v

def low_keep(v):
    return (low(v), None)

def low_pass(kept, grad):
    return (grad,)

def back_keep(v):
    return (v, None)

def back_low(kept, grad):
    return (low(grad),)
low.defvjp(low_keep, low_pass)
low_back.defvjp(back_keep, back_low)

def matmul_high(left, right):
    return jnp.dot(left, right, precision=lax.Precision.HIGHEST)

def rms_scale(values, gain):
    return values * lax.rsqrt(lax.optimization_barrier(jnp.mean(values * values, axis=-1, keepdims=True)) + epsilon) * gain

def band_blocks(array):
    shaped = array.reshape((array.shape[0] // WINDOW, WINDOW) + array.shape[1:])
    return jnp.concatenate([shaped[:-1], shaped[1:]], axis=1)

def segment_ids(lengths):
    ends = jnp.cumsum(lengths).astype(jnp.int32)
    positions = jnp.arange(TOKENS, dtype=jnp.int32)
    return lax.optimization_barrier(jnp.sum((positions[None, :] >= ends[:, None]).astype(jnp.int32), axis=0)).astype(jnp.int32)

def attention(queries, keys, values, segment):
    count = TOKENS // WINDOW
    front = jnp.zeros((WINDOW, D), jnp.float32)
    key_blocks = band_blocks(jnp.concatenate([front, keys])).reshape(count, 2 * WINDOW, HEADS, HEAD_DIM)
    value_blocks = band_blocks(jnp.concatenate([front, values])).reshape(count, 2 * WINDOW, HEADS, HEAD_DIM)
    query_blocks = queries.reshape(count, WINDOW, HEADS, HEAD_DIM)
    positions = jnp.arange(TOKENS + WINDOW, dtype=jnp.int32) - WINDOW
    key_pos = band_blocks(positions)
    key_seg = band_blocks(jnp.concatenate([jnp.zeros((WINDOW,), jnp.int32), segment]))
    query_pos = positions[WINDOW:].reshape(count, WINDOW)
    query_seg = segment.reshape(count, WINDOW)
    visible = (key_pos[:, None, :] <= query_pos[:, :, None]) & (key_pos[:, None, :] > query_pos[:, :, None] - WINDOW)
    visible = visible & (key_pos[:, None, :] >= 0) & (key_seg[:, None, :] == query_seg[:, :, None])
    scores = jnp.einsum('bqhd,bkhd->bhqk', query_blocks, key_blocks, precision=lax.Precision.HIGHEST) * HEAD_DIM ** (-0.5)
    scores = low_back(scores)
    scores = jnp.where(visible[:, None], scores, masked_score)
    probs = low(jax.nn.softmax(scores, axis=-1))
    mixed = jnp.einsum('bhqk,bkhd->bqhd', probs, value_blocks, precision=lax.Precision.HIGHEST)
    return mixed.reshape(TOKENS, D)

def forward(hidden, gain_attn, query_w, key_w, value_w, out_w, gain_mlp, gate_w, up_w, down_w, segment):
    normed_attn = low(rms_scale(hidden, gain_attn))
    queries = low(low_back(matmul_high(normed_attn, query_w)))
    keys = low(low_back(matmul_high(normed_attn, key_w)))
    values = low(low_back(matmul_high(normed_attn, value_w)))
    mixed = low(low_back(attention(queries, keys, values, segment)))
    branch = low_back(matmul_high(mixed, out_w))
    resid = hidden + branch
    normed_mlp = low(rms_scale(resid, gain_mlp))
    gate = low_back(matmul_high(normed_mlp, gate_w))
    up = low_back(matmul_high(normed_mlp, up_w))
    activated = low(jax.nn.silu(gate) * up)
    result = low_back(matmul_high(activated, down_w))
    return resid + result

def reference(hidden_in, norm_gain_attn, w_query, w_key, w_value, w_out, norm_gain_mlp, w_gate, w_up, w_down, lengths, cotangent):
    segment = segment_ids(lengths)
    floats = tuple((array.astype(jnp.float32) for array in (hidden_in, norm_gain_attn, w_query, w_key, w_value, w_out, norm_gain_mlp, w_gate, w_up, w_down)))
    result, pullback = jax.vjp(lambda *items: forward(*items, segment), *floats)
    grads = pullback(cotangent.astype(jnp.float32))
    return (result.astype(jnp.bfloat16), grads[0].astype(jnp.bfloat16), grads[1], grads[2], grads[3], grads[4], grads[5], grads[6], grads[7], grads[8], grads[9])
```

```python
import jax
import jax.numpy as jnp
from jax import lax
from jax.sharding import Mesh, PartitionSpec as P

HEAD_DIM = 128
WINDOW = 64
BLOCK = 512
OWNED = 128
AXES = ("y", "xh", "z", "xl", "c")
RING = ("xh", "xl")

epsilon = 1e-05
masked_score = -1e30
f32 = jnp.float32
bf16 = jnp.bfloat16


def shift(value, axis, steps):
    return lax.ppermute(value, axis, [(i, (i + steps) % 4) for i in range(4)])


def flip(value, axis):
    return lax.ppermute(value, axis, [(0, 1), (1, 0)])


def dot_plain(left, right):
    return jnp.dot(left, right, preferred_element_type=f32)


def dot_right_turned(left, right):
    return lax.dot_general(left, right, (((1,), (1,)), ((), ())), preferred_element_type=f32)


def dot_left_turned(left, right):
    return lax.dot_general(left, right, (((0,), (0,)), ((), ())), preferred_element_type=f32)


def rms_scale(values, gain):
    return values * lax.rsqrt(jnp.mean(values * values, axis=-1, keepdims=True) + epsilon) * gain


def in_order(flag, mine, other, axis):
    return jnp.where(
        flag == 0,
        jnp.concatenate([mine, other], axis=axis),
        jnp.concatenate([other, mine], axis=axis),
    )


def pick(array, axis, index):
    return lax.dynamic_slice_in_dim(array, index, 1, axis)


def place(pieces, axis, index):
    shape = list(pieces[0].shape)
    shape[axis] = 4
    total = jnp.zeros(shape, pieces[0].dtype)
    for k, piece in enumerate(pieces):
        total = lax.dynamic_update_slice_in_dim(total, piece, (index + k) % 4, axis)
    return total


def gather4(block, mesh_axis, axis, split):
    index = lax.axis_index(mesh_axis)
    before = shift(block, mesh_axis, 1)
    after = shift(block, mesh_axis, -1)
    half = block.shape[split] // 2
    far = jnp.concatenate(
        [
            shift(lax.slice_in_dim(before, 0, half, axis=split), mesh_axis, 1),
            shift(lax.slice_in_dim(after, half, 2 * half, axis=split), mesh_axis, -1),
        ],
        axis=split,
    )
    return place([block, after, far, before], axis, index)


def reduce4(total, mesh_axis, axis, split):
    index = lax.axis_index(mesh_axis)
    half = total.shape[split] // 2
    own, nxt, far, prev = [pick(total, axis, (index + k) % 4) for k in range(4)]
    low = lambda a: lax.slice_in_dim(a, 0, half, axis=split)
    high = lambda a: lax.slice_in_dim(a, half, 2 * half, axis=split)
    add = lambda a, b: (a.astype(f32) + b.astype(f32)).astype(bf16)
    from_prev = shift(low(far), mesh_axis, 1)
    from_next = shift(high(far), mesh_axis, -1)
    from_prev_own = shift(high(nxt), mesh_axis, 1)
    from_next_own = shift(low(prev), mesh_axis, -1)
    from_prev_sum = shift(add(low(nxt), from_prev), mesh_axis, 1)
    from_next_sum = shift(add(high(prev), from_next), mesh_axis, -1)
    got_prev = jnp.concatenate([from_prev_sum, from_prev_own], axis=split)
    got_next = jnp.concatenate([from_next_own, from_next_sum], axis=split)
    return (own.astype(f32) + got_prev.astype(f32) + got_next.astype(f32)).astype(bf16)


def gather_weights(pack):
    cols = pack.shape[2]
    cut = cols // 256 * 128
    a = pack[None, :, None, :, :cut]
    b = pack[None, :, None, :, cut:]
    a = gather4(gather4(a, "z", 2, 3), "y", 0, 3)
    b = gather4(gather4(b, "y", 0, 3), "z", 2, 3)
    return a.reshape(2048, cut), b.reshape(2048, cols - cut)


def reduce_weights(a, b):
    a = a.reshape(4, 2, 4, 64, a.shape[1])
    b = b.reshape(4, 2, 4, 64, b.shape[1])
    a = reduce4(reduce4(a, "y", 0, 3), "z", 2, 3)
    b = reduce4(reduce4(b, "z", 2, 3), "y", 0, 3)
    return jnp.concatenate([a[0, :, 0], b[0, :, 0]], axis=2)


def gather_block(value):
    c = lax.axis_index("c")
    part = lax.dynamic_slice_in_dim(value, c * 256, 256, 0)
    got = lax.ppermute(part, RING, [(i, 3 - i) for i in range(4)])
    other = in_order(c, got, flip(got, "c"), 0)
    return in_order(lax.axis_index("xh"), value, other, 0)


def reduce_group(total):
    c = lax.axis_index("c")
    x = lax.axis_index(RING)
    parts = total.reshape(4, 2, OWNED, 2048)
    mine = pick(parts, 1, c)[:, 0]
    theirs = pick(parts, 1, 1 - c)[:, 0].astype(bf16)
    mine = mine + flip(theirs, "c").astype(f32)
    low = mine.astype(bf16)
    result = pick(mine, 0, x)[0]
    for k in (1, 3, 2):
        result = result + shift(pick(low, 0, (x + k) % 4)[0], RING, k).astype(f32)
    return result


def gather_group(owned):
    c = lax.axis_index("c")
    x = lax.axis_index(RING)
    mine = owned[None]
    pieces = [mine, shift(mine, RING, -1), shift(mine, RING, 2), shift(mine, RING, 1)]
    half = place(pieces, 0, x)[:, None]
    return in_order(c, half, flip(half, "c"), 1).reshape(1024, 2048)


def gather_owned(owned):
    pair = in_order(lax.axis_index("xl"), owned[None], flip(owned, "xl")[None], 0)[:, None]
    return in_order(lax.axis_index("c"), pair, flip(pair, "c"), 1).reshape(BLOCK, 2048)


def band_blocks(array):
    shaped = array.reshape((2, 9, WINDOW) + array.shape[2:])
    both = jnp.concatenate([shaped[:, :-1], shaped[:, 1:]], axis=2)
    return both.reshape((16, 2 * WINDOW) + array.shape[2:])


def fold_blocks(blocks):
    shaped = blocks.reshape(2, 8, 2, WINDOW, -1)
    edge = jnp.zeros((2, 1, WINDOW, shaped.shape[-1]), f32)
    total = jnp.concatenate([shaped[:, :, 0], edge], axis=1) + jnp.concatenate(
        [edge, shaped[:, :, 1]], axis=1
    )
    return total.reshape(2, 576, -1)


def visibility(lengths):
    y, z = lax.axis_index("y"), lax.axis_index("z")
    starts = (y * 8 + z + 4 * jnp.arange(2, dtype=jnp.int32)) * BLOCK
    positions = starts[:, None] - WINDOW + jnp.arange(BLOCK + WINDOW, dtype=jnp.int32)
    ends = jnp.cumsum(lengths)
    segment = jnp.sum((positions[..., None] >= ends).astype(jnp.int32), axis=-1)
    key_pos = band_blocks(positions)
    key_seg = band_blocks(segment)
    query_pos = positions[:, WINDOW:].reshape(16, WINDOW)
    query_seg = segment[:, WINDOW:].reshape(16, WINDOW)
    visible = (key_pos[:, None, :] <= query_pos[:, :, None]) & (
        key_pos[:, None, :] > query_pos[:, :, None] - WINDOW
    )
    return visible & (key_pos[:, None, :] >= 0) & (key_seg[:, None, :] == query_seg[:, :, None])


YZ = ("y", "z")


def tails_forward(tails):
    z = lax.axis_index("z")
    ring = shift(tails, "z", 1)
    step = lax.ppermute(tails[1], YZ, [(4 * y + 3, 4 * y + 4) for y in range(3)])
    return jnp.where(z == 0, jnp.stack([step, ring[0]]), ring)


def tails_back(heads):
    z = lax.axis_index("z")
    ring = shift(heads, "z", -1)
    step = lax.ppermute(heads[0], YZ, [(4 * y + 4, 4 * y + 3) for y in range(3)])
    return jnp.where(z == 3, jnp.stack([ring[1], step]), ring)


def score_blocks(query_blocks, key_blocks, visible):
    scores = jnp.einsum(
        "bqhd,bkhd->bhqk", query_blocks, key_blocks, preferred_element_type=f32
    ) * HEAD_DIM ** (-0.5)
    return jnp.where(visible[:, None], scores, masked_score)


def per_device(
    hidden_in,
    norm_gain_attn,
    w_query,
    w_key,
    w_value,
    w_out,
    norm_gain_mlp,
    w_gate,
    w_up,
    w_down,
    lengths,
    cotangent,
):
    xh, xl, c = lax.axis_index("xh"), lax.axis_index("xl"), lax.axis_index("c")

    def halves(w):
        n = w.shape[1] // 2
        return jnp.where(xh == 0, w[:, :n], w[:, n:]), jnp.where(xh == 0, w[:, n:], w[:, :n])

    def swap(pairs):
        mine = jnp.concatenate([p[0] for p in pairs], axis=1)
        theirs = jnp.concatenate([p[1] for p in pairs], axis=1)
        return in_order(xh, mine[None], flip(theirs, "xh")[None], 0)

    gains = jnp.stack([norm_gain_attn, norm_gain_mlp], axis=1)
    gains = jnp.pad(gains, ((0, 0), (0, 126)))
    attn_pack = swap([halves(w) for w in (w_query, w_key, w_value, w_out.T)] + [(gains, gains)])
    ff_pack = swap([halves(w) for w in (w_gate, w_up, w_down.T)])
    attn_a, attn_b = gather_weights(attn_pack)
    attn = jnp.concatenate([attn_a, attn_b], axis=1)
    qkv_w = attn[:, :768]
    out_w = attn[:, 768:1024]
    gain_attn = attn[:, 1024].astype(f32)
    gain_mlp = attn[:, 1025].astype(f32)

    hidden = gather_block(hidden_in)
    cot = gather_block(cotangent)
    q = xl * 2 + c
    owned_rows = lambda a: lax.dynamic_slice_in_dim(a, q * OWNED, OWNED, 0)
    hidden_owned = owned_rows(hidden_in).astype(f32)
    cot_owned = owned_rows(cotangent).astype(f32)

    ff_a, ff_b = gather_weights(ff_pack)
    ff = jnp.concatenate([ff_a, ff_b], axis=1)
    gate_w, up_w, down_w = ff[:, :688], ff[:, 688:1376], ff[:, 1376:]

    visible = visibility(lengths)
    normed_attn = rms_scale(hidden.astype(f32), gain_attn).astype(bf16)
    qkv = dot_plain(normed_attn, qkv_w).astype(bf16)
    queries = qkv[:, :256].reshape(16, WINDOW, 2, HEAD_DIM)
    kv = qkv[:, 256:].reshape(2, BLOCK, 512)
    kv_ext = jnp.concatenate([tails_forward(kv[:, -WINDOW:]), kv], axis=1)
    key_blocks = band_blocks(kv_ext[..., :256]).reshape(16, 2 * WINDOW, 2, HEAD_DIM)
    value_blocks = band_blocks(kv_ext[..., 256:]).reshape(16, 2 * WINDOW, 2, HEAD_DIM)
    scores = score_blocks(queries, key_blocks, visible)
    highest = jnp.max(scores, axis=-1, keepdims=True)
    expo = jnp.exp(scores - highest)
    probs = expo / jnp.sum(expo, axis=-1, keepdims=True)
    probs_low = probs.astype(bf16)
    mixed = jnp.einsum("bhqk,bkhd->bqhd", probs_low, value_blocks, preferred_element_type=f32)
    mixed = mixed.reshape(1024, 256).astype(bf16)
    resid = hidden_owned + reduce_group(dot_right_turned(mixed, out_w))
    normed_mlp = gather_group(rms_scale(resid, gain_mlp).astype(bf16))

    gate = dot_plain(normed_mlp, gate_w)
    up = dot_plain(normed_mlp, up_w)
    sig = 1 / (1 + jnp.exp(-gate))
    silu = gate * sig
    activated = (silu * up).astype(bf16)
    result = resid + reduce_group(dot_right_turned(activated, down_w))
    result = gather_owned(result.astype(bf16))

    grad_act = dot_plain(cot, down_w)
    grad_gate_act = (grad_act * up * sig * (1 + gate * (1 - sig))).astype(bf16)
    grad_up_act = (grad_act * silu).astype(bf16)
    grad_normed_mlp = reduce_group(
        dot_right_turned(grad_gate_act, gate_w) + dot_right_turned(grad_up_act, up_w)
    )
    grad_down = dot_left_turned(cot, activated).astype(bf16)
    grad_gate = dot_left_turned(normed_mlp, grad_gate_act).astype(bf16)
    grad_up = dot_left_turned(normed_mlp, grad_up_act).astype(bf16)
    grad_ff = jnp.concatenate([grad_gate, grad_up, grad_down], axis=1)
    grad_ff = reduce_weights(grad_ff[:, :1024], grad_ff[:, 1024:])

    def norm_back(grad, values, gain):
        r = lax.rsqrt(jnp.mean(values * values, axis=-1, keepdims=True) + epsilon)
        e = grad * gain
        back = r * e - values * r**3 * jnp.mean(e * values, axis=-1, keepdims=True)
        return back, jnp.sum(grad * values * r, axis=0)

    back, grad_gain_mlp = norm_back(grad_normed_mlp, resid, gain_mlp)
    grad_resid = cot_owned + back
    grad_branch = gather_group(grad_resid.astype(bf16))
    grad_out = dot_left_turned(grad_branch, mixed).astype(bf16)
    grad_mixed = dot_plain(grad_branch, out_w).astype(bf16).reshape(16, WINDOW, 2, HEAD_DIM)
    grad_probs = jnp.einsum("bqhd,bkhd->bhqk", grad_mixed, value_blocks, preferred_element_type=f32)
    inner = jnp.sum(probs * grad_probs, axis=-1, keepdims=True)
    grad_scores = (probs * (grad_probs - inner)).astype(bf16)
    scale = HEAD_DIM ** (-0.5)
    grad_queries = (
        jnp.einsum("bhqk,bkhd->bqhd", grad_scores, key_blocks, preferred_element_type=f32) * scale
    )
    grad_keys = (
        jnp.einsum("bhqk,bqhd->bkhd", grad_scores, queries, preferred_element_type=f32) * scale
    )
    grad_values = jnp.einsum("bhqk,bqhd->bkhd", probs_low, grad_mixed, preferred_element_type=f32)
    grad_kv = jnp.concatenate([fold_blocks(grad_keys), fold_blocks(grad_values)], axis=-1)
    returned = tails_back(grad_kv[:, :WINDOW].astype(bf16)).astype(f32)
    grad_kv = jnp.concatenate(
        [grad_kv[:, WINDOW:BLOCK], grad_kv[:, BLOCK:] + returned], axis=1
    ).reshape(1024, 512)
    grad_qkv_act = jnp.concatenate([grad_queries.reshape(1024, 256), grad_kv], axis=1).astype(bf16)
    grad_normed_attn = reduce_group(dot_right_turned(grad_qkv_act, qkv_w))
    grad_qkv = dot_left_turned(normed_attn, grad_qkv_act).astype(bf16)
    back, grad_gain_attn = norm_back(grad_normed_attn, hidden_owned, gain_attn)
    input_grad = gather_owned((grad_resid + back).astype(bf16))

    grad_gains = jnp.stack([grad_gain_attn, grad_gain_mlp], axis=1)
    grad_gains = jnp.pad(grad_gains, ((0, 0), (0, 126))).astype(bf16)
    grad_attn = jnp.concatenate([grad_qkv, grad_out, grad_gains], axis=1)
    grad_attn = reduce_weights(grad_attn[:, :512], grad_attn[:, 512:])

    def unswap(pack):
        mine = pick(pack, 0, xh)[0]
        return mine, flip(pick(pack, 0, 1 - xh)[0], "xh")

    mine_a, other_a = unswap(grad_attn)
    mine_f, other_f = unswap(grad_ff)

    def whole(mine, other, start, width):
        return in_order(xh, mine[:, start : start + width], other[:, start : start + width], 1).astype(f32)

    grads_gain = mine_a[:, 1024:1026].astype(f32) + other_a[:, 1024:1026].astype(f32)
    grads_gain = grads_gain + flip(grads_gain, "xl")
    grads_gain = grads_gain + flip(grads_gain, "c")
    return (
        result,
        input_grad,
        grads_gain[:, 0],
        whole(mine_a, other_a, 0, 256),
        whole(mine_a, other_a, 256, 256),
        whole(mine_a, other_a, 512, 256),
        whole(mine_a, other_a, 768, 256).T,
        grads_gain[:, 1],
        whole(mine_f, other_f, 0, 688),
        whole(mine_f, other_f, 688, 688),
        whole(mine_f, other_f, 1376, 688).T,
    )


def solution(mesh):
    mesh = Mesh(mesh.devices.reshape(4, 2, 4, 2, 2), AXES)
    seq, head = ("y", "xh", "z"), ("xl", "c")
    rows, cols, flat, turned = P(seq, None), P(seq, head), P(seq), P(head, seq)
    return jax.shard_map(
        per_device,
        mesh=mesh,
        in_specs=(rows, flat, cols, cols, cols, turned, flat, cols, cols, turned, P(), rows),
        out_specs=(rows, rows, flat, cols, cols, cols, turned, flat, cols, cols, turned),
        check_vma=False,
    )
```

```python
import functools

import jax
import jax.numpy as jnp
from jax import lax
from jax.experimental import pallas as pl
from jax.experimental.pallas import tpu as pltpu
from jax.sharding import Mesh, PartitionSpec as P

HEAD_DIM = 128
WINDOW = 64
BLOCK = 512
OWNED = 128
AXES = ("y", "xh", "z", "xl", "c")
RING = ("xh", "xl")

epsilon = 1e-05
masked_score = -1e30
f32 = jnp.float32
bf16 = jnp.bfloat16


def shift(value, axis, steps):
    return lax.ppermute(value, axis, [(i, (i + steps) % 4) for i in range(4)])


def flip(value, axis):
    return lax.ppermute(value, axis, [(0, 1), (1, 0)])


def dot_plain(left, right):
    return jnp.dot(left, right, preferred_element_type=f32)


def dot_right_turned(left, right):
    return lax.dot_general(left, right, (((1,), (1,)), ((), ())), preferred_element_type=f32)


def dot_left_turned(left, right):
    return lax.dot_general(left, right, (((0,), (0,)), ((), ())), preferred_element_type=f32)


def rms_scale(values, gain):
    return values * lax.rsqrt(jnp.mean(values * values, axis=-1, keepdims=True) + epsilon) * gain


def in_order(flag, mine, other, axis):
    return jnp.where(
        flag == 0,
        jnp.concatenate([mine, other], axis=axis),
        jnp.concatenate([other, mine], axis=axis),
    )


def pick(array, axis, index):
    return lax.dynamic_slice_in_dim(array, index, 1, axis)


def place(pieces, axis, index):
    shape = list(pieces[0].shape)
    shape[axis] = 4
    total = jnp.zeros(shape, pieces[0].dtype)
    for k, piece in enumerate(pieces):
        total = lax.dynamic_update_slice_in_dim(total, piece, (index + k) % 4, axis)
    return total


def gather4(block, mesh_axis, axis, split):
    index = lax.axis_index(mesh_axis)
    before = shift(block, mesh_axis, 1)
    after = shift(block, mesh_axis, -1)
    half = block.shape[split] // 2
    far = jnp.concatenate(
        [
            shift(lax.slice_in_dim(before, 0, half, axis=split), mesh_axis, 1),
            shift(lax.slice_in_dim(after, half, 2 * half, axis=split), mesh_axis, -1),
        ],
        axis=split,
    )
    return place([block, after, far, before], axis, index)


def reduce4(total, mesh_axis, axis, split):
    index = lax.axis_index(mesh_axis)
    half = total.shape[split] // 2
    own, nxt, far, prev = [pick(total, axis, (index + k) % 4) for k in range(4)]
    low = lambda a: lax.slice_in_dim(a, 0, half, axis=split)
    high = lambda a: lax.slice_in_dim(a, half, 2 * half, axis=split)
    add = lambda a, b: (a.astype(f32) + b.astype(f32)).astype(bf16)
    from_prev = shift(low(far), mesh_axis, 1)
    from_next = shift(high(far), mesh_axis, -1)
    from_prev_own = shift(high(nxt), mesh_axis, 1)
    from_next_own = shift(low(prev), mesh_axis, -1)
    from_prev_sum = shift(add(low(nxt), from_prev), mesh_axis, 1)
    from_next_sum = shift(add(high(prev), from_next), mesh_axis, -1)
    got_prev = jnp.concatenate([from_prev_sum, from_prev_own], axis=split)
    got_next = jnp.concatenate([from_next_own, from_next_sum], axis=split)
    return (own.astype(f32) + got_prev.astype(f32) + got_next.astype(f32)).astype(bf16)


def gather_weights(pack):
    cols = pack.shape[2]
    cut = cols // 256 * 128
    a = pack[None, :, None, :, :cut]
    b = pack[None, :, None, :, cut:]
    a = gather4(gather4(a, "z", 2, 3), "y", 0, 3)
    b = gather4(gather4(b, "y", 0, 3), "z", 2, 3)
    return a.reshape(2048, cut), b.reshape(2048, cols - cut)


def reduce_weights(a, b):
    a = a.reshape(4, 2, 4, 64, a.shape[1])
    b = b.reshape(4, 2, 4, 64, b.shape[1])
    a = reduce4(reduce4(a, "y", 0, 3), "z", 2, 3)
    b = reduce4(reduce4(b, "z", 2, 3), "y", 0, 3)
    return jnp.concatenate([a[0, :, 0], b[0, :, 0]], axis=2)


def gather_block(value):
    c = lax.axis_index("c")
    part = lax.dynamic_slice_in_dim(value, c * 256, 256, 0)
    got = lax.ppermute(part, RING, [(i, 3 - i) for i in range(4)])
    other = in_order(c, got, flip(got, "c"), 0)
    return in_order(lax.axis_index("xh"), value, other, 0)


def reduce_group(total):
    c = lax.axis_index("c")
    x = lax.axis_index(RING)
    parts = total.reshape(4, 2, OWNED, 2048)
    mine = pick(parts, 1, c)[:, 0]
    theirs = pick(parts, 1, 1 - c)[:, 0].astype(bf16)
    mine = mine + flip(theirs, "c").astype(f32)
    low = mine.astype(bf16)
    result = pick(mine, 0, x)[0]
    for k in (1, 3, 2):
        result = result + shift(pick(low, 0, (x + k) % 4)[0], RING, k).astype(f32)
    return result


def gather_group(owned):
    c = lax.axis_index("c")
    x = lax.axis_index(RING)
    mine = owned[None]
    pieces = [mine, shift(mine, RING, -1), shift(mine, RING, 2), shift(mine, RING, 1)]
    half = place(pieces, 0, x)[:, None]
    return in_order(c, half, flip(half, "c"), 1).reshape(1024, 2048)


def gather_owned(owned):
    pair = in_order(lax.axis_index("xl"), owned[None], flip(owned, "xl")[None], 0)[:, None]
    return in_order(lax.axis_index("c"), pair, flip(pair, "c"), 1).reshape(BLOCK, 2048)


def band_blocks(array):
    shaped = array.reshape((2, 9, WINDOW) + array.shape[2:])
    both = jnp.concatenate([shaped[:, :-1], shaped[:, 1:]], axis=2)
    return both.reshape((16, 2 * WINDOW) + array.shape[2:])


def fold_blocks(blocks):
    shaped = blocks.reshape(2, 8, 2, WINDOW, -1)
    edge = jnp.zeros((2, 1, WINDOW, shaped.shape[-1]), f32)
    total = jnp.concatenate([shaped[:, :, 0], edge], axis=1) + jnp.concatenate(
        [edge, shaped[:, :, 1]], axis=1
    )
    return total.reshape(2, 576, -1)


def visibility(lengths):
    y, z = lax.axis_index("y"), lax.axis_index("z")
    starts = (y * 8 + z + 4 * jnp.arange(2, dtype=jnp.int32)) * BLOCK
    positions = starts[:, None] - WINDOW + jnp.arange(BLOCK + WINDOW, dtype=jnp.int32)
    ends = jnp.cumsum(lengths)
    segment = jnp.sum((positions[..., None] >= ends).astype(jnp.int32), axis=-1)
    key_pos = band_blocks(positions)
    key_seg = band_blocks(segment)
    query_pos = positions[:, WINDOW:].reshape(16, WINDOW)
    query_seg = segment[:, WINDOW:].reshape(16, WINDOW)
    visible = (key_pos[:, None, :] <= query_pos[:, :, None]) & (
        key_pos[:, None, :] > query_pos[:, :, None] - WINDOW
    )
    return visible & (key_pos[:, None, :] >= 0) & (key_seg[:, None, :] == query_seg[:, :, None])


YZ = ("y", "z")


def tails_forward(tails):
    z = lax.axis_index("z")
    ring = shift(tails, "z", 1)
    step = lax.ppermute(tails[1], YZ, [(4 * y + 3, 4 * y + 4) for y in range(3)])
    return jnp.where(z == 0, jnp.stack([step, ring[0]]), ring)


def tails_back(heads):
    z = lax.axis_index("z")
    ring = shift(heads, "z", -1)
    step = lax.ppermute(heads[0], YZ, [(4 * y + 4, 4 * y + 3) for y in range(3)])
    return jnp.where(z == 3, jnp.stack([ring[1], step]), ring)


def score_blocks(query_blocks, key_blocks, visible):
    scores = jnp.einsum(
        "bqhd,bkhd->bhqk", query_blocks, key_blocks, preferred_element_type=f32
    ) * HEAD_DIM ** (-0.5)
    return jnp.where(visible[:, None], scores, masked_score)


MESH = pl.DeviceIdType.MESH
SCALE = HEAD_DIM ** (-0.5)
ANY = pl.BlockSpec(memory_space=pl.ANY)
TURNED = (((1,), (1,)), ((), ()))
LEFT_TURNED = (((0,), (0,)), ((), ()))


class Place:
    def __init__(self):
        self.y, self.z, self.c = lax.axis_index("y"), lax.axis_index("z"), lax.axis_index("c")
        self.xh, self.xl = lax.axis_index("xh"), lax.axis_index("xl")
        self.x = self.xh * 2 + self.xl
        self.q = self.xl * 2 + self.c

    def at(self, y=None, x=None, z=None, c=None):
        y = self.y if y is None else y
        x = self.x if x is None else x
        z = self.z if z is None else z
        c = self.c if c is None else c
        return (y, x // 2, z, x % 2, c)


class Links:
    def __init__(self, send_sems, recv_sems, local_sems):
        self.send_sems, self.recv_sems, self.local_sems = send_sems, recv_sems, local_sems
        self.count, self.local_count, self.started = 0, 0, []

    def send(self, src, dst, device):
        copy = pltpu.make_async_remote_copy(
            src_ref=src,
            dst_ref=dst,
            send_sem=self.send_sems.at[self.count],
            recv_sem=self.recv_sems.at[self.count],
            device_id=device,
            device_id_type=MESH,
        )
        self.count += 1
        copy.start()
        self.started.append(copy)
        return copy

    def local(self, src, dst):
        copy = pltpu.make_async_copy(src, dst, self.local_sems.at[self.local_count])
        self.local_count += 1
        copy.start()
        return copy

    def finish(self):
        for copy in self.started:
            copy.wait_send()


class WeightGather:
    def __init__(self, links, place, pack, whole, cut):
        self.links, self.place, self.whole = links, place, whole
        cols = whole.shape[-1]
        self.parts = (pl.ds(0, cut), pl.ds(cut, cols - cut))
        self.swap = links.send(
            pack.at[1 - place.xh], whole.at[place.y, place.xh, place.z], place.at(x=(place.x + 2) % 4)
        )
        self.mine = links.local(pack.at[place.xh], whole.at[place.y, place.xh, place.z])

    def send(self, ref, device):
        return self.links.send(ref, ref, device)

    def near(self, view_z, view_y):
        p = self.place
        first, second = self.parts
        zs = (p.at(z=(p.z + 1) % 4), p.at(z=(p.z + 3) % 4))
        ys = (p.at(y=(p.y + 1) % 4), p.at(y=(p.y + 3) % 4))
        (ref_z, axis_z), (ref_y, axis_y) = view_z, view_y
        to = {"z": zs, "y": ys}
        self.got = [
            self.send(ref_z, to[axis_z][0]),
            self.send(ref_y, to[axis_y][0]),
            self.send(ref_z, to[axis_z][1]),
            self.send(ref_y, to[axis_y][1]),
        ]

    def wait(self):
        for copy in self.got:
            copy.wait_recv()

    def start0(self):
        p, w = self.place, self.whole
        first, second = self.parts
        self.swap.wait_recv()
        self.mine.wait()
        self.near(
            (w.at[p.y, :, p.z, :, first], "z"),
            (w.at[p.y, :, p.z, :, second], "y"),
        )

    def start1(self):
        p, w = self.place, self.whole
        first, second = self.parts
        self.wait()
        zn, zp, yn, yp = (p.z + 1) % 4, (p.z + 3) % 4, (p.y + 1) % 4, (p.y + 3) % 4
        self.got = [
            self.send(w.at[p.y, 0, zp, :, first], p.at(z=zn)),
            self.send(w.at[yp, 0, p.z, :, second], p.at(y=yn)),
            self.send(w.at[p.y, 1, zn, :, first], p.at(z=zp)),
            self.send(w.at[yn, 1, p.z, :, second], p.at(y=yp)),
        ]

    def start2(self):
        p, w = self.place, self.whole
        first, second = self.parts
        self.wait()
        self.near(
            (w.at[:, :, p.z, :, second], "z"),
            (w.at[p.y, :, :, :, first], "y"),
        )

    def start3(self):
        p, w = self.place, self.whole
        first, second = self.parts
        self.wait()
        zn, zp, yn, yp = (p.z + 1) % 4, (p.z + 3) % 4, (p.y + 1) % 4, (p.y + 3) % 4
        self.got = [
            self.send(w.at[yp, 0, :, :, first], p.at(y=yn)),
            self.send(w.at[:, 0, zp, :, second], p.at(z=zn)),
            self.send(w.at[yn, 1, :, :, first], p.at(y=yp)),
            self.send(w.at[:, 1, zn, :, second], p.at(z=zp)),
        ]

    def done(self):
        self.wait()


def greet(place):
    p = place
    barrier = pltpu.get_barrier_semaphore()
    partners = (
        p.at(z=(p.z + 1) % 4),
        p.at(z=(p.z + 3) % 4),
        p.at(y=(p.y + 1) % 4),
        p.at(y=(p.y + 3) % 4),
        p.at(x=(p.x + 1) % 4),
        p.at(x=(p.x + 3) % 4),
        p.at(x=(p.x + 2) % 4),
        p.at(c=1 - p.c),
    )
    for device in partners:
        pl.semaphore_signal(barrier, inc=1, device_id=device, device_id_type=MESH)

    @pl.when(p.z == 3)
    def _():
        pl.semaphore_signal(barrier, inc=1, device_id=p.at(y=(p.y + 1) % 4, z=0 * p.z), device_id_type=MESH)

    @pl.when(p.z == 0)
    def _():
        pl.semaphore_signal(barrier, inc=1, device_id=p.at(y=(p.y + 3) % 4, z=0 * p.z + 3), device_id_type=MESH)

    pl.semaphore_wait(barrier, 8 + jnp.where((p.z == 3) | (p.z == 0), 1, 0))


def unit_scale(values):
    return values * lax.rsqrt(jnp.mean(values * values, axis=-1, keepdims=True) + epsilon)


def forward_kernel(
    pk_q, pk_o, pk_gu, pk_d, hid, cot, bias_in,
    wq_o, wo_o, gu_o, d_o, xr_o, q_o, kv_o, mixed_o, resid_o, nm_o, cot_o,
    wq, wo, hidg, xr, q_v, kvx, mixed, bias, send_c, recv_c, own, send_x, recv_x, nm,
    send_sems, recv_sems, local_sems,
):
    p = Place()
    links = Links(send_sems, recv_sems, local_sems)
    sibling = p.at(c=1 - p.c)
    facing = p.at(x=3 - p.x)
    greet(p)

    g_q = WeightGather(links, p, pk_q, wq, 384)
    own_hidden = links.local(hid, hidg.at[p.xh])
    rows = [pl.ds(p.c * 256 + k * 128, 128) for k in range(2)]
    hidden_sent = [links.send(hid.at[r], hidg.at[p.xh, r], facing) for r in rows]
    g_o = WeightGather(links, p, pk_o, wo, 128)
    bias_copy = links.local(bias_in, bias)
    g_gu = WeightGather(links, p, pk_gu, gu_o, 768)
    g_d = WeightGather(links, p, pk_d, d_o, 384)
    own_cot = links.local(cot, cot_o.at[p.xh])
    g_q.start0()
    g_o.start0()

    def norm_rows(block, start, count):
        def body(i, _):
            r = pl.ds(start + i * 32, 32)
            xr[block, r] = unit_scale(hidg[block, r].astype(f32)).astype(bf16)
            return 0

        lax.fori_loop(0, count // 32, body, 0)

    own_hidden.wait()
    norm_rows(p.xh, 0, BLOCK)
    g_q.start1()
    g_o.start1()
    g_q.start2()
    g_o.start2()
    g_gu.start0()
    g_d.start0()

    shared = []
    for k in range(2):
        hidden_sent[k].wait_recv()
        part = hidg.at[1 - p.xh, rows[k]]
        shared.append(links.send(part, part, sibling))
    cot_sent = [links.send(cot.at[r], cot_o.at[p.xh, r], facing) for r in rows]
    norm_rows(1 - p.xh, p.c * 256, 256)
    for copy in shared:
        copy.wait_recv()
    norm_rows(1 - p.xh, (1 - p.c) * 256, 256)
    xr_copy = links.local(xr, xr_o)

    g_q.start3()
    g_o.start3()
    g_gu.start1()
    g_d.start1()
    g_q.done()

    def project(i, _):
        block, r = i // 2, (i % 2) * 256
        w = wq[...].reshape(2048, 768)
        out = jnp.dot(xr[block, pl.ds(r, 256)], w, preferred_element_type=f32).astype(bf16)
        q_v[block, pl.ds(r, 256)] = out[:, :256]
        kvx[block, pl.ds(r + WINDOW, 256)] = out[:, 256:]
        return 0

    lax.fori_loop(0, 4, project, 0)

    tails = []
    last = jnp.where(p.z == 3, 1, 0)
    for block in range(2):
        to_y = p.y if block == 0 else (p.y + last) % 4
        slot = last if block == 0 else 1 - last
        tails.append(
            links.send(
                kvx.at[block, pl.ds(BLOCK, WINDOW)],
                kvx.at[slot, pl.ds(0, WINDOW)],
                p.at(y=to_y, z=(p.z + 1) % 4),
            )
        )
    g_gu.start2()
    wq_copy = links.local(wq, wq_o)
    q_copy = links.local(q_v, q_o)
    bias_copy.wait()

    def attend(block, chunk, head):
        r, lane = pl.multiple_of(chunk * 128, 128), pl.multiple_of(head * 128, 128)
        query = q_v[block, pl.ds(r, 128), pl.ds(lane, 128)]
        keys = kvx[block, pl.ds(r, 192), pl.ds(lane, 128)]
        values = kvx[block, pl.ds(r, 192), pl.ds(lane + 256, 128)]
        scores = lax.dot_general(query, keys, TURNED, preferred_element_type=f32) * SCALE
        scores = scores + bias[block * 4 + chunk]
        expo = jnp.exp(scores - jnp.max(scores, axis=-1, keepdims=True))
        probs = (expo / jnp.sum(expo, axis=-1, keepdims=True)).astype(bf16)
        out = jnp.dot(probs, values, preferred_element_type=f32)
        mixed[block, pl.ds(r, 128), pl.ds(lane, 128)] = out.astype(bf16)

    def inner(i, _):
        attend(i // 6, (i % 6) // 2 + 1, i % 2)
        return 0

    lax.fori_loop(0, 12, inner, 0)
    for copy in tails:
        copy.wait_recv()

    def first(i, _):
        attend(i // 2, 0, i % 2)
        return 0

    lax.fori_loop(0, 4, first, 0)
    kv_copy = links.local(kvx, kv_o)
    mixed_copy = links.local(mixed, mixed_o)
    g_o.done()

    def branch_all():
        def sib(n, _):
            lanes = pl.ds(pl.multiple_of(n * 256, 256), 256)
            w = wo[n // 2, n % 2].reshape(256, 256)
            for x in range(4):
                left = mixed[x // 2, pl.ds((x % 2) * 256 + (1 - p.c) * OWNED, OWNED)]
                part = lax.dot_general(left, w, TURNED, preferred_element_type=f32)
                send_c[x, :, lanes] = part.astype(bf16)
            return 0

        lax.fori_loop(0, 8, sib, 0)
        crossed = links.send(send_c, recv_c, sibling)

        def mine(n, _):
            lanes = pl.ds(pl.multiple_of(n * 256, 256), 256)
            w = wo[n // 2, n % 2].reshape(256, 256)
            for x in range(4):
                left = mixed[x // 2, pl.ds((x % 2) * 256 + p.c * OWNED, OWNED)]
                own[x, :, lanes] = lax.dot_general(left, w, TURNED, preferred_element_type=f32)
            return 0

        lax.fori_loop(0, 8, mine, 0)
        return crossed

    crossed = branch_all()
    crossed.wait_recv()
    arrived = []
    for k in (2, 1, 3):
        to = (p.x + k) % 4

        def add(i, _):
            r = pl.ds(i * 16, 16)
            send_x[k - 1, r] = (own[to, r] + recv_c[to, r].astype(f32)).astype(bf16)
            return 0

        lax.fori_loop(0, OWNED // 16, add, 0)
        arrived.append(links.send(send_x.at[k - 1], recv_x.at[k - 1], p.at(x=to)))
    g_d.start2()
    g_gu.start3()
    for copy in arrived:
        copy.wait_recv()

    def finish(i, _):
        r = pl.ds(i * 16, 16)
        total = hidg[p.xh, pl.ds(p.q * OWNED + i * 16, 16)].astype(f32)
        total = total + own[p.x, r] + recv_c[p.x, r].astype(f32)
        for k in range(3):
            total = total + recv_x[k, r].astype(f32)
        own[p.x, r] = total
        nm[r] = unit_scale(total).astype(bf16)
        return 0

    lax.fori_loop(0, OWNED // 16, finish, 0)
    resid_copy = links.local(own.at[p.x], resid_o)
    spread = [links.send(nm, nm_o.at[p.x, p.c], p.at(x=(p.x + k) % 4)) for k in (2, 1, 3)]
    nm_copy = links.local(nm, nm_o.at[p.x, p.c])
    paired = [links.send(nm, nm_o.at[p.x, p.c], sibling)]
    wo_copy = links.local(wo, wo_o)
    cot_shared = []
    for k in range(2):
        cot_sent[k].wait_recv()
        part = cot_o.at[1 - p.xh, rows[k]]
        cot_shared.append(links.send(part, part, sibling))
    for i, k in ((1, 1), (2, 3), (0, 2)):
        spread[i].wait_recv()
        part = nm_o.at[(p.x + 4 - k) % 4, p.c]
        paired.append(links.send(part, part, sibling))
    g_d.start3()
    for copy in paired + cot_shared:
        copy.wait_recv()
    g_gu.done()
    g_d.done()
    for copy in (own_cot, xr_copy, wq_copy, q_copy, kv_copy, mixed_copy, resid_copy, nm_copy, wo_copy):
        copy.wait()
    links.finish()


def forward_call(pk_q, pk_o, pk_gu, pk_d, hid, cot, bias):
    sds = jax.ShapeDtypeStruct
    return pl.pallas_call(
        forward_kernel,
        out_shape=(
            sds((4, 2, 4, 64, 768), bf16),
            sds((4, 2, 4, 64, 256), bf16),
            sds((4, 2, 4, 64, 1408), bf16),
            sds((4, 2, 4, 64, 768), bf16),
            sds((2, BLOCK, 2048), bf16),
            sds((2, BLOCK, 256), bf16),
            sds((2, BLOCK + WINDOW, 512), bf16),
            sds((2, BLOCK, 256), bf16),
            sds((OWNED, 2048), f32),
            sds((4, 2, OWNED, 2048), bf16),
            sds((2, BLOCK, 2048), bf16),
        ),
        in_specs=[ANY] * 7,
        out_specs=[ANY] * 11,
        scratch_shapes=[
            pltpu.VMEM((4, 2, 4, 64, 768), bf16),
            pltpu.VMEM((4, 2, 4, 64, 256), bf16),
            pltpu.VMEM((2, BLOCK, 2048), bf16),
            pltpu.VMEM((2, BLOCK, 2048), bf16),
            pltpu.VMEM((2, BLOCK, 256), bf16),
            pltpu.VMEM((2, BLOCK + WINDOW, 512), bf16),
            pltpu.VMEM((2, BLOCK, 256), bf16),
            pltpu.VMEM((8, 128, 192), f32),
            pltpu.VMEM((4, OWNED, 2048), bf16),
            pltpu.VMEM((4, OWNED, 2048), bf16),
            pltpu.VMEM((4, OWNED, 2048), f32),
            pltpu.VMEM((3, OWNED, 2048), bf16),
            pltpu.VMEM((3, OWNED, 2048), bf16),
            pltpu.VMEM((OWNED, 2048), bf16),
            pltpu.SemaphoreType.DMA((100,)),
            pltpu.SemaphoreType.DMA((100,)),
            pltpu.SemaphoreType.DMA((20,)),
        ],
        compiler_params=pltpu.CompilerParams(
            collective_id=0, has_side_effects=True, vmem_limit_bytes=56 * 2**20
        ),
        name="forward_attention",
    )(pk_q, pk_o, pk_gu, pk_d, hid, cot, bias)


def attention_bias(lengths):
    y, z = lax.axis_index("y"), lax.axis_index("z")
    starts = (y * 8 + z + 4 * jnp.arange(2, dtype=jnp.int32)) * BLOCK
    starts = (starts[:, None] + 128 * jnp.arange(4, dtype=jnp.int32)).reshape(8, 1, 1)
    query = starts + jnp.arange(128, dtype=jnp.int32)[None, :, None]
    key = starts - WINDOW + jnp.arange(192, dtype=jnp.int32)[None, None, :]
    ends = jnp.cumsum(lengths)
    segment = lambda t: sum((t >= ends[k]).astype(jnp.int32) for k in range(3))
    visible = (key <= query) & (key > query - WINDOW) & (key >= 0) & (segment(key) == segment(query))
    return jnp.where(visible, 0.0, masked_score).astype(f32)


def pack_ff(gate, up, down):
    def tail(w):
        return jnp.pad(w[:, 640:], ((0, 0), (0, 16)))

    def one(k):
        g, u, d = (w[:, k * 688 : (k + 1) * 688] for w in (gate, up, down))
        return (
            jnp.concatenate([g[:, :640], u[:, :640], tail(g), tail(u)], axis=1),
            jnp.pad(d, ((0, 0), (0, 80))),
        )

    (gu0, d0), (gu1, d1) = one(0), one(1)
    return jnp.stack([gu0, gu1]), jnp.stack([d0, d1])


def pack_attn(query, key, value, out):
    def one(k):
        part = slice(k * 256, (k + 1) * 256)
        return jnp.concatenate([query[:, part], key[:, part], value[:, part]], axis=1), out[:, part]

    (q0, o0), (q1, o1) = one(0), one(1)
    return jnp.stack([q0, q1]), jnp.stack([o0, o1])


def per_device(
    hidden_in,
    norm_gain_attn,
    w_query,
    w_key,
    w_value,
    w_out,
    norm_gain_mlp,
    w_gate,
    w_up,
    w_down,
    lengths,
    cotangent,
):
    xh, xl, c = lax.axis_index("xh"), lax.axis_index("xl"), lax.axis_index("c")
    gain_attn = norm_gain_attn.astype(f32)[:, None]
    gain_mlp = norm_gain_mlp.astype(f32)[:, None]
    scaled = lambda w, g: (w.astype(f32) * g).astype(bf16)
    pk_q, pk_o = pack_attn(
        scaled(w_query, gain_attn), scaled(w_key, gain_attn), scaled(w_value, gain_attn), w_out.T
    )
    pk_gu, pk_d = pack_ff(scaled(w_gate, gain_mlp), scaled(w_up, gain_mlp), w_down.T)
    bias = attention_bias(lengths)
    wq, wo, gu, d, xr, queries, kv_ext, mixed, resid, nm, cot = forward_call(
        pk_q, pk_o, pk_gu, pk_d, hidden_in, cotangent, bias
    )
    qkv_w = wq.reshape(2048, 768)
    out_w = wo.reshape(2048, 256)
    gu = gu.reshape(2048, 1408)
    gate_w = jnp.concatenate([gu[:, :640], gu[:, 1280:1328]], axis=1)
    up_w = jnp.concatenate([gu[:, 640:1280], gu[:, 1344:1392]], axis=1)
    down_w = d.reshape(2048, 768)[:, :688]
    normed_attn = xr.reshape(1024, 2048)
    mixed = mixed.reshape(1024, 256)
    normed_mlp = nm.reshape(1024, 2048)
    cot = cot.reshape(1024, 2048)

    q = xl * 2 + c
    owned_rows = lambda a: lax.dynamic_slice_in_dim(a, q * OWNED, OWNED, 0)
    hidden_owned = owned_rows(hidden_in).astype(f32)
    cot_owned = owned_rows(cotangent).astype(f32)
    visible = visibility(lengths)
    queries = queries.reshape(16, WINDOW, 2, HEAD_DIM)
    key_blocks = band_blocks(kv_ext[..., :256]).reshape(16, 2 * WINDOW, 2, HEAD_DIM)
    value_blocks = band_blocks(kv_ext[..., 256:]).reshape(16, 2 * WINDOW, 2, HEAD_DIM)
    scores = score_blocks(queries, key_blocks, visible)
    highest = jnp.max(scores, axis=-1, keepdims=True)
    expo = jnp.exp(scores - highest)
    probs = expo / jnp.sum(expo, axis=-1, keepdims=True)
    probs_low = probs.astype(bf16)

    gate = dot_plain(normed_mlp, gate_w)
    up = dot_plain(normed_mlp, up_w)
    sig = 1 / (1 + jnp.exp(-gate))
    silu = gate * sig
    activated = (silu * up).astype(bf16)
    result = resid + reduce_group(dot_right_turned(activated, down_w))
    result = gather_owned(result.astype(bf16))

    grad_act = dot_plain(cot, down_w)
    grad_gate_act = (grad_act * up * sig * (1 + gate * (1 - sig))).astype(bf16)
    grad_up_act = (grad_act * silu).astype(bf16)
    grad_normed_mlp = reduce_group(
        dot_right_turned(grad_gate_act, gate_w) + dot_right_turned(grad_up_act, up_w)
    )
    grad_down = dot_left_turned(cot, activated).astype(bf16)
    grad_gate = dot_left_turned(normed_mlp, grad_gate_act).astype(bf16)
    grad_up = dot_left_turned(normed_mlp, grad_up_act).astype(bf16)
    grad_ff = jnp.concatenate([grad_gate, grad_up, grad_down], axis=1)
    grad_ff = reduce_weights(grad_ff[:, :1024], grad_ff[:, 1024:])

    def norm_back(e, values):
        r = lax.rsqrt(jnp.mean(values * values, axis=-1, keepdims=True) + epsilon)
        return r * e - values * r**3 * jnp.mean(e * values, axis=-1, keepdims=True)

    grad_resid = cot_owned + norm_back(grad_normed_mlp, resid)
    grad_branch = gather_group(grad_resid.astype(bf16))
    grad_out = dot_left_turned(grad_branch, mixed).astype(bf16)
    grad_mixed = dot_plain(grad_branch, out_w).astype(bf16).reshape(16, WINDOW, 2, HEAD_DIM)
    grad_probs = jnp.einsum("bqhd,bkhd->bhqk", grad_mixed, value_blocks, preferred_element_type=f32)
    inner = jnp.sum(probs * grad_probs, axis=-1, keepdims=True)
    grad_scores = (probs * (grad_probs - inner)).astype(bf16)
    scale = HEAD_DIM ** (-0.5)
    grad_queries = (
        jnp.einsum("bhqk,bkhd->bqhd", grad_scores, key_blocks, preferred_element_type=f32) * scale
    )
    grad_keys = (
        jnp.einsum("bhqk,bqhd->bkhd", grad_scores, queries, preferred_element_type=f32) * scale
    )
    grad_values = jnp.einsum("bhqk,bqhd->bkhd", probs_low, grad_mixed, preferred_element_type=f32)
    grad_kv = jnp.concatenate([fold_blocks(grad_keys), fold_blocks(grad_values)], axis=-1)
    returned = tails_back(grad_kv[:, :WINDOW].astype(bf16)).astype(f32)
    grad_kv = jnp.concatenate(
        [grad_kv[:, WINDOW:BLOCK], grad_kv[:, BLOCK:] + returned], axis=1
    ).reshape(1024, 512)
    grad_qkv_act = jnp.concatenate([grad_queries.reshape(1024, 256), grad_kv], axis=1).astype(bf16)
    grad_normed_attn = reduce_group(dot_right_turned(grad_qkv_act, qkv_w))
    grad_qkv = dot_left_turned(normed_attn, grad_qkv_act).astype(bf16)
    input_grad = gather_owned((grad_resid + norm_back(grad_normed_attn, hidden_owned)).astype(bf16))

    grad_attn = jnp.concatenate([grad_qkv, grad_out], axis=1)
    grad_attn = reduce_weights(grad_attn[:, :512], grad_attn[:, 512:])

    def unswap(pack):
        mine = pick(pack, 0, xh)[0]
        return mine, flip(pick(pack, 0, 1 - xh)[0], "xh")

    mine_a, other_a = unswap(grad_attn)
    mine_f, other_f = unswap(grad_ff)

    def whole(mine, other, start, width):
        return in_order(xh, mine[:, start : start + width], other[:, start : start + width], 1).astype(f32)

    dq, dk, dv = (whole(mine_a, other_a, 256 * i, 256) for i in range(3))
    dg, du = (whole(mine_f, other_f, 688 * i, 688) for i in range(2))

    def dots(pairs):
        return sum(jnp.sum(w.astype(f32) * g, axis=1) for w, g in pairs)

    grads_gain = jnp.stack(
        [dots([(w_query, dq), (w_key, dk), (w_value, dv)]), dots([(w_gate, dg), (w_up, du)])]
    )
    grads_gain = grads_gain + flip(grads_gain, "xl")
    grads_gain = grads_gain + flip(grads_gain, "c")
    return (
        result,
        input_grad,
        grads_gain[0],
        dq * gain_attn,
        dk * gain_attn,
        dv * gain_attn,
        whole(mine_a, other_a, 768, 256).T,
        grads_gain[1],
        dg * gain_mlp,
        du * gain_mlp,
        whole(mine_f, other_f, 1376, 688).T,
    )


def solution(mesh):
    mesh = Mesh(mesh.devices.reshape(4, 2, 4, 2, 2), AXES)
    seq, head = ("y", "xh", "z"), ("xl", "c")
    rows, cols, flat, turned = P(seq, None), P(seq, head), P(seq), P(head, seq)
    return jax.shard_map(
        per_device,
        mesh=mesh,
        in_specs=(rows, flat, cols, cols, cols, turned, flat, cols, cols, turned, P(), rows),
        out_specs=(rows, rows, flat, cols, cols, cols, turned, flat, cols, cols, turned),
        check_vma=False,
    )
```

```python
import jax
import jax.numpy as jnp
from jax import lax
from jax.experimental import pallas as pl
from jax.experimental.pallas import tpu as pltpu
from jax.sharding import Mesh, PartitionSpec as P

HEAD_DIM = 128
WINDOW = 64
BLOCK = 512
OWNED = 128
AXES = ("y", "xh", "z", "xl", "c")

epsilon = 1e-05
masked_score = -1e30
f32 = jnp.float32
bf16 = jnp.bfloat16


def flip(value, axis):
    return lax.ppermute(value, axis, [(0, 1), (1, 0)])


MESH = pl.DeviceIdType.MESH
SCALE = HEAD_DIM ** (-0.5)
ANY = pl.BlockSpec(memory_space=pl.ANY)
TURNED = (((1,), (1,)), ((), ()))
LEFT_TURNED = (((0,), (0,)), ((), ()))


class Place:
    def __init__(self):
        self.y, self.z, self.c = lax.axis_index("y"), lax.axis_index("z"), lax.axis_index("c")
        self.xh, self.xl = lax.axis_index("xh"), lax.axis_index("xl")
        self.x = self.xh * 2 + self.xl
        self.q = self.xl * 2 + self.c

    def at(self, y=None, x=None, z=None, c=None):
        y = self.y if y is None else y
        x = self.x if x is None else x
        z = self.z if z is None else z
        c = self.c if c is None else c
        return (y, x // 2, z, x % 2, c)


class Links:
    def __init__(self, send_sems, recv_sems, local_sems):
        self.send_sems, self.recv_sems, self.local_sems = send_sems, recv_sems, local_sems
        self.count, self.local_count, self.started = 0, 0, []

    def send(self, src, dst, device):
        copy = pltpu.make_async_remote_copy(
            src_ref=src,
            dst_ref=dst,
            send_sem=self.send_sems.at[self.count],
            recv_sem=self.recv_sems.at[self.count],
            device_id=device,
            device_id_type=MESH,
        )
        self.count += 1
        copy.start()
        self.started.append(copy)
        return copy

    def local(self, src, dst):
        copy = pltpu.make_async_copy(src, dst, self.local_sems.at[self.local_count])
        self.local_count += 1
        copy.start()
        return copy

    def finish(self):
        for copy in self.started:
            copy.wait_send()


class WeightGather:
    def __init__(self, links, place, pack, whole, cut):
        self.links, self.place, self.whole = links, place, whole
        cols = whole.shape[-1]
        self.parts = (pl.ds(0, cut), pl.ds(cut, cols - cut))
        self.swap = links.send(
            pack.at[1 - place.xh], whole.at[place.y, place.xh, place.z], place.at(x=(place.x + 2) % 4)
        )
        self.mine = links.local(pack.at[place.xh], whole.at[place.y, place.xh, place.z])

    def send(self, ref, device):
        return self.links.send(ref, ref, device)

    def near(self, view_z, view_y):
        p = self.place
        first, second = self.parts
        zs = (p.at(z=(p.z + 1) % 4), p.at(z=(p.z + 3) % 4))
        ys = (p.at(y=(p.y + 1) % 4), p.at(y=(p.y + 3) % 4))
        (ref_z, axis_z), (ref_y, axis_y) = view_z, view_y
        to = {"z": zs, "y": ys}
        self.got = [
            self.send(ref_z, to[axis_z][0]),
            self.send(ref_y, to[axis_y][0]),
            self.send(ref_z, to[axis_z][1]),
            self.send(ref_y, to[axis_y][1]),
        ]

    def wait(self):
        for copy in self.got:
            copy.wait_recv()

    def start0(self):
        p, w = self.place, self.whole
        first, second = self.parts
        self.swap.wait_recv()
        self.mine.wait()
        self.near(
            (w.at[p.y, :, p.z, :, first], "z"),
            (w.at[p.y, :, p.z, :, second], "y"),
        )

    def start1(self):
        p, w = self.place, self.whole
        first, second = self.parts
        self.wait()
        zn, zp, yn, yp = (p.z + 1) % 4, (p.z + 3) % 4, (p.y + 1) % 4, (p.y + 3) % 4
        self.got = [
            self.send(w.at[p.y, 0, zp, :, first], p.at(z=zn)),
            self.send(w.at[yp, 0, p.z, :, second], p.at(y=yn)),
            self.send(w.at[p.y, 1, zn, :, first], p.at(z=zp)),
            self.send(w.at[yn, 1, p.z, :, second], p.at(y=yp)),
        ]

    def start2(self):
        p, w = self.place, self.whole
        first, second = self.parts
        self.wait()
        self.near(
            (w.at[:, :, p.z, :, second], "z"),
            (w.at[p.y, :, :, :, first], "y"),
        )

    def start3(self):
        p, w = self.place, self.whole
        first, second = self.parts
        self.wait()
        zn, zp, yn, yp = (p.z + 1) % 4, (p.z + 3) % 4, (p.y + 1) % 4, (p.y + 3) % 4
        self.got = [
            self.send(w.at[yp, 0, :, :, first], p.at(y=yn)),
            self.send(w.at[:, 0, zp, :, second], p.at(z=zn)),
            self.send(w.at[yn, 1, :, :, first], p.at(y=yp)),
            self.send(w.at[:, 1, zn, :, second], p.at(z=zp)),
        ]

    def done(self):
        self.wait()


def greet(place):
    p = place
    barrier = pltpu.get_barrier_semaphore()
    partners = (
        p.at(z=(p.z + 1) % 4),
        p.at(z=(p.z + 3) % 4),
        p.at(y=(p.y + 1) % 4),
        p.at(y=(p.y + 3) % 4),
        p.at(x=(p.x + 1) % 4),
        p.at(x=(p.x + 3) % 4),
        p.at(x=(p.x + 2) % 4),
        p.at(c=1 - p.c),
    )
    for device in partners:
        pl.semaphore_signal(barrier, inc=1, device_id=device, device_id_type=MESH)

    @pl.when(p.z == 3)
    def _():
        pl.semaphore_signal(barrier, inc=1, device_id=p.at(y=(p.y + 1) % 4, z=0 * p.z), device_id_type=MESH)

    @pl.when(p.z == 0)
    def _():
        pl.semaphore_signal(barrier, inc=1, device_id=p.at(y=(p.y + 3) % 4, z=0 * p.z + 3), device_id_type=MESH)

    pl.semaphore_wait(barrier, 8 + jnp.where((p.z == 3) | (p.z == 0), 1, 0))


def unit_scale(values):
    return values * lax.rsqrt(jnp.mean(values * values, axis=-1, keepdims=True) + epsilon)


def forward_kernel(
    pk_q, pk_o, pk_gu, pk_d, hid, cot, bias_in,
    wq_o, wo_o, gu_o, d_o, xr_o, q_o, kv_o, mixed_o, resid_o, nm_o, cot_o,
    wq, wo, hidg, xr, q_v, kvx, mixed, bias, send_c, recv_c, own, send_x, recv_x, nm,
    send_sems, recv_sems, local_sems,
):
    p = Place()
    links = Links(send_sems, recv_sems, local_sems)
    sibling = p.at(c=1 - p.c)
    facing = p.at(x=3 - p.x)
    greet(p)

    g_q = WeightGather(links, p, pk_q, wq, 384)
    own_hidden = links.local(hid, hidg.at[p.xh])
    rows = [pl.ds(p.c * 256 + k * 128, 128) for k in range(2)]
    hidden_sent = [links.send(hid.at[r], hidg.at[p.xh, r], facing) for r in rows]
    g_o = WeightGather(links, p, pk_o, wo, 128)
    bias_copy = links.local(bias_in, bias)
    g_gu = WeightGather(links, p, pk_gu, gu_o, 768)
    g_d = WeightGather(links, p, pk_d, d_o, 384)
    own_cot = links.local(cot, cot_o.at[p.xh])
    g_q.start0()
    g_o.start0()

    def norm_rows(block, start, count):
        def body(i, _):
            r = pl.ds(start + i * 32, 32)
            xr[block, r] = unit_scale(hidg[block, r].astype(f32)).astype(bf16)
            return 0

        lax.fori_loop(0, count // 32, body, 0)

    own_hidden.wait()
    norm_rows(p.xh, 0, BLOCK)
    g_q.start1()
    g_o.start1()
    g_q.start2()
    g_o.start2()
    g_gu.start0()
    g_d.start0()

    shared = []
    for k in range(2):
        hidden_sent[k].wait_recv()
        part = hidg.at[1 - p.xh, rows[k]]
        shared.append(links.send(part, part, sibling))
    cot_sent = [links.send(cot.at[r], cot_o.at[p.xh, r], facing) for r in rows]
    norm_rows(1 - p.xh, p.c * 256, 256)
    for copy in shared:
        copy.wait_recv()
    norm_rows(1 - p.xh, (1 - p.c) * 256, 256)
    xr_copy = links.local(xr, xr_o)

    g_q.start3()
    g_o.start3()
    g_gu.start1()
    g_d.start1()
    g_q.done()

    def project(i, _):
        block, r = i // 2, (i % 2) * 256
        w = wq[...].reshape(2048, 768)
        out = jnp.dot(xr[block, pl.ds(r, 256)], w, preferred_element_type=f32).astype(bf16)
        q_v[block, pl.ds(r, 256)] = out[:, :256]
        kvx[block, pl.ds(r + WINDOW, 256)] = out[:, 256:]
        return 0

    lax.fori_loop(0, 4, project, 0)

    tails = []
    last = jnp.where(p.z == 3, 1, 0)
    for block in range(2):
        to_y = p.y if block == 0 else (p.y + last) % 4
        slot = last if block == 0 else 1 - last
        tails.append(
            links.send(
                kvx.at[block, pl.ds(BLOCK, WINDOW)],
                kvx.at[slot, pl.ds(0, WINDOW)],
                p.at(y=to_y, z=(p.z + 1) % 4),
            )
        )
    g_gu.start2()
    wq_copy = links.local(wq, wq_o)
    q_copy = links.local(q_v, q_o)
    bias_copy.wait()

    def attend(block, chunk, head):
        r, lane = pl.multiple_of(chunk * 128, 128), pl.multiple_of(head * 128, 128)
        query = q_v[block, pl.ds(r, 128), pl.ds(lane, 128)]
        keys = kvx[block, pl.ds(r, 192), pl.ds(lane, 128)]
        values = kvx[block, pl.ds(r, 192), pl.ds(lane + 256, 128)]
        scores = lax.dot_general(query, keys, TURNED, preferred_element_type=f32) * SCALE
        scores = scores + bias[block * 4 + chunk].astype(f32)
        expo = jnp.exp(scores - jnp.max(scores, axis=-1, keepdims=True))
        probs = (expo / jnp.sum(expo, axis=-1, keepdims=True)).astype(bf16)
        out = jnp.dot(probs, values, preferred_element_type=f32)
        mixed[block, pl.ds(r, 128), pl.ds(lane, 128)] = out.astype(bf16)

    def inner(i, _):
        attend(i // 6, (i % 6) // 2 + 1, i % 2)
        return 0

    lax.fori_loop(0, 12, inner, 0)
    for copy in tails:
        copy.wait_recv()

    def first(i, _):
        attend(i // 2, 0, i % 2)
        return 0

    lax.fori_loop(0, 4, first, 0)
    kv_copy = links.local(kvx, kv_o)
    mixed_copy = links.local(mixed, mixed_o)
    g_o.done()

    def branch_all():
        def sib(n, _):
            lanes = pl.ds(pl.multiple_of(n * 256, 256), 256)
            w = wo[n // 2, n % 2].reshape(256, 256)
            for x in range(4):
                left = mixed[x // 2, pl.ds((x % 2) * 256 + (1 - p.c) * OWNED, OWNED)]
                part = lax.dot_general(left, w, TURNED, preferred_element_type=f32)
                send_c[x, :, lanes] = part.astype(bf16)
            return 0

        lax.fori_loop(0, 8, sib, 0)
        crossed = links.send(send_c, recv_c, sibling)

        def mine(n, _):
            lanes = pl.ds(pl.multiple_of(n * 256, 256), 256)
            w = wo[n // 2, n % 2].reshape(256, 256)
            for x in range(4):
                left = mixed[x // 2, pl.ds((x % 2) * 256 + p.c * OWNED, OWNED)]
                own[x, :, lanes] = lax.dot_general(left, w, TURNED, preferred_element_type=f32)
            return 0

        lax.fori_loop(0, 8, mine, 0)
        return crossed

    crossed = branch_all()
    crossed.wait_recv()
    arrived = []
    for k in (2, 1, 3):
        to = (p.x + k) % 4

        def add(i, _):
            r = pl.ds(i * 16, 16)
            send_x[k - 1, r] = (own[to, r] + recv_c[to, r].astype(f32)).astype(bf16)
            return 0

        lax.fori_loop(0, OWNED // 16, add, 0)
        arrived.append(links.send(send_x.at[k - 1], recv_x.at[k - 1], p.at(x=to)))
    g_d.start2()
    g_gu.start3()
    for copy in arrived:
        copy.wait_recv()

    def finish(i, _):
        r = pl.ds(i * 16, 16)
        total = hidg[p.xh, pl.ds(p.q * OWNED + i * 16, 16)].astype(f32)
        total = total + own[p.x, r] + recv_c[p.x, r].astype(f32)
        for k in range(3):
            total = total + recv_x[k, r].astype(f32)
        own[p.x, r] = total
        nm[r] = unit_scale(total).astype(bf16)
        return 0

    lax.fori_loop(0, OWNED // 16, finish, 0)
    resid_copy = links.local(own.at[p.x], resid_o)
    spread = [links.send(nm, nm_o.at[p.x, p.c], p.at(x=(p.x + k) % 4)) for k in (2, 1, 3)]
    nm_copy = links.local(nm, nm_o.at[p.x, p.c])
    paired = [links.send(nm, nm_o.at[p.x, p.c], sibling)]
    wo_copy = links.local(wo, wo_o)
    cot_shared = []
    for k in range(2):
        cot_sent[k].wait_recv()
        part = cot_o.at[1 - p.xh, rows[k]]
        cot_shared.append(links.send(part, part, sibling))
    for i, k in ((1, 1), (2, 3), (0, 2)):
        spread[i].wait_recv()
        part = nm_o.at[(p.x + 4 - k) % 4, p.c]
        paired.append(links.send(part, part, sibling))
    g_d.start3()
    for copy in paired + cot_shared:
        copy.wait_recv()
    g_gu.done()
    g_d.done()
    for copy in (own_cot, xr_copy, wq_copy, q_copy, kv_copy, mixed_copy, resid_copy, nm_copy, wo_copy):
        copy.wait()
    links.finish()


def forward_call(pk_q, pk_o, pk_gu, pk_d, hid, cot, bias):
    sds = jax.ShapeDtypeStruct
    return pl.pallas_call(
        forward_kernel,
        out_shape=(
            sds((4, 2, 4, 64, 768), bf16),
            sds((4, 2, 4, 64, 256), bf16),
            sds((4, 2, 4, 64, 1408), bf16),
            sds((4, 2, 4, 64, 768), bf16),
            sds((2, BLOCK, 2048), bf16),
            sds((2, BLOCK, 256), bf16),
            sds((2, BLOCK + WINDOW, 512), bf16),
            sds((2, BLOCK, 256), bf16),
            sds((OWNED, 2048), f32),
            sds((4, 2, OWNED, 2048), bf16),
            sds((2, BLOCK, 2048), bf16),
        ),
        in_specs=[ANY] * 7,
        out_specs=[ANY] * 11,
        scratch_shapes=[
            pltpu.VMEM((4, 2, 4, 64, 768), bf16),
            pltpu.VMEM((4, 2, 4, 64, 256), bf16),
            pltpu.VMEM((2, BLOCK, 2048), bf16),
            pltpu.VMEM((2, BLOCK, 2048), bf16),
            pltpu.VMEM((2, BLOCK, 256), bf16),
            pltpu.VMEM((2, BLOCK + WINDOW, 512), bf16),
            pltpu.VMEM((2, BLOCK, 256), bf16),
            pltpu.VMEM((8, 128, 192), bf16),
            pltpu.VMEM((4, OWNED, 2048), bf16),
            pltpu.VMEM((4, OWNED, 2048), bf16),
            pltpu.VMEM((4, OWNED, 2048), f32),
            pltpu.VMEM((3, OWNED, 2048), bf16),
            pltpu.VMEM((3, OWNED, 2048), bf16),
            pltpu.VMEM((OWNED, 2048), bf16),
            pltpu.SemaphoreType.DMA((100,)),
            pltpu.SemaphoreType.DMA((100,)),
            pltpu.SemaphoreType.DMA((20,)),
        ],
        compiler_params=pltpu.CompilerParams(
            collective_id=0, has_side_effects=True, vmem_limit_bytes=56 * 2**20
        ),
        name="forward_attention",
    )(pk_q, pk_o, pk_gu, pk_d, hid, cot, bias)


def attention_bias(lengths):
    y, z = lax.axis_index("y"), lax.axis_index("z")
    starts = (y * 8 + z + 4 * jnp.arange(2, dtype=jnp.int32)) * BLOCK
    starts = (starts[:, None] + 128 * jnp.arange(4, dtype=jnp.int32)).reshape(8, 1, 1)
    query = starts + jnp.arange(128, dtype=jnp.int32)[None, :, None]
    key = starts - WINDOW + jnp.arange(192, dtype=jnp.int32)[None, None, :]
    ends = jnp.cumsum(lengths)
    segment = lambda t: sum((t >= ends[k]).astype(jnp.int32) for k in range(3))
    visible = (key <= query) & (key > query - WINDOW) & (key >= 0) & (segment(key) == segment(query))
    return jnp.where(visible, 0.0, masked_score).astype(bf16)


def pack_ff(gate, up, down):
    def tail(w):
        return jnp.pad(w[:, 640:], ((0, 0), (0, 16)))

    def one(k):
        g, u, d = (w[:, k * 688 : (k + 1) * 688] for w in (gate, up, down))
        return (
            jnp.concatenate([g[:, :640], u[:, :640], tail(g), tail(u)], axis=1),
            jnp.pad(d, ((0, 0), (0, 80))),
        )

    (gu0, d0), (gu1, d1) = one(0), one(1)
    return jnp.stack([gu0, gu1]), jnp.stack([d0, d1])


def pack_attn(query, key, value, out):
    def one(k):
        part = slice(k * 256, (k + 1) * 256)
        return jnp.concatenate([query[:, part], key[:, part], value[:, part]], axis=1), out[:, part]

    (q0, o0), (q1, o1) = one(0), one(1)
    return jnp.stack([q0, q1]), jnp.stack([o0, o1])


class WeightReduce:
    def __init__(self, links, place, total, first_in, second_in, out, cut):
        self.links, self.place, self.total, self.out = links, place, total, out
        self.one, self.two = first_in, second_in
        cols = total.shape[-1]
        self.cols = cols
        self.parts = (pl.ds(0, cut), pl.ds(cut, cols - cut))
        p = place
        self.yn, self.yp, self.yf = (p.y + 1) % 4, (p.y + 3) % 4, (p.y + 2) % 4
        self.zn, self.zp, self.zf = (p.z + 1) % 4, (p.z + 3) % 4, (p.z + 2) % 4
        self.next_y, self.prev_y = p.at(y=self.yn), p.at(y=self.yp)
        self.next_z, self.prev_z = p.at(z=self.zn), p.at(z=self.zp)

    def start0(self):
        a, b = self.parts
        t, one, send = self.total, self.one, self.links.send
        self.far = [
            send(t.at[self.yf, 0, :, :, a], one.at[0, :, :, a], self.next_y),
            send(t.at[:, 0, self.zf, :, b], one.at[0, :, :, b], self.next_z),
            send(t.at[self.yf, 1, :, :, a], one.at[2, :, :, a], self.prev_y),
            send(t.at[:, 1, self.zf, :, b], one.at[2, :, :, b], self.prev_z),
        ]
        self.near = [
            send(t.at[self.yn, 1, :, :, a], one.at[1, :, :, a], self.next_y),
            send(t.at[:, 1, self.zn, :, b], one.at[1, :, :, b], self.next_z),
            send(t.at[self.yp, 0, :, :, a], one.at[3, :, :, a], self.prev_y),
            send(t.at[:, 0, self.zp, :, b], one.at[3, :, :, b], self.prev_z),
        ]

    def add(self, target, sources, rows):
        def body(i, _):
            ref = target(i)
            value = ref[...].astype(f32)
            for source in sources:
                value = value + source(i)[...].astype(f32)
            ref[...] = value.astype(bf16)
            return 0

        lax.fori_loop(0, rows, body, 0)

    def start1(self):
        a, b = self.parts
        t, one, send = self.total, self.one, self.links.send
        yn, yp, zn, zp = self.yn, self.yp, self.zn, self.zp
        self.sums = []
        self.far[0].wait_recv()
        self.add(lambda i: t.at[yn, 0, i, :, a], [lambda i: one.at[0, i, :, a]], 4)
        self.sums.append(send(t.at[yn, 0, :, :, a], one.at[4, :, :, a], self.next_y))
        self.far[1].wait_recv()
        self.add(lambda i: t.at[i, 0, zn, :, b], [lambda i: one.at[0, i, :, b]], 4)
        self.sums.append(send(t.at[:, 0, zn, :, b], one.at[4, :, :, b], self.next_z))
        self.far[2].wait_recv()
        self.add(lambda i: t.at[yp, 1, i, :, a], [lambda i: one.at[2, i, :, a]], 4)
        self.sums.append(send(t.at[yp, 1, :, :, a], one.at[5, :, :, a], self.prev_y))
        self.far[3].wait_recv()
        self.add(lambda i: t.at[i, 1, zp, :, b], [lambda i: one.at[2, i, :, b]], 4)
        self.sums.append(send(t.at[:, 1, zp, :, b], one.at[5, :, :, b], self.prev_z))

    def start2(self):
        a, b = self.parts
        t, one, two, send = self.total, self.one, self.two, self.links.send
        p = self.place
        for copy in self.near + self.sums:
            copy.wait_recv()
        self.add(lambda i: t.at[p.y, 0, i, :, a], [lambda i: one.at[3, i, :, a], lambda i: one.at[4, i, :, a]], 4)
        self.add(lambda i: t.at[p.y, 1, i, :, a], [lambda i: one.at[1, i, :, a], lambda i: one.at[5, i, :, a]], 4)
        self.add(lambda i: t.at[i, 0, p.z, :, b], [lambda i: one.at[3, i, :, b], lambda i: one.at[4, i, :, b]], 4)
        self.add(lambda i: t.at[i, 1, p.z, :, b], [lambda i: one.at[1, i, :, b], lambda i: one.at[5, i, :, b]], 4)
        self.far = [
            send(t.at[p.y, 0, self.zf, :, a], two.at[0, :, a], self.next_z),
            send(t.at[self.yf, 0, p.z, :, b], two.at[0, :, b], self.next_y),
            send(t.at[p.y, 1, self.zf, :, a], two.at[2, :, a], self.prev_z),
            send(t.at[self.yf, 1, p.z, :, b], two.at[2, :, b], self.prev_y),
        ]
        self.near = [
            send(t.at[p.y, 1, self.zn, :, a], two.at[1, :, a], self.next_z),
            send(t.at[self.yn, 1, p.z, :, b], two.at[1, :, b], self.next_y),
            send(t.at[p.y, 0, self.zp, :, a], two.at[3, :, a], self.prev_z),
            send(t.at[self.yp, 0, p.z, :, b], two.at[3, :, b], self.prev_y),
        ]

    def plus(self, target, *sources):
        value = target[...].astype(f32)
        for source in sources:
            value = value + source[...].astype(f32)
        target[...] = value.astype(bf16)

    def start3(self):
        a, b = self.parts
        t, two, send = self.total, self.two, self.links.send
        p = self.place
        yn, yp, zn, zp = self.yn, self.yp, self.zn, self.zp
        self.sums = []
        for k, ref, lanes, slot, other, device in (
            (0, t.at[p.y, 0, zn, :, a], a, 0, 4, self.next_z),
            (1, t.at[yn, 0, p.z, :, b], b, 0, 4, self.next_y),
            (2, t.at[p.y, 1, zp, :, a], a, 2, 5, self.prev_z),
            (3, t.at[yp, 1, p.z, :, b], b, 2, 5, self.prev_y),
        ):
            self.far[k].wait_recv()
            self.plus(ref, two.at[slot, :, lanes])
            self.sums.append(send(ref, two.at[other, :, lanes], device))

    def start4(self):
        t, two, out = self.total, self.two, self.out
        p = self.place
        for copy in self.near + self.sums:
            copy.wait_recv()
        self.plus(t.at[p.y, 0, p.z], two.at[3], two.at[4])
        self.plus(t.at[p.y, 1, p.z], two.at[1], two.at[5])
        self.swap = self.links.send(t.at[p.y, 1 - p.xh, p.z], out.at[p.xh], p.at(x=(p.x + 2) % 4))
        self.mine = self.links.local(t.at[p.y, p.xh, p.z], out.at[p.xh])

    def done(self):
        self.swap.wait_recv()
        self.mine.wait()


class GroupReduce:
    def __init__(self, place, partial, bufs, sems):
        self.place, self.partial = place, partial
        self.send_c, self.recv_c, self.tmp, self.snd, self.rcv, self.own = bufs
        self.send_sems, self.recv_sems = sems

    def copy(self, src, dst, index, device):
        return pltpu.make_async_remote_copy(
            src_ref=src,
            dst_ref=dst,
            send_sem=self.send_sems.at[index],
            recv_sem=self.recv_sems.at[index],
            device_id=device,
            device_id_type=MESH,
        )

    def crossing(self, n):
        return self.copy(self.send_c.at[n], self.recv_c.at[n], n, self.place.at(c=1 - self.place.c))

    def to_next(self, n):
        pair = pl.ds(0, 2)
        return self.copy(
            self.snd.at[n, pair], self.rcv.at[n, pair], 4 + n, self.place.at(x=(self.place.x + 1) % 4)
        )

    def to_prev(self, n):
        pair = pl.ds(2, 2)
        return self.copy(
            self.snd.at[n, pair], self.rcv.at[n, pair], 8 + n, self.place.at(x=(self.place.x + 3) % 4)
        )

    def sum_next(self, n):
        return self.copy(
            self.snd.at[n, 4], self.rcv.at[n, 4], 12 + n, self.place.at(x=(self.place.x + 1) % 4)
        )

    def sum_prev(self, n):
        return self.copy(
            self.snd.at[n, 5], self.rcv.at[n, 5], 16 + n, self.place.at(x=(self.place.x + 3) % 4)
        )

    def sibling_part(self, n):
        part = self.partial(n, 1 - self.place.c)
        self.send_c[n] = part.astype(bf16).reshape(4, OWNED, 512)
        self.crossing(n).start()

    def own_part(self, n):
        p, tmp, snd = self.place, self.tmp, self.snd
        part = self.partial(n, p.c).reshape(4, OWNED, 512)
        self.crossing(n).wait_recv()
        tmp[...] = part + self.recv_c[n].astype(f32)
        far, nxt, prev = (p.x + 2) % 4, (p.x + 1) % 4, (p.x + 3) % 4
        low, high = pl.ds(0, 64), pl.ds(64, 64)
        snd[n, 0] = tmp[far, low].astype(bf16)
        snd[n, 1] = tmp[nxt, high].astype(bf16)
        self.to_next(n).start()
        snd[n, 2] = tmp[far, high].astype(bf16)
        snd[n, 3] = tmp[prev, low].astype(bf16)
        self.to_prev(n).start()
        snd[n, 4] = tmp[nxt, low].astype(bf16)
        snd[n, 5] = tmp[prev, high].astype(bf16)
        self.own[:, pl.ds(pl.multiple_of(n * 512, 512), 512)] = tmp[p.x]

    def pass_on(self, n):
        snd, rcv = self.snd, self.rcv
        self.to_next(n).wait_recv()
        snd[n, 4] = (snd[n, 4].astype(f32) + rcv[n, 0].astype(f32)).astype(bf16)
        self.sum_next(n).start()
        self.to_prev(n).wait_recv()
        snd[n, 5] = (snd[n, 5].astype(f32) + rcv[n, 2].astype(f32)).astype(bf16)
        self.sum_prev(n).start()

    def run(self):
        def body(i, _):
            @pl.when(i < 4)
            def _():
                self.sibling_part(i)

            @pl.when((i >= 1) & (i < 5))
            def _():
                self.own_part(i - 1)

            @pl.when(i >= 2)
            def _():
                self.pass_on(i - 2)

            return 0

        lax.fori_loop(0, 6, body, 0)

    def finish(self):
        def body(n, _):
            lanes = pl.ds(pl.multiple_of(n * 512, 512), 512)
            low, high = pl.ds(0, 64), pl.ds(64, 64)
            rcv, own = self.rcv, self.own
            self.sum_next(n).wait_recv()
            own[low, lanes] = own[low, lanes] + rcv[n, 3].astype(f32) + rcv[n, 4].astype(f32)
            self.sum_prev(n).wait_recv()
            own[high, lanes] = own[high, lanes] + rcv[n, 1].astype(f32) + rcv[n, 5].astype(f32)
            return 0

        lax.fori_loop(0, 4, body, 0)

    def sent(self):
        def body(n, _):
            for copy in (self.crossing, self.to_next, self.to_prev, self.sum_next, self.sum_prev):
                copy(n).wait_send()
            return 0

        lax.fori_loop(0, 4, body, 0)


class GroupGather:
    def __init__(self, links, place, whole):
        self.links, self.place, self.whole = links, place, whole
        self.low, self.high = pl.ds(0, 64), pl.ds(64, 64)

    def send(self, ref, device):
        return self.links.send(ref, ref, device)

    def start(self):
        p, w = self.place, self.whole
        self.nxt, self.prev, self.far = (p.x + 1) % 4, (p.x + 3) % 4, (p.x + 2) % 4
        self.to_next, self.to_prev = p.at(x=self.nxt), p.at(x=self.prev)
        self.sibling = p.at(c=1 - p.c)
        low, high = w.at[p.x, p.c, self.low], w.at[p.x, p.c, self.high]
        self.first = [self.send(low, self.to_next), self.send(high, self.to_prev)]
        self.second = [self.send(high, self.to_next), self.send(low, self.to_prev)]
        self.paired = [self.send(w.at[p.x, p.c], self.sibling)]

    def forward(self):
        p, w = self.place, self.whole
        self.first[0].wait_recv()
        self.third = [self.send(w.at[self.prev, p.c, self.low], self.to_next)]
        self.first[1].wait_recv()
        self.third.append(self.send(w.at[self.nxt, p.c, self.high], self.to_prev))

    def share(self):
        p, w = self.place, self.whole
        self.second[0].wait_recv()
        self.paired.append(self.send(w.at[self.prev, p.c], self.sibling))
        self.second[1].wait_recv()
        self.paired.append(self.send(w.at[self.nxt, p.c], self.sibling))
        for copy in self.third:
            copy.wait_recv()
        self.paired.append(self.send(w.at[self.far, p.c], self.sibling))

    def done(self):
        for copy in self.paired:
            copy.wait_recv()


class BlockGather:
    def __init__(self, links, place, own, out):
        p = place
        self.links, self.place, self.out = links, place, out
        self.sibling = p.at(c=1 - p.c)
        mine = out.at[pl.ds(p.q * OWNED, OWNED)]
        self.local = links.local(own, mine)
        self.across = links.send(own, mine, p.at(x=p.xh * 2 + 1 - p.xl))
        self.paired = [links.send(own, mine, self.sibling)]

    def share(self):
        p = self.place
        self.across.wait_recv()
        theirs = self.out.at[pl.ds(((1 - p.xl) * 2 + p.c) * OWNED, OWNED)]
        self.paired.append(self.links.send(theirs, theirs, self.sibling))

    def done(self):
        for copy in self.paired:
            copy.wait_recv()
        self.local.wait()


def norm_back(e, values):
    r = lax.rsqrt(jnp.mean(values * values, axis=-1, keepdims=True) + epsilon)
    return r * e - values * r**3 * jnp.mean(e * values, axis=-1, keepdims=True)


def backward_kernel(
    wq_in, wo_in, gu_in, d_in, xr_in, q_in, kv_in, mixed_in, resid_in, nm_in, cot_in, hid, bias_in,
    result_o, grad_o, fin_gu, fin_d, fin_q, fin_o,
    wq, wo, gu, d, nm, cot, act, gg, kv, bias, resid, hid_own, gres, own, low_own, res_own, gb,
    acc, last_kv, tail_out, tail_in, in_gu, in_d, in_q, in_o, in2_gu, in2_d, in2_q, in2_o,
    send_c, snd, tmp, recv_c1, rcv1,
    send_sems, recv_sems, local_sems, group_send, group_recv, ready,
):
    p = Place()
    links = Links(send_sems, recv_sems, local_sems)
    sibling = p.at(c=1 - p.c)
    load_nm = links.local(nm_in, nm)
    load_gu = links.local(gu_in, gu)
    load_cot = links.local(cot_in, cot)
    load_d = links.local(d_in, d)
    load_resid = links.local(resid_in, resid)
    load_wo = links.local(wo_in, wo)
    load_kv = links.local(kv_in, kv)
    load_bias = links.local(bias_in, bias)
    load_wq = links.local(wq_in, wq)
    load_hid = links.local(hid.at[pl.ds(p.q * OWNED, OWNED)], hid_own)
    greet(p)
    for copy in (load_nm, load_gu, load_cot, load_d):
        copy.wait()

    def feed(t, _):
        part = jnp.dot(nm[t].reshape(256, 2048), gu[...].reshape(2048, 1408), preferred_element_type=f32)
        back = jnp.dot(cot[t].reshape(256, 2048), d[...].reshape(2048, 768), preferred_element_type=f32)
        tail = part[:, 1280:]
        flipped = pltpu.roll(tail, 64, 1)
        lane = lax.broadcasted_iota(jnp.int32, (256, 128), 1)
        for lanes, gate, up in (
            (slice(0, 640), part[:, :640], part[:, 640:1280]),
            (slice(640, 768), tail, flipped),
        ):
            sig = 1 / (1 + jnp.exp(-gate))
            silu = gate * sig
            grad_act = back[:, lanes]
            act[t, :, :, lanes] = (silu * up).astype(bf16).reshape(2, OWNED, -1)
            grad_gate = grad_act * up * sig * (1 + gate * (1 - sig))
            grad_up = grad_act * silu
            if lanes.start == 0:
                gg[t, :, :, :640] = grad_gate.astype(bf16).reshape(2, OWNED, 640)
                gg[t, :, :, 640:1280] = grad_up.astype(bf16).reshape(2, OWNED, 640)
            else:
                both = jnp.where(lane < 64, grad_gate, pltpu.roll(grad_up, 64, 1))
                gg[t, :, :, 1280:] = both.astype(bf16).reshape(2, OWNED, 128)
        return 0

    lax.fori_loop(0, 4, feed, 0)

    def partial_of(left, right, width):
        def partial(n, core):
            return lax.dot_general(
                left[:, core].reshape(512, width),
                right[n].reshape(512, width),
                TURNED,
                preferred_element_type=f32,
            )

        return partial

    def sems(k):
        span = pl.ds(20 * k, 20)
        return group_send.at[span], group_recv.at[span]

    r_mlp = GroupReduce(p, partial_of(gg, gu, 1408), (send_c, recv_c1, tmp, snd, rcv1, own), sems(0))
    r_mlp.run()

    def grads_into(out, left, right, width):
        def body(n, _):
            lanes = pl.ds(pl.multiple_of(n * 256, 256), 256)
            part = lax.dot_general(
                left[:, :, :, lanes].reshape(1024, 256),
                right[...].reshape(1024, width),
                LEFT_TURNED,
                preferred_element_type=f32,
            )
            out[n // 2, n % 2] = part.astype(bf16).reshape(4, 64, width)
            return 0

        lax.fori_loop(0, 8, body, 0)

    load_resid.wait()
    r_mlp.finish()

    def grad_rows(i, _):
        r = pl.ds(i * 16, 16)
        grad = cot[p.x, p.c, r].astype(f32) + norm_back(own[r], resid[r])
        gres[r] = grad
        gb[p.x, p.c, r] = grad.astype(bf16)
        return 0

    lax.fori_loop(0, OWNED // 16, grad_rows, 0)
    g_branch = GroupGather(links, p, gb)
    g_branch.start()
    grads_into(gu, nm, gg, 1408)
    load_xr = links.local(xr_in, nm)
    load_q = links.local(q_in, gg.at[:, :, :, pl.ds(0, 256)])
    load_mixed = links.local(mixed_in, gg.at[:, :, :, pl.ds(256, 256)])
    w_gu = WeightReduce(links, p, gu, in_gu, in2_gu, fin_gu, 768)
    w_gu.start0()
    g_branch.forward()
    r_mlp.sent()

    r_out = GroupReduce(p, partial_of(act, d, 768), (send_c, recv_c1, tmp, snd, rcv1, own), sems(1))
    g_branch.share()
    g_branch.done()
    r_out.run()
    grads_into(d, cot, act, 768)
    w_d = WeightReduce(links, p, d, in_d, in2_d, fin_d, 384)
    w_d.start0()
    r_out.finish()

    def result_rows(i, _):
        r = pl.ds(i * 16, 16)
        res_own[r] = (resid[r] + own[r]).astype(bf16)
        return 0

    lax.fori_loop(0, OWNED // 16, result_rows, 0)
    w_gu.start1()
    for device in (sibling, p.at(x=(p.x + 1) % 4), p.at(x=(p.x + 3) % 4)):
        pl.semaphore_signal(ready, inc=1, device_id=device, device_id_type=MESH)
    b_out = BlockGather(links, p, res_own, result_o)

    for copy in (load_wo, load_q, load_mixed, load_kv, load_bias):
        copy.wait()

    def grad_mixed(t, _):
        out = jnp.dot(gb[t].reshape(256, 2048), wo[...].reshape(2048, 256), preferred_element_type=f32)
        gg[t, :, :, 512:768] = out.astype(bf16).reshape(2, OWNED, 256)
        return 0

    lax.fori_loop(0, 4, grad_mixed, 0)

    def attend_back(block, head):
        lane = pl.multiple_of(head * 128, 128)
        acc[...] = jnp.zeros_like(acc)

        def chunk_body(chunk, _):
            x, core = block * 2 + chunk // 2, chunk % 2
            r = pl.multiple_of(chunk * 128, 128)
            query = gg[x, core, :, pl.ds(lane, 128)]
            grad = gg[x, core, :, pl.ds(lane + 512, 128)]
            keys = kv[block, pl.ds(r, 192), pl.ds(lane, 128)]
            values = kv[block, pl.ds(r, 192), pl.ds(lane + 256, 128)]
            scores = lax.dot_general(query, keys, TURNED, preferred_element_type=f32) * SCALE
            scores = scores + bias[block * 4 + chunk].astype(f32)
            expo = jnp.exp(scores - jnp.max(scores, axis=-1, keepdims=True))
            probs = expo / jnp.sum(expo, axis=-1, keepdims=True)
            probs_low = probs.astype(bf16)
            grad_probs = lax.dot_general(grad, values, TURNED, preferred_element_type=f32)
            inner = jnp.sum(probs * grad_probs, axis=-1, keepdims=True)
            grad_scores = (probs * (grad_probs - inner)).astype(bf16)
            grad_query = jnp.dot(grad_scores, keys, preferred_element_type=f32) * SCALE
            act[x, core, :, pl.ds(lane, 128)] = grad_query.astype(bf16)
            rows = pl.ds(r, 192)
            grad_keys = lax.dot_general(grad_scores, query, LEFT_TURNED, preferred_element_type=f32)
            acc[0, rows] = acc[0, rows] + grad_keys * SCALE
            acc[1, rows] = acc[1, rows] + lax.dot_general(
                probs_low, grad, LEFT_TURNED, preferred_element_type=f32
            )
            return 0

        lax.fori_loop(0, 4, chunk_body, 0)
        for k in range(2):
            lanes = pl.ds(pl.multiple_of(lane + 256 * k, 128), 128)
            tail_out[block, :, lanes] = acc[k, pl.ds(0, WINDOW)].astype(bf16)
            last_kv[block, :, lanes] = acc[k, pl.ds(BLOCK, WINDOW)]

            def store(i, _):
                x, core = block * 2 + i // 2, i % 2
                out = pl.ds(pl.multiple_of(lane + 256 + 256 * k, 128), 128)
                act[x, core, :, out] = acc[k, pl.ds(WINDOW + i * 128, 128)].astype(bf16)
                return 0

            lax.fori_loop(0, 4, store, 0)

    def all_heads(i, _):
        attend_back(i // 2, i % 2)
        return 0

    lax.fori_loop(0, 4, all_heads, 0)
    first = jnp.where(p.z == 0, 1, 0)
    tails = []
    for block in range(2):
        to_y = (p.y + 4 - first) % 4 if block == 0 else p.y
        slot = first if block == 0 else 1 - first
        tails.append(links.send(tail_out.at[block], tail_in.at[slot], p.at(y=to_y, z=(p.z + 3) % 4)))
    w_gu.start2()
    w_d.start1()
    r_out.sent()
    b_out.share()
    for copy in tails:
        copy.wait_recv()
    for block in range(2):
        whole = last_kv[block] + tail_in[block].astype(f32)
        act[2 * block + 1, 1, pl.ds(64, 64), 256:] = whole.astype(bf16)

    load_wq.wait()
    r_attn = GroupReduce(p, partial_of(act, wq, 768), (send_c, recv_c1, tmp, snd, rcv1, own), sems(2))
    pl.semaphore_wait(ready, 3)
    r_attn.run()
    load_xr.wait()
    grads_into(wq, nm, act, 768)
    w_q = WeightReduce(links, p, wq, in_q, in2_q, fin_q, 384)
    w_q.start0()
    w_gu.start3()
    w_d.start2()
    mixed_part = gg.at[:, :, :, pl.ds(256, 256)]
    grads_into(wo, gb, mixed_part, 256)
    w_o = WeightReduce(links, p, wo, in_o, in2_o, fin_o, 128)
    w_o.start0()
    load_hid.wait()
    r_attn.finish()

    def input_rows(i, _):
        r = pl.ds(i * 16, 16)
        low_own[r] = (gres[r] + norm_back(own[r], hid_own[r].astype(f32))).astype(bf16)
        return 0

    lax.fori_loop(0, OWNED // 16, input_rows, 0)
    b_in = BlockGather(links, p, low_own, grad_o)
    w_q.start1()
    w_gu.start4()
    w_d.start3()
    w_o.start1()
    w_q.start2()
    w_o.start2()
    w_d.start4()
    w_q.start3()
    w_o.start3()
    b_in.share()
    w_q.start4()
    w_o.start4()
    for item in (b_out, b_in, w_gu, w_d, w_q, w_o):
        item.done()
    r_attn.sent()
    links.finish()


def backward_call(wq, wo, gu, d, xr, q, kv, mixed, resid, nm, cot, hid, bias):
    sds = jax.ShapeDtypeStruct
    group = (4, 2, OWNED)
    vm = pltpu.VMEM
    return pl.pallas_call(
        backward_kernel,
        out_shape=(
            sds((BLOCK, 2048), bf16),
            sds((BLOCK, 2048), bf16),
            sds((2, 64, 1408), bf16),
            sds((2, 64, 768), bf16),
            sds((2, 64, 768), bf16),
            sds((2, 64, 256), bf16),
        ),
        in_specs=[ANY] * 13,
        out_specs=[ANY] * 6,
        scratch_shapes=[
            vm((4, 2, 4, 64, 768), bf16),
            vm((4, 2, 4, 64, 256), bf16),
            vm((4, 2, 4, 64, 1408), bf16),
            vm((4, 2, 4, 64, 768), bf16),
            vm(group + (2048,), bf16),
            vm(group + (2048,), bf16),
            vm(group + (768,), bf16),
            vm(group + (1408,), bf16),
            vm((2, BLOCK + WINDOW, 512), bf16),
            vm((8, 128, 192), bf16),
            vm((OWNED, 2048), f32),
            vm((OWNED, 2048), bf16),
            vm((OWNED, 2048), f32),
            vm((OWNED, 2048), f32),
            vm((OWNED, 2048), bf16),
            vm((OWNED, 2048), bf16),
            vm(group + (2048,), bf16),
            vm((2, BLOCK + WINDOW, 128), f32),
            vm((2, WINDOW, 512), f32),
            vm((2, WINDOW, 512), bf16),
            vm((2, WINDOW, 512), bf16),
            vm((6, 4, 64, 1408), bf16),
            vm((6, 4, 64, 768), bf16),
            vm((6, 4, 64, 768), bf16),
            vm((6, 4, 64, 256), bf16),
            vm((6, 64, 1408), bf16),
            vm((6, 64, 768), bf16),
            vm((6, 64, 768), bf16),
            vm((6, 64, 256), bf16),
            vm((4, 4, OWNED, 512), bf16),
            vm((4, 6, 64, 512), bf16),
            vm((4, OWNED, 512), f32),
            vm((4, 4, OWNED, 512), bf16),
            vm((4, 6, 64, 512), bf16),
            pltpu.SemaphoreType.DMA((130,)),
            pltpu.SemaphoreType.DMA((130,)),
            pltpu.SemaphoreType.DMA((24,)),
            pltpu.SemaphoreType.DMA((60,)),
            pltpu.SemaphoreType.DMA((60,)),
            pltpu.SemaphoreType.REGULAR,
        ],
        compiler_params=pltpu.CompilerParams(
            collective_id=1, has_side_effects=True, vmem_limit_bytes=60 * 2**20
        ),
        name="backward",
    )(wq, wo, gu, d, xr, q, kv, mixed, resid, nm, cot, hid, bias)


def per_device(
    hidden_in,
    norm_gain_attn,
    w_query,
    w_key,
    w_value,
    w_out,
    norm_gain_mlp,
    w_gate,
    w_up,
    w_down,
    lengths,
    cotangent,
):
    xh = lax.axis_index("xh")
    gain_attn = norm_gain_attn.astype(f32)[:, None]
    gain_mlp = norm_gain_mlp.astype(f32)[:, None]
    scaled = lambda w, g: (w.astype(f32) * g).astype(bf16)
    pk_q, pk_o = pack_attn(
        scaled(w_query, gain_attn), scaled(w_key, gain_attn), scaled(w_value, gain_attn), w_out.T
    )
    pk_gu, pk_d = pack_ff(scaled(w_gate, gain_mlp), scaled(w_up, gain_mlp), w_down.T)
    bias = attention_bias(lengths)
    wq, wo, gu, d, xr, q, kv, mixed, resid, nm, cot = forward_call(
        pk_q, pk_o, pk_gu, pk_d, hidden_in, cotangent, bias
    )
    group = (4, 2, OWNED)
    result, input_grad, fin_gu, fin_d, fin_q, fin_o = backward_call(
        wq, wo, gu, d,
        xr.reshape(group + (2048,)),
        q.reshape(group + (256,)),
        kv,
        mixed.reshape(group + (256,)),
        resid,
        nm,
        cot.reshape(group + (2048,)),
        hidden_in,
        bias,
    )

    def joined(fin, *spans):
        return jnp.concatenate([fin[k][:, s] for k in range(2) for s in spans], axis=1).astype(f32)

    dq, dk, dv = (joined(fin_q, slice(256 * i, 256 * i + 256)) for i in range(3))
    dg = joined(fin_gu, slice(0, 640), slice(1280, 1328))
    du = joined(fin_gu, slice(640, 1280), slice(1344, 1392))

    def dots(pairs):
        return sum(jnp.sum(w.astype(f32) * g, axis=1) for w, g in pairs)

    grads_gain = jnp.stack(
        [dots([(w_query, dq), (w_key, dk), (w_value, dv)]), dots([(w_gate, dg), (w_up, du)])]
    )
    grads_gain = grads_gain + flip(grads_gain, "xl")
    grads_gain = grads_gain + flip(grads_gain, "c")
    return (
        result,
        input_grad,
        grads_gain[0],
        dq * gain_attn,
        dk * gain_attn,
        dv * gain_attn,
        joined(fin_o, slice(0, 256)).T,
        grads_gain[1],
        dg * gain_mlp,
        du * gain_mlp,
        joined(fin_d, slice(0, 688)).T,
    )


def solution(mesh):
    mesh = Mesh(mesh.devices.reshape(4, 2, 4, 2, 2), AXES)
    seq, head = ("y", "xh", "z"), ("xl", "c")
    rows, cols, flat, turned = P(seq, None), P(seq, head), P(seq), P(head, seq)
    return jax.shard_map(
        per_device,
        mesh=mesh,
        in_specs=(rows, flat, cols, cols, cols, turned, flat, cols, cols, turned, P(), rows),
        out_specs=(rows, rows, flat, cols, cols, cols, turned, flat, cols, cols, turned),
        check_vma=False,
    )
```

```python
import jax
import jax.numpy as jnp
from jax import lax
from jax.experimental import pallas as pl
from jax.experimental.pallas import tpu as pltpu
from jax.sharding import Mesh, PartitionSpec as P

HEAD_DIM = 128
WINDOW = 64
BLOCK = 512
OWNED = 128
AXES = ("y", "xh", "z", "xl", "c")

epsilon = 1e-05
masked_score = -1e30
f32 = jnp.float32
bf16 = jnp.bfloat16


def flip(value, axis):
    return lax.ppermute(value, axis, [(0, 1), (1, 0)])


MESH = pl.DeviceIdType.MESH
SCALE = HEAD_DIM ** (-0.5)
ANY = pl.BlockSpec(memory_space=pl.ANY)
TURNED = (((1,), (1,)), ((), ()))
LEFT_TURNED = (((0,), (0,)), ((), ()))


class Place:
    def __init__(self):
        self.y, self.z, self.c = lax.axis_index("y"), lax.axis_index("z"), lax.axis_index("c")
        self.xh, self.xl = lax.axis_index("xh"), lax.axis_index("xl")
        self.x = self.xh * 2 + self.xl
        self.q = self.xl * 2 + self.c

    def at(self, y=None, x=None, z=None, c=None):
        y = self.y if y is None else y
        x = self.x if x is None else x
        z = self.z if z is None else z
        c = self.c if c is None else c
        return (y, x // 2, z, x % 2, c)


class Links:
    def __init__(self, send_sems, recv_sems, local_sems):
        self.send_sems, self.recv_sems, self.local_sems = send_sems, recv_sems, local_sems
        self.count, self.local_count, self.started = 0, 0, []

    def send(self, src, dst, device):
        copy = self.prepare(src, dst, device)
        copy.start()
        return copy

    def prepare(self, src, dst, device):
        copy = pltpu.make_async_remote_copy(
            src_ref=src,
            dst_ref=dst,
            send_sem=self.send_sems.at[self.count],
            recv_sem=self.recv_sems.at[self.count],
            device_id=device,
            device_id_type=MESH,
        )
        self.count += 1
        self.started.append(copy)
        return copy

    def local(self, src, dst):
        copy = pltpu.make_async_copy(src, dst, self.local_sems.at[self.local_count])
        self.local_count += 1
        copy.start()
        return copy

    def settle(self):
        for copy in self.started:
            copy.wait_send()
        self.started = []

    finish = settle


class WeightGather:
    def __init__(self, links, place, pack, whole, cut):
        self.links, self.place, self.whole = links, place, whole
        cols = whole.shape[-1]
        self.parts = (pl.ds(0, cut), pl.ds(cut, cols - cut))
        self.swap = links.send(
            pack.at[1 - place.xh], whole.at[place.y, place.xh, place.z], place.at(x=(place.x + 2) % 4)
        )
        self.mine = links.local(pack.at[place.xh], whole.at[place.y, place.xh, place.z])

    def send(self, ref, device):
        return self.links.send(ref, ref, device)

    def near(self, view_z, view_y):
        p = self.place
        first, second = self.parts
        zs = (p.at(z=(p.z + 1) % 4), p.at(z=(p.z + 3) % 4))
        ys = (p.at(y=(p.y + 1) % 4), p.at(y=(p.y + 3) % 4))
        (ref_z, axis_z), (ref_y, axis_y) = view_z, view_y
        to = {"z": zs, "y": ys}
        self.got = [
            self.send(ref_z, to[axis_z][0]),
            self.send(ref_y, to[axis_y][0]),
            self.send(ref_z, to[axis_z][1]),
            self.send(ref_y, to[axis_y][1]),
        ]

    def wait(self):
        for copy in self.got:
            copy.wait_recv()

    def start0(self):
        p, w = self.place, self.whole
        first, second = self.parts
        self.swap.wait_recv()
        self.mine.wait()
        self.near(
            (w.at[p.y, :, p.z, :, first], "z"),
            (w.at[p.y, :, p.z, :, second], "y"),
        )

    def start1(self):
        p, w = self.place, self.whole
        first, second = self.parts
        self.wait()
        zn, zp, yn, yp = (p.z + 1) % 4, (p.z + 3) % 4, (p.y + 1) % 4, (p.y + 3) % 4
        self.got = [
            self.send(w.at[p.y, 0, zp, :, first], p.at(z=zn)),
            self.send(w.at[yp, 0, p.z, :, second], p.at(y=yn)),
            self.send(w.at[p.y, 1, zn, :, first], p.at(z=zp)),
            self.send(w.at[yn, 1, p.z, :, second], p.at(y=yp)),
        ]

    def start2(self):
        p, w = self.place, self.whole
        first, second = self.parts
        self.wait()
        self.near(
            (w.at[:, :, p.z, :, second], "z"),
            (w.at[p.y, :, :, :, first], "y"),
        )

    def start3(self):
        p, w = self.place, self.whole
        first, second = self.parts
        self.wait()
        zn, zp, yn, yp = (p.z + 1) % 4, (p.z + 3) % 4, (p.y + 1) % 4, (p.y + 3) % 4
        self.got = [
            self.send(w.at[yp, 0, :, :, first], p.at(y=yn)),
            self.send(w.at[:, 0, zp, :, second], p.at(z=zn)),
            self.send(w.at[yn, 1, :, :, first], p.at(y=yp)),
            self.send(w.at[:, 1, zn, :, second], p.at(z=zp)),
        ]

    def done(self):
        self.wait()


def greet(place):
    p = place
    barrier = pltpu.get_barrier_semaphore()
    partners = (
        p.at(z=(p.z + 1) % 4),
        p.at(z=(p.z + 3) % 4),
        p.at(y=(p.y + 1) % 4),
        p.at(y=(p.y + 3) % 4),
        p.at(x=(p.x + 1) % 4),
        p.at(x=(p.x + 3) % 4),
        p.at(x=(p.x + 2) % 4),
        p.at(c=1 - p.c),
    )
    for device in partners:
        pl.semaphore_signal(barrier, inc=1, device_id=device, device_id_type=MESH)

    @pl.when(p.z == 3)
    def _():
        pl.semaphore_signal(barrier, inc=1, device_id=p.at(y=(p.y + 1) % 4, z=0 * p.z), device_id_type=MESH)

    @pl.when(p.z == 0)
    def _():
        pl.semaphore_signal(barrier, inc=1, device_id=p.at(y=(p.y + 3) % 4, z=0 * p.z + 3), device_id_type=MESH)

    pl.semaphore_wait(barrier, 8 + jnp.where((p.z == 3) | (p.z == 0), 1, 0))


def unit_scale(values):
    return values * lax.rsqrt(jnp.mean(values * values, axis=-1, keepdims=True) + epsilon)


class WeightReduce:
    def __init__(self, links, place, total, first_in, second_in, out, cut):
        self.links, self.place, self.total, self.out = links, place, total, out
        self.one, self.two = first_in, second_in
        cols = total.shape[-1]
        self.cols = cols
        self.parts = (pl.ds(0, cut), pl.ds(cut, cols - cut))
        p = place
        self.yn, self.yp, self.yf = (p.y + 1) % 4, (p.y + 3) % 4, (p.y + 2) % 4
        self.zn, self.zp, self.zf = (p.z + 1) % 4, (p.z + 3) % 4, (p.z + 2) % 4
        self.next_y, self.prev_y = p.at(y=self.yn), p.at(y=self.yp)
        self.next_z, self.prev_z = p.at(z=self.zn), p.at(z=self.zp)

    def start0(self):
        a, b = self.parts
        t, one, send = self.total, self.one, self.links.send
        self.far = [
            send(t.at[self.yf, 0, :, :, a], one.at[0, :, :, a], self.next_y),
            send(t.at[:, 0, self.zf, :, b], one.at[0, :, :, b], self.next_z),
            send(t.at[self.yf, 1, :, :, a], one.at[2, :, :, a], self.prev_y),
            send(t.at[:, 1, self.zf, :, b], one.at[2, :, :, b], self.prev_z),
        ]
        self.near = [
            send(t.at[self.yn, 1, :, :, a], one.at[1, :, :, a], self.next_y),
            send(t.at[:, 1, self.zn, :, b], one.at[1, :, :, b], self.next_z),
            send(t.at[self.yp, 0, :, :, a], one.at[3, :, :, a], self.prev_y),
            send(t.at[:, 0, self.zp, :, b], one.at[3, :, :, b], self.prev_z),
        ]

    def add(self, target, sources, rows):
        def body(i, _):
            ref = target(i)
            value = ref[...].astype(f32)
            for source in sources:
                value = value + source(i)[...].astype(f32)
            ref[...] = value.astype(bf16)
            return 0

        lax.fori_loop(0, rows, body, 0)

    def start1(self):
        a, b = self.parts
        t, one, send = self.total, self.one, self.links.send
        yn, yp, zn, zp = self.yn, self.yp, self.zn, self.zp
        self.sums = []
        self.far[0].wait_recv()
        self.add(lambda i: t.at[yn, 0, i, :, a], [lambda i: one.at[0, i, :, a]], 4)
        self.sums.append(send(t.at[yn, 0, :, :, a], one.at[4, :, :, a], self.next_y))
        self.far[1].wait_recv()
        self.add(lambda i: t.at[i, 0, zn, :, b], [lambda i: one.at[0, i, :, b]], 4)
        self.sums.append(send(t.at[:, 0, zn, :, b], one.at[4, :, :, b], self.next_z))
        self.far[2].wait_recv()
        self.add(lambda i: t.at[yp, 1, i, :, a], [lambda i: one.at[2, i, :, a]], 4)
        self.sums.append(send(t.at[yp, 1, :, :, a], one.at[5, :, :, a], self.prev_y))
        self.far[3].wait_recv()
        self.add(lambda i: t.at[i, 1, zp, :, b], [lambda i: one.at[2, i, :, b]], 4)
        self.sums.append(send(t.at[:, 1, zp, :, b], one.at[5, :, :, b], self.prev_z))

    def start2(self):
        a, b = self.parts
        t, one, two, send = self.total, self.one, self.two, self.links.send
        p = self.place
        for copy in self.near + self.sums:
            copy.wait_recv()
        self.add(lambda i: t.at[p.y, 0, i, :, a], [lambda i: one.at[3, i, :, a], lambda i: one.at[4, i, :, a]], 4)
        self.add(lambda i: t.at[p.y, 1, i, :, a], [lambda i: one.at[1, i, :, a], lambda i: one.at[5, i, :, a]], 4)
        self.add(lambda i: t.at[i, 0, p.z, :, b], [lambda i: one.at[3, i, :, b], lambda i: one.at[4, i, :, b]], 4)
        self.add(lambda i: t.at[i, 1, p.z, :, b], [lambda i: one.at[1, i, :, b], lambda i: one.at[5, i, :, b]], 4)
        self.far = [
            send(t.at[p.y, 0, self.zf, :, a], two.at[0, :, a], self.next_z),
            send(t.at[self.yf, 0, p.z, :, b], two.at[0, :, b], self.next_y),
            send(t.at[p.y, 1, self.zf, :, a], two.at[2, :, a], self.prev_z),
            send(t.at[self.yf, 1, p.z, :, b], two.at[2, :, b], self.prev_y),
        ]
        self.near = [
            send(t.at[p.y, 1, self.zn, :, a], two.at[1, :, a], self.next_z),
            send(t.at[self.yn, 1, p.z, :, b], two.at[1, :, b], self.next_y),
            send(t.at[p.y, 0, self.zp, :, a], two.at[3, :, a], self.prev_z),
            send(t.at[self.yp, 0, p.z, :, b], two.at[3, :, b], self.prev_y),
        ]

    def plus(self, target, *sources):
        value = target[...].astype(f32)
        for source in sources:
            value = value + source[...].astype(f32)
        target[...] = value.astype(bf16)

    def start3(self):
        a, b = self.parts
        t, two, send = self.total, self.two, self.links.send
        p = self.place
        yn, yp, zn, zp = self.yn, self.yp, self.zn, self.zp
        self.sums = []
        for k, ref, lanes, slot, other, device in (
            (0, t.at[p.y, 0, zn, :, a], a, 0, 4, self.next_z),
            (1, t.at[yn, 0, p.z, :, b], b, 0, 4, self.next_y),
            (2, t.at[p.y, 1, zp, :, a], a, 2, 5, self.prev_z),
            (3, t.at[yp, 1, p.z, :, b], b, 2, 5, self.prev_y),
        ):
            self.far[k].wait_recv()
            self.plus(ref, two.at[slot, :, lanes])
            self.sums.append(send(ref, two.at[other, :, lanes], device))

    def start4(self):
        t, two, out = self.total, self.two, self.out
        p = self.place
        for copy in self.near + self.sums:
            copy.wait_recv()
        self.plus(t.at[p.y, 0, p.z], two.at[3], two.at[4])
        self.plus(t.at[p.y, 1, p.z], two.at[1], two.at[5])
        self.swap = self.links.send(t.at[p.y, 1 - p.xh, p.z], out.at[p.xh], p.at(x=(p.x + 2) % 4))
        self.mine = self.links.local(t.at[p.y, p.xh, p.z], out.at[p.xh])

    def done(self):
        self.swap.wait_recv()
        self.mine.wait()


class GroupReduce:
    def __init__(self, place, partial, bufs, sems):
        self.place, self.partial = place, partial
        self.send_c, self.recv_c, self.tmp, self.snd, self.rcv, self.own = bufs
        self.send_sems, self.recv_sems = sems

    def copy(self, src, dst, index, device):
        return pltpu.make_async_remote_copy(
            src_ref=src,
            dst_ref=dst,
            send_sem=self.send_sems.at[index],
            recv_sem=self.recv_sems.at[index],
            device_id=device,
            device_id_type=MESH,
        )

    def crossing(self, n):
        return self.copy(self.send_c.at[n], self.recv_c.at[n], n, self.place.at(c=1 - self.place.c))

    def to_next(self, n):
        pair = pl.ds(0, 2)
        return self.copy(
            self.snd.at[n, pair], self.rcv.at[n, pair], 4 + n, self.place.at(x=(self.place.x + 1) % 4)
        )

    def to_prev(self, n):
        pair = pl.ds(2, 2)
        return self.copy(
            self.snd.at[n, pair], self.rcv.at[n, pair], 8 + n, self.place.at(x=(self.place.x + 3) % 4)
        )

    def sum_next(self, n):
        return self.copy(
            self.snd.at[n, 4], self.rcv.at[n, 4], 12 + n, self.place.at(x=(self.place.x + 1) % 4)
        )

    def sum_prev(self, n):
        return self.copy(
            self.snd.at[n, 5], self.rcv.at[n, 5], 16 + n, self.place.at(x=(self.place.x + 3) % 4)
        )

    def sibling_part(self, n):
        part = self.partial(n, 1 - self.place.c)
        self.send_c[n] = part.astype(bf16).reshape(4, OWNED, 512)
        self.crossing(n).start()

    def own_part(self, n, launch):
        p, tmp, snd = self.place, self.tmp, self.snd
        part = self.partial(n, p.c).reshape(4, OWNED, 512)
        self.crossing(n).wait_recv()
        tmp[...] = part + self.recv_c[n].astype(f32)
        far, nxt, prev = (p.x + 2) % 4, (p.x + 1) % 4, (p.x + 3) % 4
        low, high = pl.ds(0, 64), pl.ds(64, 64)
        snd[n, 0] = tmp[far, low].astype(bf16)
        snd[n, 1] = tmp[nxt, high].astype(bf16)
        if launch:
            self.to_next(n).start()
        snd[n, 2] = tmp[far, high].astype(bf16)
        snd[n, 3] = tmp[prev, low].astype(bf16)
        if launch:
            self.to_prev(n).start()
        snd[n, 4] = tmp[nxt, low].astype(bf16)
        snd[n, 5] = tmp[prev, high].astype(bf16)
        self.own[:, pl.ds(pl.multiple_of(n * 512, 512), 512)] = tmp[p.x]

    def pass_on(self, n):
        snd, rcv = self.snd, self.rcv
        self.to_next(n).wait_recv()
        snd[n, 4] = (snd[n, 4].astype(f32) + rcv[n, 0].astype(f32)).astype(bf16)
        self.sum_next(n).start()
        self.to_prev(n).wait_recv()
        snd[n, 5] = (snd[n, 5].astype(f32) + rcv[n, 2].astype(f32)).astype(bf16)
        self.sum_prev(n).start()

    def run(self, launch=True):
        def body(i, _):
            @pl.when(i < 4)
            def _():
                self.sibling_part(i)

            @pl.when((i >= 1) & (i < 5))
            def _():
                self.own_part(i - 1, launch)

            if launch:

                @pl.when(i >= 2)
                def _():
                    self.pass_on(i - 2)

            return 0

        lax.fori_loop(0, 6 if launch else 5, body, 0)

    def launch(self):
        def body(n, _):
            self.to_next(n).start()
            self.to_prev(n).start()
            return 0

        lax.fori_loop(0, 4, body, 0)

    def pass_all(self):
        def body(n, _):
            self.pass_on(n)
            return 0

        lax.fori_loop(0, 4, body, 0)

    def finish(self):
        def body(n, _):
            lanes = pl.ds(pl.multiple_of(n * 512, 512), 512)
            low, high = pl.ds(0, 64), pl.ds(64, 64)
            rcv, own = self.rcv, self.own
            self.sum_next(n).wait_recv()
            own[low, lanes] = own[low, lanes] + rcv[n, 3].astype(f32) + rcv[n, 4].astype(f32)
            self.sum_prev(n).wait_recv()
            own[high, lanes] = own[high, lanes] + rcv[n, 1].astype(f32) + rcv[n, 5].astype(f32)
            return 0

        lax.fori_loop(0, 4, body, 0)

    def sent(self):
        def body(n, _):
            for copy in (self.crossing, self.to_next, self.to_prev, self.sum_next, self.sum_prev):
                copy(n).wait_send()
            return 0

        lax.fori_loop(0, 4, body, 0)


class GroupGather:
    def __init__(self, links, place, whole):
        self.links, self.place, self.whole = links, place, whole
        self.low, self.high = pl.ds(0, 64), pl.ds(64, 64)

    def send(self, ref, device):
        return self.links.send(ref, ref, device)

    def start(self):
        p, w = self.place, self.whole
        self.nxt, self.prev, self.far = (p.x + 1) % 4, (p.x + 3) % 4, (p.x + 2) % 4
        self.to_next, self.to_prev = p.at(x=self.nxt), p.at(x=self.prev)
        self.sibling = p.at(c=1 - p.c)
        low, high = w.at[p.x, p.c, self.low], w.at[p.x, p.c, self.high]
        self.first = [self.send(low, self.to_next), self.send(high, self.to_prev)]
        self.second = [self.send(high, self.to_next), self.send(low, self.to_prev)]
        tiles = (p.x, self.prev, self.nxt, self.far)
        self.paired = [self.later(w.at[x, p.c], self.sibling) for x in tiles]
        self.paired[0].start()
        self.third = [
            self.later(w.at[self.prev, p.c, self.low], self.to_next),
            self.later(w.at[self.nxt, p.c, self.high], self.to_prev),
        ]

    def later(self, ref, device):
        return self.links.prepare(ref, ref, device)

    def forward(self):
        for k in range(2):
            self.first[k].wait_recv()
            self.third[k].start()

    def share_near(self):
        for k in range(2):
            self.second[k].wait_recv()
            self.paired[1 + k].start()

    def share_far(self):
        for copy in self.third:
            copy.wait_recv()
        self.paired[3].start()

    def ready(self, k):
        self.paired[k].wait_recv()


class BlockGather:
    def __init__(self, links, place, own, out):
        p = place
        self.links, self.place, self.out = links, place, out
        self.sibling = p.at(c=1 - p.c)
        mine = out.at[pl.ds(p.q * OWNED, OWNED)]
        self.local = links.local(own, mine)
        self.across = links.send(own, mine, p.at(x=p.xh * 2 + 1 - p.xl))
        self.paired = [links.send(own, mine, self.sibling)]

    def share(self):
        p = self.place
        self.across.wait_recv()
        theirs = self.out.at[pl.ds(((1 - p.xl) * 2 + p.c) * OWNED, OWNED)]
        self.paired.append(self.links.send(theirs, theirs, self.sibling))

    def done(self):
        for copy in self.paired:
            copy.wait_recv()
        self.local.wait()


def norm_back(e, values):
    r = lax.rsqrt(jnp.mean(values * values, axis=-1, keepdims=True) + epsilon)
    return r * e - values * r**3 * jnp.mean(e * values, axis=-1, keepdims=True)


def block_kernel(
    lengths, pk_q, pk_o, pk_gu, pk_d, hid, cot_in,
    result_o, grad_o, fin_gu, fin_d, fin_q, fin_o, xr_o, qm_o,
    wq, wo, gu, d, nm, cot, act, gg, kv, resid, hid_own, gres, own, low_own, res_own, gb,
    acc, last_kv, tail_out, tail_in, in_gu, in_d, in_q, in_o, in2_gu, in2_d, in2_q, in2_o,
    send_c, snd, tmp, recv_c, rcv,
    send_sems, recv_sems, local_sems, group_send, group_recv, ready,
):
    p = Place()
    links = Links(send_sems, recv_sems, local_sems)
    sibling = p.at(c=1 - p.c)
    facing = p.at(x=3 - p.x)
    hidg, xr = gb, nm

    own_pair = pl.ds(2 * p.xh, 2)
    own_hidden = links.local(hid, hidg.at[own_pair])
    load_hid = links.local(hid.at[p.xl, p.c], hid_own)
    own_cot = links.local(cot_in, cot.at[own_pair])
    greet(p)

    def cross(ref, whole):
        return [links.send(ref.at[p.c, k], whole.at[2 * p.xh + p.c, k], facing) for k in range(2)]

    def handed(whole, copies):
        shared = []
        for k in range(2):
            copies[k].wait_recv()
            part = whole.at[2 * (1 - p.xh) + p.c, k]
            shared.append(links.send(part, part, sibling))
        return shared

    g_q = WeightGather(links, p, pk_q, wq, 384)
    hidden_sent = cross(hid, hidg)
    g_o = WeightGather(links, p, pk_o, wo, 128)
    g_gu = WeightGather(links, p, pk_gu, gu, 768)
    g_d = WeightGather(links, p, pk_d, d, 384)
    g_q.start0()
    g_o.start0()

    def norm_rows(tile):
        def body(i, _):
            core, r = i // 4, pl.ds((i % 4) * 32, 32)
            xr[tile, core, r] = unit_scale(hidg[tile, core, r].astype(f32)).astype(bf16)
            return 0

        lax.fori_loop(0, 8, body, 0)

    own_hidden.wait()
    norm_rows(2 * p.xh)
    norm_rows(2 * p.xh + 1)
    g_q.start1()
    g_o.start1()
    g_q.start2()
    g_o.start2()
    g_gu.start0()
    g_d.start0()
    shared = handed(hidg, hidden_sent)
    cot_sent = cross(cot_in, cot)
    norm_rows(2 * (1 - p.xh) + p.c)
    for copy in shared:
        copy.wait_recv()
    norm_rows(2 * (1 - p.xh) + 1 - p.c)
    xr_spill = links.local(xr, xr_o)
    g_q.start3()
    g_o.start3()
    g_gu.start1()
    g_d.start1()
    g_q.done()

    def project(t, _):
        w = wq[...].reshape(2048, 768)
        out = jnp.dot(xr[t].reshape(256, 2048), w, preferred_element_type=f32).astype(bf16)
        gg[t, :, :, 0:256] = out[:, :256].reshape(2, OWNED, 256)
        kv[t // 2, pl.ds((t % 2) * 256 + WINDOW, 256)] = out[:, 256:]
        return 0

    lax.fori_loop(0, 4, project, 0)

    tails = []
    last = jnp.where(p.z == 3, 1, 0)
    for block in range(2):
        to_y = p.y if block == 0 else (p.y + last) % 4
        slot = last if block == 0 else 1 - last
        tails.append(
            links.send(
                kv.at[block, pl.ds(BLOCK, WINDOW)],
                kv.at[slot, pl.ds(0, WINDOW)],
                p.at(y=to_y, z=(p.z + 1) % 4),
            )
        )
    g_gu.start2()

    end0 = lengths[0]
    end1 = end0 + lengths[1]

    def masked(scores, block, chunk):
        start = (p.y * 8 + block * 4 + p.z) * BLOCK + chunk * 128
        query = start + lax.broadcasted_iota(jnp.int32, (128, 192), 0)
        key = start - WINDOW + lax.broadcasted_iota(jnp.int32, (128, 192), 1)
        seen = (key <= query) & (key > query - WINDOW) & (key >= 0)
        for end in (end0, end1):
            seen = seen & ((key >= end) | (query < end))
        return jnp.where(seen, scores, masked_score)

    def probabilities(query, keys, block, chunk):
        scores = lax.dot_general(query, keys, TURNED, preferred_element_type=f32) * SCALE
        scores = masked(scores, block, chunk)
        expo = jnp.exp(scores - jnp.max(scores, axis=-1, keepdims=True))
        return expo / jnp.sum(expo, axis=-1, keepdims=True)

    def attend(block, chunk, head):
        x, core = block * 2 + chunk // 2, chunk % 2
        r, lane = pl.multiple_of(chunk * 128, 128), pl.multiple_of(head * 128, 128)
        query = gg[x, core, :, pl.ds(lane, 128)]
        keys = kv[block, pl.ds(r, 192), pl.ds(lane, 128)]
        values = kv[block, pl.ds(r, 192), pl.ds(lane + 256, 128)]
        probs = probabilities(query, keys, block, chunk).astype(bf16)
        out = jnp.dot(probs, values, preferred_element_type=f32)
        gg[x, core, :, pl.ds(lane + 256, 128)] = out.astype(bf16)

    def inner(i, _):
        attend(i // 6, (i % 6) // 2 + 1, i % 2)
        return 0

    lax.fori_loop(0, 12, inner, 0)
    for copy in tails:
        copy.wait_recv()

    def first_chunk(i, _):
        attend(i // 2, 0, i % 2)
        return 0

    lax.fori_loop(0, 4, first_chunk, 0)
    mixed = gg.at[:, :, :, pl.ds(256, 256)]
    g_o.done()
    xr_spill.wait()

    def partial_of(left, right, width, start=0):
        def partial(n, core):
            return lax.dot_general(
                left[:, core, :, start : start + width].reshape(512, width),
                right[n].reshape(512, width),
                TURNED,
                preferred_element_type=f32,
            )

        return partial

    def group_reduce(k, partial):
        span = pl.ds(20 * k, 20)
        return GroupReduce(
            p, partial, (send_c, recv_c, tmp, snd, rcv, own), (group_send.at[span], group_recv.at[span])
        )

    r_branch = group_reduce(0, partial_of(gg, wo, 256, 256))
    r_branch.run()
    cot_shared = handed(cot, cot_sent)
    g_d.start2()
    g_gu.start3()
    load_hid.wait()
    r_branch.finish()

    def resid_rows(i, _):
        r = pl.ds(i * 16, 16)
        total = hid_own[r].astype(f32) + own[r]
        resid[r] = total
        nm[p.x, p.c, r] = unit_scale(total).astype(bf16)
        return 0

    lax.fori_loop(0, OWNED // 16, resid_rows, 0)
    g_nm = GroupGather(links, p, nm)
    g_nm.start()
    q_spill = links.local(gg.at[:, :, :, pl.ds(0, 512)], qm_o)
    g_gu.done()
    g_d.start3()
    own_cot.wait()
    for copy in cot_shared:
        copy.wait_recv()
    q_spill.wait()
    g_nm.forward()
    g_d.done()
    g_nm.ready(0)

    def feed(k, _):
        @pl.when(k == 1)
        def _():
            g_nm.share_near()
            g_nm.ready(1)

        @pl.when(k == 2)
        def _():
            g_nm.ready(2)

        @pl.when(k == 3)
        def _():
            g_nm.share_far()
            g_nm.ready(3)

        t = (p.x + jnp.where(k == 0, 0, jnp.where(k == 1, 3, k - 1))) % 4
        part = jnp.dot(nm[t].reshape(256, 2048), gu[...].reshape(2048, 1408), preferred_element_type=f32)
        back = jnp.dot(cot[t].reshape(256, 2048), d[...].reshape(2048, 768), preferred_element_type=f32)
        tail = part[:, 1280:]
        flipped = pltpu.roll(tail, 64, 1)
        lane = lax.broadcasted_iota(jnp.int32, (256, 128), 1)
        for lanes, gate, up in (
            (slice(0, 640), part[:, :640], part[:, 640:1280]),
            (slice(640, 768), tail, flipped),
        ):
            sig = 1 / (1 + jnp.exp(-gate))
            silu = gate * sig
            grad_act = back[:, lanes]
            act[t, :, :, lanes] = (silu * up).astype(bf16).reshape(2, OWNED, -1)
            grad_gate = grad_act * up * sig * (1 + gate * (1 - sig))
            grad_up = grad_act * silu
            if lanes.start == 0:
                gg[t, :, :, :640] = grad_gate.astype(bf16).reshape(2, OWNED, 640)
                gg[t, :, :, 640:1280] = grad_up.astype(bf16).reshape(2, OWNED, 640)
            else:
                both = jnp.where(lane < 64, grad_gate, pltpu.roll(grad_up, 64, 1))
                gg[t, :, :, 1280:] = both.astype(bf16).reshape(2, OWNED, 128)
        return 0

    lax.fori_loop(0, 4, feed, 0)

    r_branch.sent()
    links.settle()
    r_mlp = group_reduce(1, partial_of(gg, gu, 1408))
    r_mlp.run()

    def grads_into(out, left, right, width):
        def body(n, _):
            lanes = pl.ds(pl.multiple_of(n * 256, 256), 256)
            part = lax.dot_general(
                left[:, :, :, lanes].reshape(1024, 256),
                right[...].reshape(1024, width),
                LEFT_TURNED,
                preferred_element_type=f32,
            )
            out[n // 2, n % 2] = part.astype(bf16).reshape(4, 64, width)
            return 0

        lax.fori_loop(0, 8, body, 0)

    grads_into(gu, nm, gg, 1408)
    w_gu = WeightReduce(links, p, gu, in_gu, in2_gu, fin_gu, 768)
    w_gu.start0()
    load_xr = links.local(xr_o, nm)
    load_qm = links.local(qm_o, gg.at[:, :, :, pl.ds(0, 512)])
    r_mlp.finish()

    def grad_rows(i, _):
        r = pl.ds(i * 16, 16)
        grad = cot[p.x, p.c, r].astype(f32) + norm_back(own[r], resid[r])
        gres[r] = grad
        gb[p.x, p.c, r] = grad.astype(bf16)
        return 0

    lax.fori_loop(0, OWNED // 16, grad_rows, 0)
    g_branch = GroupGather(links, p, gb)
    g_branch.start()
    r_mlp.sent()
    g_branch.ready(0)

    r_out = group_reduce(2, partial_of(act, d, 768))
    r_out.run(launch=False)
    g_branch.forward()
    grads_into(d, cot, act, 768)
    w_d = WeightReduce(links, p, d, in_d, in2_d, fin_d, 384)
    w_gu.start1()
    w_d.start0()
    g_branch.share_near()

    def grad_mixed(t):
        out = jnp.dot(gb[t].reshape(256, 2048), wo[...].reshape(2048, 256), preferred_element_type=f32)
        gg[t, :, :, 512:768] = out.astype(bf16).reshape(2, OWNED, 256)

    def attend_back(block, head):
        lane = pl.multiple_of(head * 128, 128)
        acc[...] = jnp.zeros_like(acc)

        def chunk_body(chunk, _):
            x, core = block * 2 + chunk // 2, chunk % 2
            r = pl.multiple_of(chunk * 128, 128)
            query = gg[x, core, :, pl.ds(lane, 128)]
            grad = gg[x, core, :, pl.ds(lane + 512, 128)]
            keys = kv[block, pl.ds(r, 192), pl.ds(lane, 128)]
            values = kv[block, pl.ds(r, 192), pl.ds(lane + 256, 128)]
            probs = probabilities(query, keys, block, chunk)
            probs_low = probs.astype(bf16)
            grad_probs = lax.dot_general(grad, values, TURNED, preferred_element_type=f32)
            inner = jnp.sum(probs * grad_probs, axis=-1, keepdims=True)
            grad_scores = (probs * (grad_probs - inner)).astype(bf16)
            grad_query = jnp.dot(grad_scores, keys, preferred_element_type=f32) * SCALE
            act[x, core, :, pl.ds(lane, 128)] = grad_query.astype(bf16)
            rows = pl.ds(r, 192)
            grad_keys = lax.dot_general(grad_scores, query, LEFT_TURNED, preferred_element_type=f32)
            acc[0, rows] = acc[0, rows] + grad_keys * SCALE
            acc[1, rows] = acc[1, rows] + lax.dot_general(
                probs_low, grad, LEFT_TURNED, preferred_element_type=f32
            )
            return 0

        lax.fori_loop(0, 4, chunk_body, 0)
        for k in range(2):
            lanes = pl.ds(pl.multiple_of(lane + 256 * k, 128), 128)
            tail_out[block, :, lanes] = acc[k, pl.ds(0, WINDOW)].astype(bf16)
            last_kv[block, :, lanes] = acc[k, pl.ds(BLOCK, WINDOW)]

            def store(i, _):
                x, core = block * 2 + i // 2, i % 2
                out = pl.ds(pl.multiple_of(lane + 256 + 256 * k, 128), 128)
                act[x, core, :, out] = acc[k, pl.ds(WINDOW + i * 128, 128)].astype(bf16)
                return 0

            lax.fori_loop(0, 4, store, 0)

    load_qm.wait()
    g_branch.ready(1)
    g_branch.ready(2)

    def half_block(i, _):
        @pl.when(i == 2)
        def _():
            g_branch.share_far()
            r_out.launch()
            g_branch.ready(3)

        block = jnp.where(i < 2, p.xh, 1 - p.xh)

        @pl.when(i % 2 == 0)
        def _():
            grad_mixed(2 * block)
            grad_mixed(2 * block + 1)

        attend_back(block, i % 2)
        return 0

    lax.fori_loop(0, 4, half_block, 0)
    first = jnp.where(p.z == 0, 1, 0)
    tails = []
    for block in range(2):
        to_y = (p.y + 4 - first) % 4 if block == 0 else p.y
        slot = first if block == 0 else 1 - first
        tails.append(links.send(tail_out.at[block], tail_in.at[slot], p.at(y=to_y, z=(p.z + 3) % 4)))
    r_out.pass_all()
    w_gu.start2()
    grads_into(wo, gb, mixed, 256)
    w_o = WeightReduce(links, p, wo, in_o, in2_o, fin_o, 128)
    w_o.start0()
    w_d.start1()
    for copy in tails:
        copy.wait_recv()
    for block in range(2):
        whole = last_kv[block] + tail_in[block].astype(f32)
        act[2 * block + 1, 1, pl.ds(64, 64), 256:] = whole.astype(bf16)
    r_out.finish()

    def result_rows(i, _):
        r = pl.ds(i * 16, 16)
        res_own[r] = (resid[r] + own[r]).astype(bf16)
        return 0

    lax.fori_loop(0, OWNED // 16, result_rows, 0)
    for device in (sibling, p.at(x=(p.x + 1) % 4), p.at(x=(p.x + 3) % 4)):
        pl.semaphore_signal(ready, inc=1, device_id=device, device_id_type=MESH)
    r_out.sent()
    pl.semaphore_wait(ready, 3)
    r_attn = group_reduce(3, partial_of(act, wq, 768))
    r_attn.run()
    b_out = BlockGather(links, p, res_own, result_o)
    load_xr.wait()
    grads_into(wq, nm, act, 768)
    w_q = WeightReduce(links, p, wq, in_q, in2_q, fin_q, 384)
    w_q.start0()
    w_gu.start3()
    w_d.start2()
    w_o.start1()
    r_attn.finish()

    def input_rows(i, _):
        r = pl.ds(i * 16, 16)
        low_own[r] = (gres[r] + norm_back(own[r], hid_own[r].astype(f32))).astype(bf16)
        return 0

    lax.fori_loop(0, OWNED // 16, input_rows, 0)
    b_in = BlockGather(links, p, low_own, grad_o)
    w_q.start1()
    w_gu.start4()
    w_d.start3()
    w_o.start2()
    b_out.share()
    w_q.start2()
    w_d.start4()
    w_o.start3()
    w_q.start3()
    w_o.start4()
    b_in.share()
    w_q.start4()
    for item in (b_out, b_in, w_gu, w_d, w_q, w_o):
        item.done()
    r_attn.sent()
    links.finish()


def block_call(lengths, pk_q, pk_o, pk_gu, pk_d, hid, cot):
    sds = jax.ShapeDtypeStruct
    group = (4, 2, OWNED)
    vm = pltpu.VMEM
    outs = pl.pallas_call(
        block_kernel,
        out_shape=(
            sds((BLOCK, 2048), bf16),
            sds((BLOCK, 2048), bf16),
            sds((2, 64, 1408), bf16),
            sds((2, 64, 768), bf16),
            sds((2, 64, 768), bf16),
            sds((2, 64, 256), bf16),
            sds(group + (2048,), bf16),
            sds(group + (512,), bf16),
        ),
        in_specs=[pl.BlockSpec(memory_space=pltpu.SMEM)] + [ANY] * 6,
        out_specs=[ANY] * 8,
        scratch_shapes=[
            vm((4, 2, 4, 64, 768), bf16),
            vm((4, 2, 4, 64, 256), bf16),
            vm((4, 2, 4, 64, 1408), bf16),
            vm((4, 2, 4, 64, 768), bf16),
            vm(group + (2048,), bf16),
            vm(group + (2048,), bf16),
            vm(group + (768,), bf16),
            vm(group + (1408,), bf16),
            vm((2, BLOCK + WINDOW, 512), bf16),
            vm((OWNED, 2048), f32),
            vm((OWNED, 2048), bf16),
            vm((OWNED, 2048), f32),
            vm((OWNED, 2048), f32),
            vm((OWNED, 2048), bf16),
            vm((OWNED, 2048), bf16),
            vm(group + (2048,), bf16),
            vm((2, BLOCK + WINDOW, 128), f32),
            vm((2, WINDOW, 512), f32),
            vm((2, WINDOW, 512), bf16),
            vm((2, WINDOW, 512), bf16),
            vm((6, 4, 64, 1408), bf16),
            vm((6, 4, 64, 768), bf16),
            vm((6, 4, 64, 768), bf16),
            vm((6, 4, 64, 256), bf16),
            vm((6, 64, 1408), bf16),
            vm((6, 64, 768), bf16),
            vm((6, 64, 768), bf16),
            vm((6, 64, 256), bf16),
            vm((4, 4, OWNED, 512), bf16),
            vm((4, 6, 64, 512), bf16),
            vm((4, OWNED, 512), f32),
            vm((4, 4, OWNED, 512), bf16),
            vm((4, 6, 64, 512), bf16),
            pltpu.SemaphoreType.DMA((220,)),
            pltpu.SemaphoreType.DMA((220,)),
            pltpu.SemaphoreType.DMA((24,)),
            pltpu.SemaphoreType.DMA((80,)),
            pltpu.SemaphoreType.DMA((80,)),
            pltpu.SemaphoreType.REGULAR,
        ],
        compiler_params=pltpu.CompilerParams(
            collective_id=0, has_side_effects=True, vmem_limit_bytes=60 * 2**20
        ),
        name="block",
    )(lengths, pk_q, pk_o, pk_gu, pk_d, hid.reshape(2, 2, OWNED, 2048), cot.reshape(2, 2, OWNED, 2048))
    return outs[:6]


def pack_ff(gate, up, down):
    def tail(w):
        return jnp.pad(w[:, 640:], ((0, 0), (0, 16)))

    def one(k):
        g, u, d = (w[:, k * 688 : (k + 1) * 688] for w in (gate, up, down))
        return (
            jnp.concatenate([g[:, :640], u[:, :640], tail(g), tail(u)], axis=1),
            jnp.pad(d, ((0, 0), (0, 80))),
        )

    (gu0, d0), (gu1, d1) = one(0), one(1)
    return jnp.stack([gu0, gu1]), jnp.stack([d0, d1])


def pack_attn(query, key, value, out):
    def one(k):
        part = slice(k * 256, (k + 1) * 256)
        return jnp.concatenate([query[:, part], key[:, part], value[:, part]], axis=1), out[:, part]

    (q0, o0), (q1, o1) = one(0), one(1)
    return jnp.stack([q0, q1]), jnp.stack([o0, o1])


def per_device(
    hidden_in,
    norm_gain_attn,
    w_query,
    w_key,
    w_value,
    w_out,
    norm_gain_mlp,
    w_gate,
    w_up,
    w_down,
    lengths,
    cotangent,
):
    gain_attn = norm_gain_attn.astype(f32)[:, None]
    gain_mlp = norm_gain_mlp.astype(f32)[:, None]
    scaled = lambda w, g: (w.astype(f32) * g).astype(bf16)
    pk_q, pk_o = pack_attn(
        scaled(w_query, gain_attn), scaled(w_key, gain_attn), scaled(w_value, gain_attn), w_out.T
    )
    pk_gu, pk_d = pack_ff(scaled(w_gate, gain_mlp), scaled(w_up, gain_mlp), w_down.T)
    result, input_grad, fin_gu, fin_d, fin_q, fin_o = block_call(
        lengths, pk_q, pk_o, pk_gu, pk_d, hidden_in, cotangent
    )

    def joined(fin, *spans):
        return jnp.concatenate([fin[k][:, s] for k in range(2) for s in spans], axis=1).astype(f32)

    dq, dk, dv = (joined(fin_q, slice(256 * i, 256 * i + 256)) for i in range(3))
    dg = joined(fin_gu, slice(0, 640), slice(1280, 1328))
    du = joined(fin_gu, slice(640, 1280), slice(1344, 1392))

    def dots(pairs):
        return sum(jnp.sum(w.astype(f32) * g, axis=1) for w, g in pairs)

    grads_gain = jnp.stack(
        [dots([(w_query, dq), (w_key, dk), (w_value, dv)]), dots([(w_gate, dg), (w_up, du)])]
    )
    grads_gain = grads_gain + flip(grads_gain, "xl")
    grads_gain = grads_gain + flip(grads_gain, "c")
    return (
        result,
        input_grad,
        grads_gain[0],
        dq * gain_attn,
        dk * gain_attn,
        dv * gain_attn,
        joined(fin_o, slice(0, 256)).T,
        grads_gain[1],
        dg * gain_mlp,
        du * gain_mlp,
        joined(fin_d, slice(0, 688)).T,
    )


def solution(mesh):
    mesh = Mesh(mesh.devices.reshape(4, 2, 4, 2, 2), AXES)
    seq, head = ("y", "xh", "z"), ("xl", "c")
    rows, cols, flat, turned = P(seq, None), P(seq, head), P(seq), P(head, seq)
    return jax.shard_map(
        per_device,
        mesh=mesh,
        in_specs=(rows, flat, cols, cols, cols, turned, flat, cols, cols, turned, P(), rows),
        out_specs=(rows, rows, flat, cols, cols, cols, turned, flat, cols, cols, turned),
        check_vma=False,
    )
```

```python
import jax
import jax.numpy as jnp
from jax import lax
from jax.experimental import pallas as pl
from jax.experimental.pallas import tpu as pltpu
from jax.sharding import Mesh, PartitionSpec as P

HEAD_DIM = 128
WINDOW = 64
BLOCK = 512
OWNED = 128
PIECES = 4
WIDE = 2048 // PIECES
AXES = ("y", "xh", "z", "xl", "c")

epsilon = 1e-05
masked_score = -1e30
f32 = jnp.float32
bf16 = jnp.bfloat16


def flip(value, axis):
    return lax.ppermute(value, axis, [(0, 1), (1, 0)])


MESH = pl.DeviceIdType.MESH
SCALE = HEAD_DIM ** (-0.5)
ANY = pl.BlockSpec(memory_space=pl.ANY)
TURNED = (((1,), (1,)), ((), ()))
LEFT_TURNED = (((0,), (0,)), ((), ()))


class Place:
    def __init__(self):
        self.y, self.z, self.c = lax.axis_index("y"), lax.axis_index("z"), lax.axis_index("c")
        self.xh, self.xl = lax.axis_index("xh"), lax.axis_index("xl")
        self.x = self.xh * 2 + self.xl
        self.q = self.xl * 2 + self.c

    def at(self, y=None, x=None, z=None, c=None):
        y = self.y if y is None else y
        x = self.x if x is None else x
        z = self.z if z is None else z
        c = self.c if c is None else c
        return (y, x // 2, z, x % 2, c)


class Links:
    def __init__(self, send_sems, recv_sems, local_sems):
        self.send_sems, self.recv_sems, self.local_sems = send_sems, recv_sems, local_sems
        self.count, self.local_count, self.started = 0, 0, []

    def send(self, src, dst, device):
        copy = self.prepare(src, dst, device)
        copy.start()
        return copy

    def prepare(self, src, dst, device):
        copy = pltpu.make_async_remote_copy(
            src_ref=src,
            dst_ref=dst,
            send_sem=self.send_sems.at[self.count],
            recv_sem=self.recv_sems.at[self.count],
            device_id=device,
            device_id_type=MESH,
        )
        self.count += 1
        self.started.append(copy)
        return copy

    def local(self, src, dst):
        copy = pltpu.make_async_copy(src, dst, self.local_sems.at[self.local_count])
        self.local_count += 1
        copy.start()
        return copy

    def settle(self, copies=None):
        copies = self.started if copies is None else copies
        for copy in copies:
            copy.wait_send()
        self.started = [copy for copy in self.started if not any(copy is other for other in copies)]


class WeightGather:
    def __init__(self, links, place, pack, whole, cut):
        self.links, self.place, self.whole = links, place, whole
        cols = whole.shape[-1]
        self.parts = (pl.ds(0, cut), pl.ds(cut, cols - cut))
        self.swap = links.send(
            pack.at[1 - place.xh], whole.at[place.y, place.xh, place.z], place.at(x=(place.x + 2) % 4)
        )
        self.mine = links.local(pack.at[place.xh], whole.at[place.y, place.xh, place.z])

    def send(self, ref, device):
        return self.links.send(ref, ref, device)

    def near(self, view_z, view_y):
        p = self.place
        first, second = self.parts
        zs = (p.at(z=(p.z + 1) % 4), p.at(z=(p.z + 3) % 4))
        ys = (p.at(y=(p.y + 1) % 4), p.at(y=(p.y + 3) % 4))
        (ref_z, axis_z), (ref_y, axis_y) = view_z, view_y
        to = {"z": zs, "y": ys}
        self.got = [
            self.send(ref_z, to[axis_z][0]),
            self.send(ref_y, to[axis_y][0]),
            self.send(ref_z, to[axis_z][1]),
            self.send(ref_y, to[axis_y][1]),
        ]

    def wait(self):
        for copy in self.got:
            copy.wait_recv()

    def start0(self):
        p, w = self.place, self.whole
        first, second = self.parts
        self.swap.wait_recv()
        self.mine.wait()
        self.near(
            (w.at[p.y, :, p.z, :, first], "z"),
            (w.at[p.y, :, p.z, :, second], "y"),
        )

    def start1(self):
        p, w = self.place, self.whole
        first, second = self.parts
        self.wait()
        zn, zp, yn, yp = (p.z + 1) % 4, (p.z + 3) % 4, (p.y + 1) % 4, (p.y + 3) % 4
        self.got = [
            self.send(w.at[p.y, 0, zp, :, first], p.at(z=zn)),
            self.send(w.at[yp, 0, p.z, :, second], p.at(y=yn)),
            self.send(w.at[p.y, 1, zn, :, first], p.at(z=zp)),
            self.send(w.at[yn, 1, p.z, :, second], p.at(y=yp)),
        ]

    def start2(self):
        p, w = self.place, self.whole
        first, second = self.parts
        self.wait()
        self.near(
            (w.at[:, :, p.z, :, second], "z"),
            (w.at[p.y, :, :, :, first], "y"),
        )

    def start3(self):
        p, w = self.place, self.whole
        first, second = self.parts
        self.wait()
        zn, zp, yn, yp = (p.z + 1) % 4, (p.z + 3) % 4, (p.y + 1) % 4, (p.y + 3) % 4
        self.got = [
            self.send(w.at[yp, 0, :, :, first], p.at(y=yn)),
            self.send(w.at[:, 0, zp, :, second], p.at(z=zn)),
            self.send(w.at[yn, 1, :, :, first], p.at(y=yp)),
            self.send(w.at[:, 1, zn, :, second], p.at(z=zp)),
        ]

    def done(self):
        self.wait()


def greet(place):
    p = place
    barrier = pltpu.get_barrier_semaphore()
    partners = (
        p.at(z=(p.z + 1) % 4),
        p.at(z=(p.z + 3) % 4),
        p.at(y=(p.y + 1) % 4),
        p.at(y=(p.y + 3) % 4),
        p.at(x=(p.x + 1) % 4),
        p.at(x=(p.x + 3) % 4),
        p.at(x=(p.x + 2) % 4),
        p.at(c=1 - p.c),
    )
    for device in partners:
        pl.semaphore_signal(barrier, inc=1, device_id=device, device_id_type=MESH)

    @pl.when(p.z == 3)
    def _():
        pl.semaphore_signal(barrier, inc=1, device_id=p.at(y=(p.y + 1) % 4, z=0 * p.z), device_id_type=MESH)

    @pl.when(p.z == 0)
    def _():
        pl.semaphore_signal(barrier, inc=1, device_id=p.at(y=(p.y + 3) % 4, z=0 * p.z + 3), device_id_type=MESH)

    pl.semaphore_wait(barrier, 8 + jnp.where((p.z == 3) | (p.z == 0), 1, 0))


def unit_scale(values):
    return values * lax.rsqrt(jnp.mean(values * values, axis=-1, keepdims=True) + epsilon)


class WeightReduce:
    def __init__(self, links, place, total, first_in, second_in, out, cut):
        self.links, self.place, self.total, self.out = links, place, total, out
        self.one, self.two = first_in, second_in
        cols = total.shape[-1]
        self.cols = cols
        self.parts = (pl.ds(0, cut), pl.ds(cut, cols - cut))
        p = place
        self.yn, self.yp, self.yf = (p.y + 1) % 4, (p.y + 3) % 4, (p.y + 2) % 4
        self.zn, self.zp, self.zf = (p.z + 1) % 4, (p.z + 3) % 4, (p.z + 2) % 4
        self.next_y, self.prev_y = p.at(y=self.yn), p.at(y=self.yp)
        self.next_z, self.prev_z = p.at(z=self.zn), p.at(z=self.zp)

    def start0(self):
        a, b = self.parts
        t, one, send = self.total, self.one, self.links.send
        self.far = [
            send(t.at[self.yf, 0, :, :, a], one.at[0, :, :, a], self.next_y),
            send(t.at[:, 0, self.zf, :, b], one.at[0, :, :, b], self.next_z),
            send(t.at[self.yf, 1, :, :, a], one.at[2, :, :, a], self.prev_y),
            send(t.at[:, 1, self.zf, :, b], one.at[2, :, :, b], self.prev_z),
        ]
        self.near = [
            send(t.at[self.yn, 1, :, :, a], one.at[1, :, :, a], self.next_y),
            send(t.at[:, 1, self.zn, :, b], one.at[1, :, :, b], self.next_z),
            send(t.at[self.yp, 0, :, :, a], one.at[3, :, :, a], self.prev_y),
            send(t.at[:, 0, self.zp, :, b], one.at[3, :, :, b], self.prev_z),
        ]

    def add(self, target, sources, rows):
        def body(i, _):
            ref = target(i)
            value = ref[...].astype(f32)
            for source in sources:
                value = value + source(i)[...].astype(f32)
            ref[...] = value.astype(bf16)
            return 0

        lax.fori_loop(0, rows, body, 0)

    def start1(self):
        a, b = self.parts
        t, one, send = self.total, self.one, self.links.send
        yn, yp, zn, zp = self.yn, self.yp, self.zn, self.zp
        self.sums = []
        self.far[0].wait_recv()
        self.add(lambda i: t.at[yn, 0, i, :, a], [lambda i: one.at[0, i, :, a]], 4)
        self.sums.append(send(t.at[yn, 0, :, :, a], one.at[4, :, :, a], self.next_y))
        self.far[1].wait_recv()
        self.add(lambda i: t.at[i, 0, zn, :, b], [lambda i: one.at[0, i, :, b]], 4)
        self.sums.append(send(t.at[:, 0, zn, :, b], one.at[4, :, :, b], self.next_z))
        self.far[2].wait_recv()
        self.add(lambda i: t.at[yp, 1, i, :, a], [lambda i: one.at[2, i, :, a]], 4)
        self.sums.append(send(t.at[yp, 1, :, :, a], one.at[5, :, :, a], self.prev_y))
        self.far[3].wait_recv()
        self.add(lambda i: t.at[i, 1, zp, :, b], [lambda i: one.at[2, i, :, b]], 4)
        self.sums.append(send(t.at[:, 1, zp, :, b], one.at[5, :, :, b], self.prev_z))

    def start2(self):
        a, b = self.parts
        t, one, two, send = self.total, self.one, self.two, self.links.send
        p = self.place
        for copy in self.near + self.sums:
            copy.wait_recv()
        self.add(lambda i: t.at[p.y, 0, i, :, a], [lambda i: one.at[3, i, :, a], lambda i: one.at[4, i, :, a]], 4)
        self.add(lambda i: t.at[p.y, 1, i, :, a], [lambda i: one.at[1, i, :, a], lambda i: one.at[5, i, :, a]], 4)
        self.add(lambda i: t.at[i, 0, p.z, :, b], [lambda i: one.at[3, i, :, b], lambda i: one.at[4, i, :, b]], 4)
        self.add(lambda i: t.at[i, 1, p.z, :, b], [lambda i: one.at[1, i, :, b], lambda i: one.at[5, i, :, b]], 4)
        self.far = [
            send(t.at[p.y, 0, self.zf, :, a], two.at[0, :, a], self.next_z),
            send(t.at[self.yf, 0, p.z, :, b], two.at[0, :, b], self.next_y),
            send(t.at[p.y, 1, self.zf, :, a], two.at[2, :, a], self.prev_z),
            send(t.at[self.yf, 1, p.z, :, b], two.at[2, :, b], self.prev_y),
        ]
        self.near = [
            send(t.at[p.y, 1, self.zn, :, a], two.at[1, :, a], self.next_z),
            send(t.at[self.yn, 1, p.z, :, b], two.at[1, :, b], self.next_y),
            send(t.at[p.y, 0, self.zp, :, a], two.at[3, :, a], self.prev_z),
            send(t.at[self.yp, 0, p.z, :, b], two.at[3, :, b], self.prev_y),
        ]

    def plus(self, target, *sources):
        value = target[...].astype(f32)
        for source in sources:
            value = value + source[...].astype(f32)
        target[...] = value.astype(bf16)

    def start3(self):
        a, b = self.parts
        t, two, send = self.total, self.two, self.links.send
        p = self.place
        yn, yp, zn, zp = self.yn, self.yp, self.zn, self.zp
        self.sums = []
        for k, ref, lanes, slot, other, device in (
            (0, t.at[p.y, 0, zn, :, a], a, 0, 4, self.next_z),
            (1, t.at[yn, 0, p.z, :, b], b, 0, 4, self.next_y),
            (2, t.at[p.y, 1, zp, :, a], a, 2, 5, self.prev_z),
            (3, t.at[yp, 1, p.z, :, b], b, 2, 5, self.prev_y),
        ):
            self.far[k].wait_recv()
            self.plus(ref, two.at[slot, :, lanes])
            self.sums.append(send(ref, two.at[other, :, lanes], device))

    def start4(self):
        t, two, out = self.total, self.two, self.out
        p = self.place
        for copy in self.near + self.sums:
            copy.wait_recv()
        self.plus(t.at[p.y, 0, p.z], two.at[3], two.at[4])
        self.plus(t.at[p.y, 1, p.z], two.at[1], two.at[5])
        self.swap = self.links.send(t.at[p.y, 1 - p.xh, p.z], out.at[p.xh], p.at(x=(p.x + 2) % 4))
        self.mine = self.links.local(t.at[p.y, p.xh, p.z], out.at[p.xh])

    def done(self):
        self.swap.wait_recv()
        self.mine.wait()


class GroupReduce:
    def __init__(self, place, partial, bufs, sems):
        self.place, self.partial = place, partial
        self.send_c, self.recv_c, self.tmp, self.snd, self.rcv, self.own = bufs
        self.send_sems, self.recv_sems = sems

    def copy(self, src, dst, index, device):
        return pltpu.make_async_remote_copy(
            src_ref=src,
            dst_ref=dst,
            send_sem=self.send_sems.at[index],
            recv_sem=self.recv_sems.at[index],
            device_id=device,
            device_id_type=MESH,
        )

    def crossing(self, n):
        return self.copy(self.send_c.at[n % 2], self.recv_c.at[n], n, self.place.at(c=1 - self.place.c))

    def to_next(self, n):
        pair = pl.ds(0, 2)
        return self.copy(
            self.snd.at[n, pair], self.rcv.at[n, pair], PIECES + n, self.place.at(x=(self.place.x + 1) % 4)
        )

    def to_prev(self, n):
        pair = pl.ds(2, 2)
        return self.copy(
            self.snd.at[n, pair], self.rcv.at[n, pair], 2 * PIECES + n, self.place.at(x=(self.place.x + 3) % 4)
        )

    def sum_next(self, n):
        return self.copy(
            self.snd.at[n, 4], self.rcv.at[n, 4], 3 * PIECES + n, self.place.at(x=(self.place.x + 1) % 4)
        )

    def sum_prev(self, n):
        return self.copy(
            self.snd.at[n, 5], self.rcv.at[n, 5], 4 * PIECES + n, self.place.at(x=(self.place.x + 3) % 4)
        )

    def sibling_part(self, n):
        part = self.partial(n, 1 - self.place.c)

        @pl.when(n >= 2)
        def _():
            self.crossing(n - 2).wait_send()

        self.send_c[n % 2] = part.astype(bf16).reshape(4, OWNED, WIDE)
        self.crossing(n).start()

    def own_part(self, n, launch):
        p, tmp, snd = self.place, self.tmp, self.snd
        part = self.partial(n, p.c).reshape(4, OWNED, WIDE)
        self.crossing(n).wait_recv()
        tmp[...] = part + self.recv_c[n].astype(f32)
        far, nxt, prev = (p.x + 2) % 4, (p.x + 1) % 4, (p.x + 3) % 4
        low, high = pl.ds(0, 64), pl.ds(64, 64)
        snd[n, 0] = tmp[far, low].astype(bf16)
        snd[n, 1] = tmp[nxt, high].astype(bf16)
        if launch:
            self.to_next(n).start()
        snd[n, 2] = tmp[far, high].astype(bf16)
        snd[n, 3] = tmp[prev, low].astype(bf16)
        if launch:
            self.to_prev(n).start()
        snd[n, 4] = tmp[nxt, low].astype(bf16)
        snd[n, 5] = tmp[prev, high].astype(bf16)
        self.own[:, pl.ds(pl.multiple_of(n * WIDE, WIDE), WIDE)] = tmp[p.x]

    def pass_on(self, n):
        snd, rcv = self.snd, self.rcv
        self.to_next(n).wait_recv()
        snd[n, 4] = (snd[n, 4].astype(f32) + rcv[n, 0].astype(f32)).astype(bf16)
        self.sum_next(n).start()
        self.to_prev(n).wait_recv()
        snd[n, 5] = (snd[n, 5].astype(f32) + rcv[n, 2].astype(f32)).astype(bf16)
        self.sum_prev(n).start()

    def run(self, launch=True, pass_on=True, hooks=()):
        def body(i, _):
            @pl.when(i < PIECES)
            def _():
                self.sibling_part(i)

            @pl.when((i >= 1) & (i < PIECES + 1))
            def _():
                self.own_part(i - 1, launch)

            if pass_on:

                @pl.when(i >= 2)
                def _():
                    self.pass_on(i - 2)

            for step, hook in hooks:
                pl.when(i == step)(hook)
            return 0

        lax.fori_loop(0, PIECES + 2 if pass_on else PIECES + 1, body, 0)

    def launch(self):
        def body(n, _):
            self.to_next(n).start()
            self.to_prev(n).start()
            return 0

        lax.fori_loop(0, PIECES, body, 0)

    def pass_range(self, start, stop):
        def body(n, _):
            self.pass_on(n)
            return 0

        lax.fori_loop(start, stop, body, 0)

    def finish(self):
        def body(n, _):
            lanes = pl.ds(pl.multiple_of(n * WIDE, WIDE), WIDE)
            low, high = pl.ds(0, 64), pl.ds(64, 64)
            rcv, own = self.rcv, self.own
            self.sum_next(n).wait_recv()
            own[low, lanes] = own[low, lanes] + rcv[n, 3].astype(f32) + rcv[n, 4].astype(f32)
            self.sum_prev(n).wait_recv()
            own[high, lanes] = own[high, lanes] + rcv[n, 1].astype(f32) + rcv[n, 5].astype(f32)
            return 0

        lax.fori_loop(0, PIECES, body, 0)

    def sent(self):
        def body(n, _):
            for copy in (self.to_next, self.to_prev, self.sum_next, self.sum_prev):
                copy(n).wait_send()
            return 0

        self.crossing(PIECES - 2).wait_send()
        self.crossing(PIECES - 1).wait_send()

        lax.fori_loop(0, PIECES, body, 0)


class GroupGather:
    def __init__(self, links, place, whole):
        self.links, self.place, self.whole = links, place, whole
        self.low, self.high = pl.ds(0, 64), pl.ds(64, 64)

    def send(self, ref, device):
        return self.links.send(ref, ref, device)

    def start(self):
        p, w = self.place, self.whole
        self.nxt, self.prev, self.far = (p.x + 1) % 4, (p.x + 3) % 4, (p.x + 2) % 4
        self.to_next, self.to_prev = p.at(x=self.nxt), p.at(x=self.prev)
        self.sibling = p.at(c=1 - p.c)
        low, high = w.at[p.x, p.c, self.low], w.at[p.x, p.c, self.high]
        self.first = [self.send(low, self.to_next), self.send(high, self.to_prev)]
        self.second = [self.send(high, self.to_next), self.send(low, self.to_prev)]
        tiles = (p.x, self.prev, self.nxt, self.far)
        self.paired = [self.later(w.at[x, p.c], self.sibling) for x in tiles]
        self.paired[0].start()
        self.third = [
            self.later(w.at[self.prev, p.c, self.low], self.to_next),
            self.later(w.at[self.nxt, p.c, self.high], self.to_prev),
        ]

    def later(self, ref, device):
        return self.links.prepare(ref, ref, device)

    def forward(self):
        for k in range(2):
            self.first[k].wait_recv()
            self.third[k].start()

    def share_near(self):
        for k in range(2):
            self.second[k].wait_recv()
            self.paired[1 + k].start()

    def share_far(self):
        for copy in self.third:
            copy.wait_recv()
        self.paired[3].start()

    def sent(self):
        self.links.settle(self.first + self.second + self.third + self.paired)

    def ready(self, k):
        self.paired[k].wait_recv()


class BlockExchange:
    def __init__(self, links, place, block, whole):
        p = place
        self.place, self.links = p, links
        beside = p.at(x=2 * p.xh + 1 - p.xl)
        sibling = p.at(c=1 - p.c)
        self.near, self.next = 3 - p.x, 2 * (1 - p.xh) + p.xl
        halves = [pl.ds(0, 64), pl.ds(64, 64)]
        self.cross = [links.send(block.at[p.xl, p.c, h], whole.at[p.x, p.c, h], p.at(x=3 - p.x)) for h in halves]
        self.across = [
            links.prepare(whole.at[self.near, p.c, h], whole.at[self.near, p.c, h], beside) for h in halves
        ]
        self.paired = [
            links.prepare(whole.at[x, p.c], whole.at[x, p.c], sibling) for x in (self.near, self.next)
        ]

    def forward(self, k):
        self.cross[k].wait_recv()
        self.across[k].start()

    def share(self):
        self.paired[0].start()

    def share_next(self):
        for copy in self.across:
            copy.wait_recv()
        self.paired[1].start()

    def done(self, k):
        self.paired[k].wait_recv()


class BlockReduce(GroupReduce):
    def __init__(self, place, partial, bufs, sems, extra=None):
        self.place, self.partial, self.extra = place, partial, extra
        self.send_c, self.recv_c, self.tmp, self.moving = bufs
        self.send_sems, self.recv_sems = sems
        self.facing, self.beside = place.at(x=3 - place.x), place.at(x=2 * place.xh + 1 - place.xl)

    def part(self, which, n):
        lanes = pl.ds(pl.multiple_of(n * WIDE, WIDE), WIDE)
        return self.moving.at[pl.ds(2 * (which // 2), 2), which % 2, :, lanes]

    def over(self, n):
        return self.copy(self.part(0, n), self.part(1, n), PIECES + n, self.facing)

    def across(self, n):
        return self.copy(self.part(2, n), self.part(3, n), 2 * PIECES + n, self.beside)

    def own_part(self, n, launch):
        p, tmp = self.place, self.tmp
        part = self.partial(n, p.c).reshape(4, OWNED, WIDE)
        self.crossing(n).wait_recv()
        tmp[...] = part + self.recv_c[n].astype(f32)
        if self.extra is not None:
            lanes = pl.ds(pl.multiple_of(n * WIDE, WIDE), WIDE)
            tmp[p.x] += self.extra[:, lanes]
        self.part(0, n)[...] = tmp[pl.ds(2 * (1 - p.xh), 2)].astype(bf16)
        if launch:
            self.over(n).start()
        self.part(2, n)[...] = tmp[pl.ds(2 * p.xh, 2)].astype(bf16)

    def pass_on(self, n):
        self.over(n).wait_recv()
        mine = self.part(2, n)
        mine[...] = (mine[...].astype(f32) + self.part(1, n)[...].astype(f32)).astype(bf16)
        self.across(n).start()

    def launch(self):
        def body(n, _):
            self.over(n).start()
            return 0

        lax.fori_loop(0, PIECES, body, 0)

    def finish(self):
        def body(n, _):
            self.across(n).wait_recv()
            return 0

        lax.fori_loop(0, PIECES, body, 0)

    def total(self, tile, rows):
        return self.moving[2 + tile, 0, rows].astype(f32) + self.moving[2 + tile, 1, rows].astype(f32)

    def crossed(self):
        self.crossing(PIECES - 2).wait_send()
        self.crossing(PIECES - 1).wait_send()

    def sent(self):
        def body(n, _):
            self.over(n).wait_send()
            self.across(n).wait_send()
            return 0

        lax.fori_loop(0, PIECES, body, 0)


class BlockOut:
    def __init__(self, links, place, rows, out):
        mine = out.at[:, place.c]
        self.local = links.local(rows, mine)
        self.paired = links.send(rows, mine, place.at(c=1 - place.c))

    def done(self):
        self.paired.wait_recv()
        self.local.wait()


def norm_back(e, values):
    r = lax.rsqrt(jnp.mean(values * values, axis=-1, keepdims=True) + epsilon)
    return r * e - values * r**3 * jnp.mean(e * values, axis=-1, keepdims=True)


def block_kernel(
    lengths, pk_q, pk_o, pk_gu, pk_d, hid, cot_in,
    result_o, grad_o, fin_gu, fin_d, fin_q, fin_o, xr_o, qm_o,
    wq, wo, gu, d, nm, cot, act, gg, kv, resid, hid_pair, own, gb,
    acc, last_kv, tail_out, tail_in, in_gu, in_d, in_q, in_o, in2_gu, in2_d, in2_q, in2_o,
    send_c, snd, tmp, recv_c, rcv,
    send_sems, recv_sems, local_sems, group_send, group_recv, ready,
):
    p = Place()
    links = Links(send_sems, recv_sems, local_sems)
    sibling = p.at(c=1 - p.c)
    facing, beside = p.at(x=3 - p.x), p.at(x=2 * p.xh + 1 - p.xl)

    def signal(semaphore, devices):
        for device in devices:
            pl.semaphore_signal(semaphore, inc=1, device_id=device, device_id_type=MESH)

    hidg, xr = gb, nm

    own_pair = pl.ds(2 * p.xh, 2)
    own_hidden = links.local(hid, hidg.at[own_pair])
    load_hid = links.local(hid.at[:, p.c], hid_pair)
    own_cot = links.local(cot_in, cot.at[own_pair])
    greet(p)
    g_q = WeightGather(links, p, pk_q, wq, 384)
    g_o = WeightGather(links, p, pk_o, wo, 128)
    e_hid = BlockExchange(links, p, hid, hidg)
    g_q.start0()
    g_o.start0()
    def norm_rows(tile, core):
        def body(i, _):
            r = pl.ds(i * 32, 32)
            xr[tile, core, r] = unit_scale(hidg[tile, core, r].astype(f32)).astype(bf16)
            return 0

        lax.fori_loop(0, 4, body, 0)

    def norm_own(i, _):
        norm_rows(2 * p.xh + i // 2, i % 2)
        return 0

    own_hidden.wait()
    lax.fori_loop(0, 4, norm_own, 0)
    g_q.start1()
    g_o.start1()
    e_hid.forward(0)
    g_q.start2()
    g_gu = WeightGather(links, p, pk_gu, gu, 768)
    g_d = WeightGather(links, p, pk_d, d, 384)
    e_hid.forward(1)
    e_hid.share()
    e_cot = BlockExchange(links, p, cot_in, cot)
    norm_rows(e_hid.near, p.c)
    g_q.start3()
    g_o.start2()
    g_gu.start0()
    g_d.start0()
    e_hid.done(0)
    norm_rows(e_hid.near, 1 - p.c)
    g_q.done()

    def project(t):
        w = wq[...].reshape(2048, 768)
        out = jnp.dot(xr[t].reshape(256, 2048), w, preferred_element_type=f32).astype(bf16)
        gg[t, :, :, 0:256] = out[:, :256].reshape(2, OWNED, 256)
        kv[t // 2, pl.ds((t % 2) * 256 + WINDOW, 256)] = out[:, 256:]

    def project_three(i, _):
        project(jnp.where(i < 2, 2 * p.xh + i, e_hid.near))
        return 0

    lax.fori_loop(0, 3, project_three, 0)
    g_o.start3()
    e_hid.share_next()
    norm_rows(e_hid.next, p.c)
    g_gu.start1()
    g_d.start1()
    e_cot.forward(0)
    e_hid.done(1)
    norm_rows(e_hid.next, 1 - p.c)
    xr_spill = links.local(xr, xr_o)
    project(e_hid.next)

    tails = []
    last = jnp.where(p.z == 3, 1, 0)
    for block in range(2):
        to_y = p.y if block == 0 else (p.y + last) % 4
        slot = last if block == 0 else 1 - last
        tails.append(
            links.send(
                kv.at[block, pl.ds(BLOCK, WINDOW)],
                kv.at[slot, pl.ds(0, WINDOW)],
                p.at(y=to_y, z=(p.z + 1) % 4),
            )
        )
    end0 = lengths[0]
    end1 = end0 + lengths[1]

    def masked(scores, block, chunk):
        start = (p.y * 8 + block * 4 + p.z) * BLOCK + chunk * 128
        query = start + lax.broadcasted_iota(jnp.int32, (128, 192), 0)
        key = start - WINDOW + lax.broadcasted_iota(jnp.int32, (128, 192), 1)
        seen = (key <= query) & (key > query - WINDOW) & (key >= 0)
        for end in (end0, end1):
            seen = seen & ((key >= end) | (query < end))
        return jnp.where(seen, scores, masked_score)

    def probabilities(query, keys, block, chunk):
        scores = lax.dot_general(query, keys, TURNED, preferred_element_type=f32) * SCALE
        scores = masked(scores, block, chunk)
        expo = jnp.exp(scores - jnp.max(scores, axis=-1, keepdims=True))
        return expo / jnp.sum(expo, axis=-1, keepdims=True)

    def attend(block, chunk):
        x, core = block * 2 + chunk // 2, chunk % 2
        r = pl.multiple_of(chunk * 128, 128)
        for head in range(2):
            lane = head * 128
            query = gg[x, core, :, lane : lane + 128]
            keys = kv[block, pl.ds(r, 192), lane : lane + 128]
            values = kv[block, pl.ds(r, 192), lane + 256 : lane + 384]
            probs = probabilities(query, keys, block, chunk).astype(bf16)
            out = jnp.dot(probs, values, preferred_element_type=f32)
            gg[x, core, :, lane + 256 : lane + 384] = out.astype(bf16)

    def inner(i, _):
        attend(i // 3, i % 3 + 1)
        return 0

    e_cot.forward(1)
    e_cot.share()
    g_gu.start2()
    g_d.start2()
    lax.fori_loop(0, 6, inner, 0)
    e_cot.share_next()
    for copy in tails:
        copy.wait_recv()

    def first_chunk(i, _):
        attend(i, 0)
        return 0

    lax.fori_loop(0, 2, first_chunk, 0)
    mixed = gg.at[:, :, :, pl.ds(256, 256)]
    g_o.done()
    xr_spill.wait()

    def partial_of(left, right, width, start=0):
        def partial(n, core):
            return lax.dot_general(
                left[:, core, :, start : start + width].reshape(512, width),
                right[n].reshape(WIDE, width),
                TURNED,
                preferred_element_type=f32,
            )

        return partial

    def group_reduce(k, partial):
        span = pl.ds(5 * PIECES * k, 5 * PIECES)
        return GroupReduce(
            p, partial, (send_c, recv_c, tmp, snd, rcv, own), (group_send.at[span], group_recv.at[span])
        )

    r_branch = group_reduce(0, partial_of(gg, wo, 256, 256))
    r_branch.run(pass_on=False)
    r_branch.pass_range(0, PIECES)
    g_gu.start3()
    g_d.start3()
    load_hid.wait()
    r_branch.finish()

    def resid_rows(i, _):
        r = pl.ds(i * 16, 16)
        total = hid_pair[p.xl, r].astype(f32) + own[r]
        resid[r] = total
        nm[p.x, p.c, r] = unit_scale(total).astype(bf16)
        return 0

    lax.fori_loop(0, OWNED // 16, resid_rows, 0)
    g_nm = GroupGather(links, p, nm)
    g_nm.start()
    q_spill = links.local(gg.at[:, :, :, pl.ds(0, 512)], qm_o)
    g_gu.done()
    own_cot.wait()
    for k in range(2):
        e_cot.done(k)
    q_spill.wait()
    g_d.done()
    g_nm.ready(0)

    def feed(k, _):
        @pl.when(k == 1)
        def _():
            g_nm.forward()
            g_nm.share_near()
            g_nm.ready(1)

        @pl.when(k == 2)
        def _():
            g_nm.ready(2)

        @pl.when(k == 3)
        def _():
            g_nm.share_far()
            g_nm.ready(3)

        t = (p.x + jnp.where(k == 0, 0, jnp.where(k == 1, 3, k - 1))) % 4
        part = jnp.dot(nm[t].reshape(256, 2048), gu[...].reshape(2048, 1408), preferred_element_type=f32)
        back = jnp.dot(cot[t].reshape(256, 2048), d[...].reshape(2048, 768), preferred_element_type=f32)
        tail = part[:, 1280:]
        flipped = pltpu.roll(tail, 64, 1)
        lane = lax.broadcasted_iota(jnp.int32, (256, 128), 1)
        for lanes, gate, up in (
            (slice(0, 640), part[:, :640], part[:, 640:1280]),
            (slice(640, 768), tail, flipped),
        ):
            sig = 1 / (1 + jnp.exp(-gate))
            silu = gate * sig
            grad_act = back[:, lanes]
            act[t, :, :, lanes] = (silu * up).astype(bf16).reshape(2, OWNED, -1)
            grad_gate = grad_act * up * sig * (1 + gate * (1 - sig))
            grad_up = grad_act * silu
            if lanes.start == 0:
                gg[t, :, :, :640] = grad_gate.astype(bf16).reshape(2, OWNED, 640)
                gg[t, :, :, 640:1280] = grad_up.astype(bf16).reshape(2, OWNED, 640)
            else:
                both = jnp.where(lane < 64, grad_gate, pltpu.roll(grad_up, 64, 1))
                gg[t, :, :, 1280:] = both.astype(bf16).reshape(2, OWNED, 128)
        return 0

    lax.fori_loop(0, 4, feed, 0)

    r_branch.sent()
    links.settle()
    r_mlp = group_reduce(1, partial_of(gg, gu, 1408))
    r_mlp.run(pass_on=False)

    def grads_into(out, left, right, width, reduce=None):
        def body(n, _):
            lanes = pl.ds(pl.multiple_of(n * 256, 256), 256)
            part = lax.dot_general(
                left[:, :, :, lanes].reshape(1024, 256),
                right[...].reshape(1024, width),
                LEFT_TURNED,
                preferred_element_type=f32,
            )
            out[n // 2, n % 2] = part.astype(bf16).reshape(4, 64, width)
            if reduce is not None:

                @pl.when(n % 2 == 0)
                def _():
                    reduce.pass_on(n // 2)

            return 0

        lax.fori_loop(0, 8, body, 0)

    grads_into(gu, nm, gg, 1408, r_mlp)
    w_gu = WeightReduce(links, p, gu, in_gu, in2_gu, fin_gu, 768)
    w_gu.start0()
    signal(ready.at[0], (facing, beside))
    load_qm = links.local(qm_o, gg.at[:, :, :, pl.ds(0, 512)])
    r_mlp.finish()

    def grad_rows(i, _):
        r = pl.ds(i * 16, 16)
        grad = cot[p.x, p.c, r].astype(f32) + norm_back(own[r], resid[r])
        gb[p.x, p.c, r] = grad.astype(bf16)
        return 0

    lax.fori_loop(0, OWNED // 16, grad_rows, 0)
    g_branch = GroupGather(links, p, gb)
    g_branch.start()
    r_mlp.sent()
    g_branch.ready(0)

    def block_reduce(k, partial, moving, extra=None):
        span = pl.ds(5 * PIECES * k, 5 * PIECES)
        sems = (group_send.at[span], group_recv.at[span])
        return BlockReduce(p, partial, (send_c, recv_c, tmp, moving), sems, extra)

    r_out = block_reduce(2, partial_of(act, d, 768), nm, resid)
    r_out.run(launch=False, pass_on=False)
    g_branch.forward()
    w_gu.start1()
    grads_into(d, cot, act, 768)
    signal(ready.at[1], (facing, beside, sibling))
    w_d = WeightReduce(links, p, d, in_d, in2_d, fin_d, 384)
    w_d.start0()
    g_branch.share_near()

    def grad_mixed(t):
        out = jnp.dot(gb[t].reshape(256, 2048), wo[...].reshape(2048, 256), preferred_element_type=f32)
        gg[t, :, :, 512:768] = out.astype(bf16).reshape(2, OWNED, 256)

    first = jnp.where(p.z == 0, 1, 0)
    tails = []

    def attend_back(block):
        acc[...] = jnp.zeros_like(acc)

        def chunk_body(chunk, _):
            x, core = block * 2 + chunk // 2, chunk % 2
            r = pl.multiple_of(chunk * 128, 128)
            rows = pl.ds(r, 192)
            for head in range(2):
                lane = head * 128
                query = gg[x, core, :, lane : lane + 128]
                grad = gg[x, core, :, lane + 512 : lane + 640]
                keys = kv[block, rows, lane : lane + 128]
                values = kv[block, rows, lane + 256 : lane + 384]
                probs = probabilities(query, keys, block, chunk)
                probs_low = probs.astype(bf16)
                grad_probs = lax.dot_general(grad, values, TURNED, preferred_element_type=f32)
                inner = jnp.sum(probs * grad_probs, axis=-1, keepdims=True)
                grad_scores = (probs * (grad_probs - inner)).astype(bf16)
                grad_query = jnp.dot(grad_scores, keys, preferred_element_type=f32) * SCALE
                act[x, core, :, lane : lane + 128] = grad_query.astype(bf16)
                grad_keys = lax.dot_general(grad_scores, query, LEFT_TURNED, preferred_element_type=f32)
                grad_values = lax.dot_general(probs_low, grad, LEFT_TURNED, preferred_element_type=f32)
                acc[rows, lane : lane + 128] += grad_keys * SCALE
                acc[rows, lane + 256 : lane + 384] += grad_values
            return 0

        chunk_body(0, 0)
        tail_out[block] = acc[0:WINDOW].astype(bf16)
        to_y = jnp.where(block == 0, (p.y + 4 - first) % 4, p.y)
        slot = jnp.where(block == 0, first, 1 - first)
        tails.append(links.send(tail_out.at[block], tail_in.at[slot], p.at(y=to_y, z=(p.z + 3) % 4)))
        lax.fori_loop(1, 4, chunk_body, 0)
        last_kv[block] = acc[BLOCK:]

        def store(i, _):
            r = pl.ds(pl.multiple_of(WINDOW + i * 128, 64), 128)
            act[block * 2 + i // 2, i % 2, :, 256:] = acc[r].astype(bf16)
            return 0

        lax.fori_loop(0, 4, store, 0)

    pl.semaphore_wait(ready.at[0], 2)
    r_out.launch()
    load_qm.wait()
    g_branch.ready(1)
    g_branch.ready(2)

    grad_mixed(2 * p.xh)
    grad_mixed(2 * p.xh + 1)

    attend_back(p.xh)
    g_branch.share_far()
    r_out.pass_range(0, 1)
    w_gu.start2()
    g_branch.ready(3)
    grad_mixed(2 * (1 - p.xh))
    grad_mixed(2 * (1 - p.xh) + 1)
    attend_back(1 - p.xh)
    r_out.pass_range(1, 2)
    w_gu.start3()
    grads_into(wo, gb, mixed, 256)
    own[...] = gb[2 * p.xh, p.c].astype(f32)
    resid[...] = gb[2 * p.xh + 1, p.c].astype(f32)
    g_branch.sent()
    load_xr = links.local(xr_o, gb)
    for copy in tails:
        copy.wait_recv()
    for block in range(2):
        whole = last_kv[block] + tail_in[block].astype(f32)
        act[2 * block + 1, 1, pl.ds(64, 64), 256:] = whole.astype(bf16)
    w_d.start1()
    w_o = WeightReduce(links, p, wo, in_o, in2_o, fin_o, 128)
    w_o.start0()
    w_gu.start4()
    r_out.pass_range(2, 3)
    r_out.crossed()
    pl.semaphore_wait(ready.at[1], 3)
    r_attn = block_reduce(3, partial_of(act, wq, 768), cot)
    r_attn.run(pass_on=False)
    r_out.pass_range(3, 4)
    w_d.start2()
    w_o.start1()
    load_xr.wait()
    grads_into(wq, gb, act, 768)
    w_d.start3()
    w_q = WeightReduce(links, p, wq, in_q, in2_q, fin_q, 384)
    w_q.start0()
    r_attn.pass_range(0, 1)
    w_o.start2()
    r_out.finish()
    r_out.sent()

    def result_rows(i, _):
        tile, r = i // 8, pl.ds((i % 8) * 16, 16)
        nm[2 + tile, 0, r] = r_out.total(tile, r).astype(bf16)
        return 0

    lax.fori_loop(0, 16, result_rows, 0)
    b_out = BlockOut(links, p, nm.at[pl.ds(2, 2), 0], result_o)
    w_d.start4()
    r_attn.pass_range(1, 2)
    w_q.start1()
    w_o.start3()
    r_attn.pass_range(2, 3)
    w_q.start2()
    w_o.start4()
    r_attn.pass_range(3, 4)
    w_q.start3()
    w_q.start4()
    r_attn.finish()

    def input_rows(i, _):
        tile, r = i // 8, pl.ds((i % 8) * 16, 16)
        values = hid_pair[tile, r].astype(f32)
        base = jnp.where(tile == 0, own[r], resid[r])
        hid_pair[tile, r] = (base + norm_back(r_attn.total(tile, r), values)).astype(bf16)
        return 0

    lax.fori_loop(0, 16, input_rows, 0)
    b_in = BlockOut(links, p, hid_pair, grad_o)
    for item in (b_out, b_in, w_gu, w_d, w_q, w_o):
        item.done()
    r_attn.crossed()
    r_attn.sent()
    links.settle()


def block_call(lengths, pk_q, pk_o, pk_gu, pk_d, hid, cot):
    sds = jax.ShapeDtypeStruct
    group = (4, 2, OWNED)
    vm = pltpu.VMEM
    outs = pl.pallas_call(
        block_kernel,
        out_shape=(
            sds((2, 2, OWNED, 2048), bf16),
            sds((2, 2, OWNED, 2048), bf16),
            sds((2, 64, 1408), bf16),
            sds((2, 64, 768), bf16),
            sds((2, 64, 768), bf16),
            sds((2, 64, 256), bf16),
            sds(group + (2048,), bf16),
            sds(group + (512,), bf16),
        ),
        in_specs=[pl.BlockSpec(memory_space=pltpu.SMEM)] + [ANY] * 6,
        out_specs=[ANY] * 8,
        scratch_shapes=[
            vm((4, 2, 4, 64, 768), bf16),
            vm((4, 2, 4, 64, 256), bf16),
            vm((4, 2, 4, 64, 1408), bf16),
            vm((4, 2, 4, 64, 768), bf16),
            vm(group + (2048,), bf16),
            vm(group + (2048,), bf16),
            vm(group + (768,), bf16),
            vm(group + (1408,), bf16),
            vm((2, BLOCK + WINDOW, 512), bf16),
            vm((OWNED, 2048), f32),
            vm((2, OWNED, 2048), bf16),
            vm((OWNED, 2048), f32),
            vm(group + (2048,), bf16),
            vm((BLOCK + WINDOW, 512), f32),
            vm((2, WINDOW, 512), f32),
            vm((2, WINDOW, 512), bf16),
            vm((2, WINDOW, 512), bf16),
            vm((6, 4, 64, 1408), bf16),
            vm((6, 4, 64, 768), bf16),
            vm((6, 4, 64, 768), bf16),
            vm((6, 4, 64, 256), bf16),
            vm((6, 64, 1408), bf16),
            vm((6, 64, 768), bf16),
            vm((6, 64, 768), bf16),
            vm((6, 64, 256), bf16),
            vm((2, 4, OWNED, WIDE), bf16),
            vm((PIECES, 6, 64, WIDE), bf16),
            vm((4, OWNED, WIDE), f32),
            vm((PIECES, 4, OWNED, WIDE), bf16),
            vm((PIECES, 6, 64, WIDE), bf16),
            pltpu.SemaphoreType.DMA((220,)),
            pltpu.SemaphoreType.DMA((220,)),
            pltpu.SemaphoreType.DMA((24,)),
            pltpu.SemaphoreType.DMA((20 * PIECES,)),
            pltpu.SemaphoreType.DMA((20 * PIECES,)),
            pltpu.SemaphoreType.REGULAR((2,)),
        ],
        compiler_params=pltpu.CompilerParams(
            collective_id=0, has_side_effects=True, vmem_limit_bytes=60 * 2**20
        ),
        name="block",
    )(lengths, pk_q, pk_o, pk_gu, pk_d, hid.reshape(2, 2, OWNED, 2048), cot.reshape(2, 2, OWNED, 2048))
    return tuple(out.reshape(BLOCK, 2048) for out in outs[:2]) + tuple(outs[2:6])


def pack_ff(gate, up, down):
    def tail(w):
        return jnp.pad(w[:, 640:], ((0, 0), (0, 16)))

    def one(k):
        g, u, d = (w[:, k * 688 : (k + 1) * 688] for w in (gate, up, down))
        return (
            jnp.concatenate([g[:, :640], u[:, :640], tail(g), tail(u)], axis=1),
            jnp.pad(d, ((0, 0), (0, 80))),
        )

    (gu0, d0), (gu1, d1) = one(0), one(1)
    return jnp.stack([gu0, gu1]), jnp.stack([d0, d1])


def pack_attn(query, key, value, out):
    def one(k):
        part = slice(k * 256, (k + 1) * 256)
        return jnp.concatenate([query[:, part], key[:, part], value[:, part]], axis=1), out[:, part]

    (q0, o0), (q1, o1) = one(0), one(1)
    return jnp.stack([q0, q1]), jnp.stack([o0, o1])


def per_device(
    hidden_in,
    norm_gain_attn,
    w_query,
    w_key,
    w_value,
    w_out,
    norm_gain_mlp,
    w_gate,
    w_up,
    w_down,
    lengths,
    cotangent,
):
    gain_attn = norm_gain_attn.astype(f32)[:, None]
    gain_mlp = norm_gain_mlp.astype(f32)[:, None]
    scaled = lambda w, g: (w.astype(f32) * g).astype(bf16)
    pk_q, pk_o = pack_attn(
        scaled(w_query, gain_attn), scaled(w_key, gain_attn), scaled(w_value, gain_attn), w_out.T
    )
    pk_gu, pk_d = pack_ff(scaled(w_gate, gain_mlp), scaled(w_up, gain_mlp), w_down.T)
    result, input_grad, fin_gu, fin_d, fin_q, fin_o = block_call(
        lengths, pk_q, pk_o, pk_gu, pk_d, hidden_in, cotangent
    )

    def joined(fin, *spans):
        return jnp.concatenate([fin[k][:, s] for k in range(2) for s in spans], axis=1).astype(f32)

    dq, dk, dv = (joined(fin_q, slice(256 * i, 256 * i + 256)) for i in range(3))
    dg = joined(fin_gu, slice(0, 640), slice(1280, 1328))
    du = joined(fin_gu, slice(640, 1280), slice(1344, 1392))

    def dots(pairs):
        return sum(jnp.sum(w.astype(f32) * g, axis=1) for w, g in pairs)

    grads_gain = jnp.stack(
        [dots([(w_query, dq), (w_key, dk), (w_value, dv)]), dots([(w_gate, dg), (w_up, du)])]
    )
    grads_gain = grads_gain + flip(grads_gain, "xl")
    grads_gain = grads_gain + flip(grads_gain, "c")
    return (
        result,
        input_grad,
        grads_gain[0],
        dq * gain_attn,
        dk * gain_attn,
        dv * gain_attn,
        joined(fin_o, slice(0, 256)).T,
        grads_gain[1],
        dg * gain_mlp,
        du * gain_mlp,
        joined(fin_d, slice(0, 688)).T,
    )


def solution(mesh):
    mesh = Mesh(mesh.devices.reshape(4, 2, 4, 2, 2), AXES)
    seq, head = ("y", "xh", "z"), ("xl", "c")
    rows, cols, flat, turned = P(seq, None), P(seq, head), P(seq), P(head, seq)
    return jax.shard_map(
        per_device,
        mesh=mesh,
        in_specs=(rows, flat, cols, cols, cols, turned, flat, cols, cols, turned, P(), rows),
        out_specs=(rows, rows, flat, cols, cols, cols, turned, flat, cols, cols, turned),
        check_vma=False,
    )
```

```python
import jax
import jax.numpy as jnp
from jax import lax
from jax.experimental import pallas as pl
from jax.experimental.pallas import tpu as pltpu
from jax.sharding import Mesh, PartitionSpec as P

HEAD_DIM = 128
WINDOW = 64
BLOCK = 512
OWNED = 128
PIECES = 4
WIDE = 2048 // PIECES
AXES = ("y", "xh", "z", "xl", "c")

epsilon = 1e-05
masked_score = -1e30
f32 = jnp.float32
bf16 = jnp.bfloat16


MESH = pl.DeviceIdType.MESH
SCALE = HEAD_DIM ** (-0.5)
ANY = pl.BlockSpec(memory_space=pl.ANY)
TURNED = (((1,), (1,)), ((), ()))
LEFT_TURNED = (((0,), (0,)), ((), ()))


class Place:
    def __init__(self):
        self.y, self.z, self.c = lax.axis_index("y"), lax.axis_index("z"), lax.axis_index("c")
        self.xh, self.xl = lax.axis_index("xh"), lax.axis_index("xl")
        self.x = self.xh * 2 + self.xl
        self.q = self.xl * 2 + self.c

    def at(self, y=None, x=None, z=None, c=None):
        y = self.y if y is None else y
        x = self.x if x is None else x
        z = self.z if z is None else z
        c = self.c if c is None else c
        return (y, x // 2, z, x % 2, c)


class Links:
    def __init__(self, send_sems, recv_sems, local_sems):
        self.send_sems, self.recv_sems, self.local_sems = send_sems, recv_sems, local_sems
        self.count, self.local_count, self.started = 0, 0, []

    def send(self, src, dst, device):
        copy = self.prepare(src, dst, device)
        copy.start()
        return copy

    def prepare(self, src, dst, device):
        copy = pltpu.make_async_remote_copy(
            src_ref=src,
            dst_ref=dst,
            send_sem=self.send_sems.at[self.count],
            recv_sem=self.recv_sems.at[self.count],
            device_id=device,
            device_id_type=MESH,
        )
        self.count += 1
        self.started.append(copy)
        return copy

    def local(self, src, dst):
        copy = pltpu.make_async_copy(src, dst, self.local_sems.at[self.local_count])
        self.local_count += 1
        copy.start()
        return copy

    def settle(self, copies=None):
        copies = self.started if copies is None else copies
        for copy in copies:
            copy.wait_send()
        self.started = [copy for copy in self.started if not any(copy is other for other in copies)]


class WeightGather:
    def __init__(self, links, place, pack, whole, cut):
        self.links, self.place, self.whole = links, place, whole
        cols = whole.shape[-1]
        self.parts = (pl.ds(0, cut), pl.ds(cut, cols - cut))
        self.swap = links.send(
            pack(1 - place.xh), whole.at[place.y, place.xh, place.z], place.at(x=(place.x + 2) % 4)
        )
        self.mine = links.local(pack(place.xh), whole.at[place.y, place.xh, place.z])

    def send(self, ref, device):
        return self.links.send(ref, ref, device)

    def near(self, view_z, view_y):
        p = self.place
        first, second = self.parts
        zs = (p.at(z=(p.z + 1) % 4), p.at(z=(p.z + 3) % 4))
        ys = (p.at(y=(p.y + 1) % 4), p.at(y=(p.y + 3) % 4))
        (ref_z, axis_z), (ref_y, axis_y) = view_z, view_y
        to = {"z": zs, "y": ys}
        self.got = [
            self.send(ref_z, to[axis_z][0]),
            self.send(ref_y, to[axis_y][0]),
            self.send(ref_z, to[axis_z][1]),
            self.send(ref_y, to[axis_y][1]),
        ]

    def wait(self):
        for copy in self.got:
            copy.wait_recv()

    def start0(self):
        p, w = self.place, self.whole
        first, second = self.parts
        self.swap.wait_recv()
        self.mine.wait()
        self.near(
            (w.at[p.y, :, p.z, :, first], "z"),
            (w.at[p.y, :, p.z, :, second], "y"),
        )

    def start1(self):
        p, w = self.place, self.whole
        first, second = self.parts
        self.wait()
        zn, zp, yn, yp = (p.z + 1) % 4, (p.z + 3) % 4, (p.y + 1) % 4, (p.y + 3) % 4
        self.got = [
            self.send(w.at[p.y, 0, zp, :, first], p.at(z=zn)),
            self.send(w.at[yp, 0, p.z, :, second], p.at(y=yn)),
            self.send(w.at[p.y, 1, zn, :, first], p.at(z=zp)),
            self.send(w.at[yn, 1, p.z, :, second], p.at(y=yp)),
        ]

    def start2(self):
        p, w = self.place, self.whole
        first, second = self.parts
        self.wait()
        self.near(
            (w.at[:, :, p.z, :, second], "z"),
            (w.at[p.y, :, :, :, first], "y"),
        )

    def start3(self):
        p, w = self.place, self.whole
        first, second = self.parts
        self.wait()
        zn, zp, yn, yp = (p.z + 1) % 4, (p.z + 3) % 4, (p.y + 1) % 4, (p.y + 3) % 4
        self.got = [
            self.send(w.at[yp, 0, :, :, first], p.at(y=yn)),
            self.send(w.at[:, 0, zp, :, second], p.at(z=zn)),
            self.send(w.at[yn, 1, :, :, first], p.at(y=yp)),
            self.send(w.at[:, 1, zn, :, second], p.at(z=zp)),
        ]

    def done(self):
        self.wait()


def greet(place):
    p = place
    barrier = pltpu.get_barrier_semaphore()
    partners = (
        p.at(z=(p.z + 1) % 4),
        p.at(z=(p.z + 3) % 4),
        p.at(y=(p.y + 1) % 4),
        p.at(y=(p.y + 3) % 4),
        p.at(x=(p.x + 1) % 4),
        p.at(x=(p.x + 3) % 4),
        p.at(x=(p.x + 2) % 4),
        p.at(c=1 - p.c),
        p.at(x=2 * p.xh + 1 - p.xl, c=1 - p.c),
    )
    for device in partners:
        pl.semaphore_signal(barrier, inc=1, device_id=device, device_id_type=MESH)

    @pl.when(p.z == 3)
    def _():
        pl.semaphore_signal(barrier, inc=1, device_id=p.at(y=(p.y + 1) % 4, z=0 * p.z), device_id_type=MESH)

    @pl.when(p.z == 0)
    def _():
        pl.semaphore_signal(barrier, inc=1, device_id=p.at(y=(p.y + 3) % 4, z=0 * p.z + 3), device_id_type=MESH)

    pl.semaphore_wait(barrier, 9 + jnp.where((p.z == 3) | (p.z == 0), 1, 0))


def unit_scale(values):
    return values * lax.rsqrt(jnp.mean(values * values, axis=-1, keepdims=True) + epsilon)


class WeightReduce:
    def __init__(self, links, place, total, first_in, second_in, out, cut):
        self.links, self.place, self.total, self.out = links, place, total, out
        self.one, self.two = first_in, second_in
        cols = total.shape[-1]
        self.cols = cols
        self.parts = (pl.ds(0, cut), pl.ds(cut, cols - cut))
        p = place
        self.yn, self.yp, self.yf = (p.y + 1) % 4, (p.y + 3) % 4, (p.y + 2) % 4
        self.zn, self.zp, self.zf = (p.z + 1) % 4, (p.z + 3) % 4, (p.z + 2) % 4
        self.next_y, self.prev_y = p.at(y=self.yn), p.at(y=self.yp)
        self.next_z, self.prev_z = p.at(z=self.zn), p.at(z=self.zp)

    def start0(self):
        a, b = self.parts
        t, one, send = self.total, self.one, self.links.send
        self.far = [
            send(t.at[self.yf, 0, :, :, a], one.at[0, :, :, a], self.next_y),
            send(t.at[:, 0, self.zf, :, b], one.at[0, :, :, b], self.next_z),
            send(t.at[self.yf, 1, :, :, a], one.at[2, :, :, a], self.prev_y),
            send(t.at[:, 1, self.zf, :, b], one.at[2, :, :, b], self.prev_z),
        ]
        self.near = [
            send(t.at[self.yn, 1, :, :, a], one.at[1, :, :, a], self.next_y),
            send(t.at[:, 1, self.zn, :, b], one.at[1, :, :, b], self.next_z),
            send(t.at[self.yp, 0, :, :, a], one.at[3, :, :, a], self.prev_y),
            send(t.at[:, 0, self.zp, :, b], one.at[3, :, :, b], self.prev_z),
        ]

    def add(self, target, sources, rows):
        def body(i, _):
            ref = target(i)
            value = ref[...].astype(f32)
            for source in sources:
                value = value + source(i)[...].astype(f32)
            ref[...] = value.astype(bf16)
            return 0

        lax.fori_loop(0, rows, body, 0)

    def start1(self):
        a, b = self.parts
        t, one, send = self.total, self.one, self.links.send
        yn, yp, zn, zp = self.yn, self.yp, self.zn, self.zp
        self.sums = []
        self.far[0].wait_recv()
        self.add(lambda i: t.at[yn, 0, i, :, a], [lambda i: one.at[0, i, :, a]], 4)
        self.sums.append(send(t.at[yn, 0, :, :, a], one.at[4, :, :, a], self.next_y))
        self.far[1].wait_recv()
        self.add(lambda i: t.at[i, 0, zn, :, b], [lambda i: one.at[0, i, :, b]], 4)
        self.sums.append(send(t.at[:, 0, zn, :, b], one.at[4, :, :, b], self.next_z))
        self.far[2].wait_recv()
        self.add(lambda i: t.at[yp, 1, i, :, a], [lambda i: one.at[2, i, :, a]], 4)
        self.sums.append(send(t.at[yp, 1, :, :, a], one.at[5, :, :, a], self.prev_y))
        self.far[3].wait_recv()
        self.add(lambda i: t.at[i, 1, zp, :, b], [lambda i: one.at[2, i, :, b]], 4)
        self.sums.append(send(t.at[:, 1, zp, :, b], one.at[5, :, :, b], self.prev_z))

    def start2(self):
        a, b = self.parts
        t, one, two, send = self.total, self.one, self.two, self.links.send
        p = self.place
        for copy in self.near + self.sums:
            copy.wait_recv()
        self.add(lambda i: t.at[p.y, 0, i, :, a], [lambda i: one.at[3, i, :, a], lambda i: one.at[4, i, :, a]], 4)
        self.add(lambda i: t.at[p.y, 1, i, :, a], [lambda i: one.at[1, i, :, a], lambda i: one.at[5, i, :, a]], 4)
        self.add(lambda i: t.at[i, 0, p.z, :, b], [lambda i: one.at[3, i, :, b], lambda i: one.at[4, i, :, b]], 4)
        self.add(lambda i: t.at[i, 1, p.z, :, b], [lambda i: one.at[1, i, :, b], lambda i: one.at[5, i, :, b]], 4)
        self.far = [
            send(t.at[p.y, 0, self.zf, :, a], two.at[0, :, a], self.next_z),
            send(t.at[self.yf, 0, p.z, :, b], two.at[0, :, b], self.next_y),
            send(t.at[p.y, 1, self.zf, :, a], two.at[2, :, a], self.prev_z),
            send(t.at[self.yf, 1, p.z, :, b], two.at[2, :, b], self.prev_y),
        ]
        self.near = [
            send(t.at[p.y, 1, self.zn, :, a], two.at[1, :, a], self.next_z),
            send(t.at[self.yn, 1, p.z, :, b], two.at[1, :, b], self.next_y),
            send(t.at[p.y, 0, self.zp, :, a], two.at[3, :, a], self.prev_z),
            send(t.at[self.yp, 0, p.z, :, b], two.at[3, :, b], self.prev_y),
        ]

    def plus(self, target, *sources):
        value = target[...].astype(f32)
        for source in sources:
            value = value + source[...].astype(f32)
        target[...] = value.astype(bf16)

    def start3(self):
        a, b = self.parts
        t, two, send = self.total, self.two, self.links.send
        p = self.place
        yn, yp, zn, zp = self.yn, self.yp, self.zn, self.zp
        self.sums = []
        for k, ref, lanes, slot, other, device in (
            (0, t.at[p.y, 0, zn, :, a], a, 0, 4, self.next_z),
            (1, t.at[yn, 0, p.z, :, b], b, 0, 4, self.next_y),
            (2, t.at[p.y, 1, zp, :, a], a, 2, 5, self.prev_z),
            (3, t.at[yp, 1, p.z, :, b], b, 2, 5, self.prev_y),
        ):
            self.far[k].wait_recv()
            self.plus(ref, two.at[slot, :, lanes])
            self.sums.append(send(ref, two.at[other, :, lanes], device))

    def start4(self):
        t, two, out = self.total, self.two, self.out
        p = self.place
        for copy in self.near + self.sums:
            copy.wait_recv()
        self.plus(t.at[p.y, 0, p.z], two.at[3], two.at[4])
        self.plus(t.at[p.y, 1, p.z], two.at[1], two.at[5])
        self.swap = self.links.send(t.at[p.y, 1 - p.xh, p.z], out.at[p.xh], p.at(x=(p.x + 2) % 4))
        self.mine = self.links.local(t.at[p.y, p.xh, p.z], out.at[p.xh])

    def done(self):
        self.swap.wait_recv()
        self.mine.wait()


class GroupReduce:
    def __init__(self, place, partial, bufs, sems):
        self.place, self.partial = place, partial
        self.send_c, self.recv_c, self.tmp, self.snd, self.rcv, self.own = bufs
        self.send_sems, self.recv_sems = sems

    def copy(self, src, dst, index, device):
        return pltpu.make_async_remote_copy(
            src_ref=src,
            dst_ref=dst,
            send_sem=self.send_sems.at[index],
            recv_sem=self.recv_sems.at[index],
            device_id=device,
            device_id_type=MESH,
        )

    def crossing(self, n):
        return self.copy(self.send_c.at[n % 2], self.recv_c.at[n], n, self.place.at(c=1 - self.place.c))

    def to_next(self, n):
        pair = pl.ds(0, 2)
        return self.copy(
            self.snd.at[n, pair], self.rcv.at[n, pair], PIECES + n, self.place.at(x=(self.place.x + 1) % 4)
        )

    def to_prev(self, n):
        pair = pl.ds(2, 2)
        return self.copy(
            self.snd.at[n, pair], self.rcv.at[n, pair], 2 * PIECES + n, self.place.at(x=(self.place.x + 3) % 4)
        )

    def sum_next(self, n):
        return self.copy(
            self.snd.at[n, 4], self.rcv.at[n, 4], 3 * PIECES + n, self.place.at(x=(self.place.x + 1) % 4)
        )

    def sum_prev(self, n):
        return self.copy(
            self.snd.at[n, 5], self.rcv.at[n, 5], 4 * PIECES + n, self.place.at(x=(self.place.x + 3) % 4)
        )

    def sibling_part(self, n):
        part = self.partial(n, 1 - self.place.c)

        @pl.when(n >= 2)
        def _():
            self.crossing(n - 2).wait_send()

        self.send_c[n % 2] = part.astype(bf16).reshape(4, OWNED, WIDE)
        self.crossing(n).start()

    def own_part(self, n, launch):
        p, tmp, snd = self.place, self.tmp, self.snd
        part = self.partial(n, p.c).reshape(4, OWNED, WIDE)
        self.crossing(n).wait_recv()
        tmp[...] = part + self.recv_c[n].astype(f32)
        far, nxt, prev = (p.x + 2) % 4, (p.x + 1) % 4, (p.x + 3) % 4
        low, high = pl.ds(0, 64), pl.ds(64, 64)
        snd[n, 0] = tmp[far, low].astype(bf16)
        snd[n, 1] = tmp[nxt, high].astype(bf16)
        if launch:
            self.to_next(n).start()
        snd[n, 2] = tmp[far, high].astype(bf16)
        snd[n, 3] = tmp[prev, low].astype(bf16)
        if launch:
            self.to_prev(n).start()
        snd[n, 4] = tmp[nxt, low].astype(bf16)
        snd[n, 5] = tmp[prev, high].astype(bf16)
        self.own[:, pl.ds(pl.multiple_of(n * WIDE, WIDE), WIDE)] = tmp[p.x]

    def pass_on(self, n):
        snd, rcv = self.snd, self.rcv
        self.to_next(n).wait_recv()
        snd[n, 4] = (snd[n, 4].astype(f32) + rcv[n, 0].astype(f32)).astype(bf16)
        self.sum_next(n).start()
        self.to_prev(n).wait_recv()
        snd[n, 5] = (snd[n, 5].astype(f32) + rcv[n, 2].astype(f32)).astype(bf16)
        self.sum_prev(n).start()

    def run(self, launch=True, pass_on=True, hooks=()):
        def body(i, _):
            @pl.when(i < PIECES)
            def _():
                self.sibling_part(i)

            @pl.when((i >= 1) & (i < PIECES + 1))
            def _():
                self.own_part(i - 1, launch)

            if pass_on:

                @pl.when(i >= 2)
                def _():
                    self.pass_on(i - 2)

            for step, hook in hooks:
                pl.when(i == step)(hook)
            return 0

        lax.fori_loop(0, PIECES + 2 if pass_on else PIECES + 1, body, 0)

    def launch(self):
        def body(n, _):
            self.to_next(n).start()
            self.to_prev(n).start()
            return 0

        lax.fori_loop(0, PIECES, body, 0)

    def pass_range(self, start, stop):
        def body(n, _):
            self.pass_on(n)
            return 0

        lax.fori_loop(start, stop, body, 0)

    def finish(self):
        def body(n, _):
            lanes = pl.ds(pl.multiple_of(n * WIDE, WIDE), WIDE)
            low, high = pl.ds(0, 64), pl.ds(64, 64)
            rcv, own = self.rcv, self.own
            self.sum_next(n).wait_recv()
            own[low, lanes] = own[low, lanes] + rcv[n, 3].astype(f32) + rcv[n, 4].astype(f32)
            self.sum_prev(n).wait_recv()
            own[high, lanes] = own[high, lanes] + rcv[n, 1].astype(f32) + rcv[n, 5].astype(f32)
            return 0

        lax.fori_loop(0, PIECES, body, 0)

    def sent(self):
        def body(n, _):
            for copy in (self.to_next, self.to_prev, self.sum_next, self.sum_prev):
                copy(n).wait_send()
            return 0

        self.crossing(PIECES - 2).wait_send()
        self.crossing(PIECES - 1).wait_send()

        lax.fori_loop(0, PIECES, body, 0)


class GroupGather:
    def __init__(self, links, place, whole):
        self.links, self.place, self.whole = links, place, whole
        self.low, self.high = pl.ds(0, 64), pl.ds(64, 64)

    def send(self, ref, device):
        return self.links.send(ref, ref, device)

    def start(self):
        p, w = self.place, self.whole
        self.nxt, self.prev, self.far = (p.x + 1) % 4, (p.x + 3) % 4, (p.x + 2) % 4
        self.to_next, self.to_prev = p.at(x=self.nxt), p.at(x=self.prev)
        self.sibling = p.at(c=1 - p.c)
        low, high = w.at[p.x, p.c, self.low], w.at[p.x, p.c, self.high]
        self.first = [self.send(low, self.to_next), self.send(high, self.to_prev)]
        self.second = [self.send(high, self.to_next), self.send(low, self.to_prev)]
        tiles = (p.x, self.prev, self.nxt, self.far)
        self.paired = [self.later(w.at[x, p.c], self.sibling) for x in tiles]
        self.paired[0].start()
        self.third = [
            self.later(w.at[self.prev, p.c, self.low], self.to_next),
            self.later(w.at[self.nxt, p.c, self.high], self.to_prev),
        ]

    def later(self, ref, device):
        return self.links.prepare(ref, ref, device)

    def forward(self):
        for k in range(2):
            self.first[k].wait_recv()
            self.third[k].start()

    def share_near(self):
        for k in range(2):
            self.second[k].wait_recv()
            self.paired[1 + k].start()

    def share_far(self):
        for copy in self.third:
            copy.wait_recv()
        self.paired[3].start()

    def sent(self):
        self.links.settle(self.first + self.second + self.third + self.paired)

    def ready(self, k):
        self.paired[k].wait_recv()


class BlockExchange:
    def __init__(self, links, place, block, whole):
        p = place
        self.place, self.links = p, links
        beside = p.at(x=2 * p.xh + 1 - p.xl)
        sibling = p.at(c=1 - p.c)
        self.near, self.next = 3 - p.x, 2 * (1 - p.xh) + p.xl
        halves = [pl.ds(0, 64), pl.ds(64, 64)]
        self.cross = [links.send(block.at[p.xl, p.c, h], whole.at[p.x, p.c, h], p.at(x=3 - p.x)) for h in halves]
        self.across = [
            links.prepare(whole.at[self.near, p.c, h], whole.at[self.near, p.c, h], beside) for h in halves
        ]
        self.paired = [
            links.prepare(whole.at[x, p.c], whole.at[x, p.c], sibling) for x in (self.near, self.next)
        ]

    def forward(self, k):
        self.cross[k].wait_recv()
        self.across[k].start()

    def share(self):
        self.paired[0].start()

    def share_next(self):
        for copy in self.across:
            copy.wait_recv()
        self.paired[1].start()

    def done(self, k):
        self.paired[k].wait_recv()


class BlockReduce(GroupReduce):
    def __init__(self, place, partial, bufs, sems, extra=None):
        self.place, self.partial, self.extra = place, partial, extra
        self.send_c, self.recv_c, self.tmp, self.moving = bufs
        self.send_sems, self.recv_sems = sems
        self.facing, self.beside = place.at(x=3 - place.x), place.at(x=2 * place.xh + 1 - place.xl)

    def part(self, which, n):
        lanes = pl.ds(pl.multiple_of(n * WIDE, WIDE), WIDE)
        return self.moving.at[pl.ds(2 * (which // 2), 2), which % 2, :, lanes]

    def over(self, n):
        return self.copy(self.part(0, n), self.part(1, n), PIECES + n, self.facing)

    def across(self, n):
        return self.copy(self.part(2, n), self.part(3, n), 2 * PIECES + n, self.beside)

    def own_part(self, n, launch):
        p, tmp = self.place, self.tmp
        part = self.partial(n, p.c).reshape(4, OWNED, WIDE)
        self.crossing(n).wait_recv()
        tmp[...] = part + self.recv_c[n].astype(f32)
        if self.extra is not None:
            lanes = pl.ds(pl.multiple_of(n * WIDE, WIDE), WIDE)
            tmp[p.x] += self.extra[:, lanes]
        self.part(0, n)[...] = tmp[pl.ds(2 * (1 - p.xh), 2)].astype(bf16)
        if launch:
            self.over(n).start()
        self.part(2, n)[...] = tmp[pl.ds(2 * p.xh, 2)].astype(bf16)

    def pass_on(self, n):
        self.over(n).wait_recv()
        mine = self.part(2, n)
        mine[...] = (mine[...].astype(f32) + self.part(1, n)[...].astype(f32)).astype(bf16)
        self.across(n).start()

    def launch(self):
        def body(n, _):
            self.over(n).start()
            return 0

        lax.fori_loop(0, PIECES, body, 0)

    def finish(self):
        def body(n, _):
            self.across(n).wait_recv()
            return 0

        lax.fori_loop(0, PIECES, body, 0)

    def total(self, tile, rows):
        return self.moving[2 + tile, 0, rows].astype(f32) + self.moving[2 + tile, 1, rows].astype(f32)

    def crossed(self):
        self.crossing(PIECES - 2).wait_send()
        self.crossing(PIECES - 1).wait_send()

    def sent(self):
        def body(n, _):
            self.over(n).wait_send()
            self.across(n).wait_send()
            return 0

        lax.fori_loop(0, PIECES, body, 0)


class BlockOut:
    def __init__(self, links, place, rows, out):
        mine = out.at[:, place.c]
        self.local = links.local(rows, mine)
        self.paired = links.send(rows, mine, place.at(c=1 - place.c))

    def done(self):
        self.paired.wait_recv()
        self.local.wait()


def norm_back(e, values):
    r = lax.rsqrt(jnp.mean(values * values, axis=-1, keepdims=True) + epsilon)
    return r * e - values * r**3 * jnp.mean(e * values, axis=-1, keepdims=True)


def column(gain):
    row = gain[...].astype(f32).reshape(1, 64)
    places = [lax.broadcasted_iota(jnp.int32, (64, 64), k) for k in range(2)]
    return jnp.sum(jnp.where(places[0] == places[1], row, 0.0), axis=1, keepdims=True)


def pack_attn(gain, query, key, value, pack):
    for i, ref in enumerate((query, key, value)):
        scaled = (ref[...].astype(f32) * gain).astype(bf16)
        for k in range(2):
            pack(k)[:, 256 * i : 256 * i + 256] = scaled[:, 256 * k : 256 * k + 256]


def pack_out(out, pack):
    for k in range(2):
        pack(k)[...] = out[:, 256 * k : 256 * k + 256]


def pack_ff(gain, gate, up, down, pack_gu, pack_d):
    zeros = jnp.zeros((64, 16), f32)
    for k in range(2):
        start = 688 * k
        tails = []
        for i, ref in enumerate((gate, up)):
            part = ref[:, start : start + 640].astype(f32) * gain
            pack_gu(k)[:, 640 * i : 640 * i + 640] = part.astype(bf16)
            tails += [ref[:, start + 640 : start + 688].astype(f32) * gain, zeros]
        pack_gu(k)[:, 1280:] = jnp.concatenate(tails, axis=1).astype(bf16)
        part = down[:, start : start + 688].astype(f32)
        pack_d(k)[...] = jnp.concatenate([part, jnp.zeros((64, 80), f32)], axis=1).astype(bf16)


def row_dots(weight, grads):
    return jnp.sum(weight.astype(f32) * grads.astype(f32), axis=1, keepdims=True)


def final_kernel(
    result_in, input_in, fin_gu, fin_d, fin_q, fin_o, sums, gain_attn, gain_mlp,
    result, input_grad, g_attn, query, key, value, out, g_mlp, gate, up, down,
    hold, sems,
):
    loads = [pltpu.make_async_copy(ref, hold.at[k], sems.at[k]) for k, ref in enumerate((result_in, input_in))]
    for copy in loads:
        copy.start()
    attn, mlp = column(gain_attn), column(gain_mlp)
    for i, ref in enumerate((query, key, value)):
        for k in range(2):
            ref[:, 256 * k : 256 * k + 256] = fin_q[k, :, 256 * i : 256 * i + 256].astype(f32) * attn
    for k in range(2):
        out[:, 256 * k : 256 * k + 256] = fin_o[k].astype(f32)
        down[:, 688 * k : 688 * k + 688] = fin_d[k, :, :688].astype(f32)
        tail = fin_gu[k, :, 1280:].astype(f32) * mlp
        for i, ref in enumerate((gate, up)):
            ref[:, 688 * k : 688 * k + 640] = fin_gu[k, :, 640 * i : 640 * i + 640].astype(f32) * mlp
            ref[:, 688 * k + 640 : 688 * k + 688] = tail[:, 64 * i : 64 * i + 48]
    turned = sums[...].T
    g_attn[...] = turned[0:1]
    g_mlp[...] = turned[1:2]
    stores = [pltpu.make_async_copy(hold.at[k], ref, sems.at[2 + k]) for k, ref in enumerate((result, input_grad))]
    for k in range(2):
        loads[k].wait()
        stores[k].start()
    for copy in stores:
        copy.wait()


def final_call(result, input_grad, fin_gu, fin_d, fin_q, fin_o, sums, gain_attn, gain_mlp):
    sds = jax.ShapeDtypeStruct
    vmem = pl.BlockSpec(memory_space=pltpu.VMEM)
    whole = (2, 2, OWNED, 2048)
    outs = pl.pallas_call(
        final_kernel,
        out_shape=(
            sds(whole, bf16),
            sds(whole, bf16),
            sds((1, 64), f32),
            sds((64, 512), f32),
            sds((64, 512), f32),
            sds((64, 512), f32),
            sds((64, 512), f32),
            sds((1, 64), f32),
            sds((64, 1376), f32),
            sds((64, 1376), f32),
            sds((64, 1376), f32),
        ),
        in_specs=[ANY] * 2 + [vmem] * 7,
        out_specs=[ANY] * 2 + [vmem] * 9,
        scratch_shapes=[pltpu.VMEM((2,) + whole, bf16), pltpu.SemaphoreType.DMA((4,))],
        compiler_params=pltpu.CompilerParams(vmem_limit_bytes=62 * 2**20),
        name="final",
    )(result, input_grad, fin_gu, fin_d, fin_q, fin_o, sums, gain_attn, gain_mlp)
    result, input_grad, g_attn, query, key, value, out, g_mlp, gate, up, down = outs
    return (
        result.reshape(BLOCK, 2048),
        input_grad.reshape(BLOCK, 2048),
        g_attn.reshape(64),
        query,
        key,
        value,
        out.T,
        g_mlp.reshape(64),
        gate,
        up,
        down.T,
    )


def block_kernel(
    lengths, gain_attn, gain_mlp, w_query, w_key, w_value, w_out, w_gate, w_up, w_down, hid, cot_in,
    result_o, grad_o, fin_gu_o, fin_d_o, fin_q_o, fin_o_o, sums_o, xr_o, qm_o,
    raw_g, raw_u, raw_d,
    fin_gu, fin_d, fin_q, fin_o, sums, sums_in,
    wq, wo, gu, d, nm, cot, act, gg, kv, resid, hid_pair, own, gb,
    last_kv, tail_out, tail_in, in_gu, in_d, in_q, in_o, in2_gu, in2_d, in2_q, in2_o,
    send_c, snd, tmp, recv_c, rcv,
    send_sems, recv_sems, local_sems, group_send, group_recv, ready,
):
    p = Place()
    links = Links(send_sems, recv_sems, local_sems)
    sibling = p.at(c=1 - p.c)
    facing, beside = p.at(x=3 - p.x), p.at(x=2 * p.xh + 1 - p.xl)

    def signal(semaphore, devices):
        for device in devices:
            pl.semaphore_signal(semaphore, inc=1, device_id=device, device_id_type=MESH)

    hidg, xr = gb, nm

    own_pair = pl.ds(2 * p.xh, 2)
    own_hidden = links.local(hid, hidg.at[own_pair])
    load_hid = links.local(hid.at[:, p.c], hid_pair)
    own_cot = links.local(cot_in, cot.at[own_pair])
    raw_q, raw_k, raw_v, raw_o = (snd.at[0, k] for k in range(4))
    half = lambda k: pl.ds(64 * k, 64)
    pk_q, pk_d = (lambda k: act.at[0, 0, half(k)]), (lambda k: act.at[0, 1, half(k)])
    pk_o, pk_gu = (lambda k: act.at[1, 0, half(k), pl.ds(0, 256)]), (lambda k: gg.at[0, 0, half(k)])
    raws = ((w_query, raw_q), (w_key, raw_k), (w_value, raw_v), (w_out, raw_o), (w_gate, raw_g), (w_up, raw_u), (w_down, raw_d))
    loads = [links.local(ref, raw) for ref, raw in raws]
    greet(p)
    scale_attn, scale_mlp = column(gain_attn), column(gain_mlp)
    for copy in loads[:4]:
        copy.wait()
    pack_attn(scale_attn, raw_q, raw_k, raw_v, pk_q)
    pack_out(raw_o, pk_o)
    g_q = WeightGather(links, p, pk_q, wq, 384)
    g_o = WeightGather(links, p, pk_o, wo, 128)
    e_hid = BlockExchange(links, p, hid, hidg)
    for copy in loads[4:]:
        copy.wait()
    pack_ff(scale_mlp, raw_g, raw_u, raw_d, pk_gu, pk_d)
    g_q.start0()
    g_o.start0()
    def norm_rows(tile, core):
        def body(i, _):
            r = pl.ds(i * 32, 32)
            xr[tile, core, r] = unit_scale(hidg[tile, core, r].astype(f32)).astype(bf16)
            return 0

        lax.fori_loop(0, 4, body, 0)

    def norm_own(i, _):
        norm_rows(2 * p.xh + i // 2, i % 2)
        return 0

    own_hidden.wait()
    lax.fori_loop(0, 4, norm_own, 0)
    g_q.start1()
    g_o.start1()
    e_hid.forward(0)
    g_q.start2()
    g_gu = WeightGather(links, p, pk_gu, gu, 768)
    g_d = WeightGather(links, p, pk_d, d, 384)
    e_hid.forward(1)
    e_hid.share()
    e_cot = BlockExchange(links, p, cot_in, cot)
    norm_rows(e_hid.near, p.c)
    g_q.start3()
    g_o.start2()
    g_gu.start0()
    g_d.start0()
    e_hid.done(0)
    norm_rows(e_hid.near, 1 - p.c)
    g_q.done()

    links.settle([g_q.swap, g_o.swap, g_gu.swap, g_d.swap])

    def project(t):
        w = wq[...].reshape(2048, 768)
        out = jnp.dot(xr[t].reshape(256, 2048), w, preferred_element_type=f32).astype(bf16)
        gg[t, :, :, 0:256] = out[:, :256].reshape(2, OWNED, 256)
        kv[t // 2, pl.ds((t % 2) * 256 + WINDOW, 256)] = out[:, 256:]

    def project_three(i, _):
        project(jnp.where(i < 2, 2 * p.xh + i, e_hid.near))
        return 0

    lax.fori_loop(0, 3, project_three, 0)
    g_o.start3()
    e_hid.share_next()
    norm_rows(e_hid.next, p.c)
    g_gu.start1()
    g_d.start1()
    e_cot.forward(0)
    e_hid.done(1)
    norm_rows(e_hid.next, 1 - p.c)
    xr_spill = links.local(xr, xr_o)
    project(e_hid.next)

    tails = []
    last = jnp.where(p.z == 3, 1, 0)
    for block in range(2):
        to_y = p.y if block == 0 else (p.y + last) % 4
        slot = last if block == 0 else 1 - last
        tails.append(
            links.send(
                kv.at[block, pl.ds(BLOCK, WINDOW)],
                kv.at[slot, pl.ds(0, WINDOW)],
                p.at(y=to_y, z=(p.z + 1) % 4),
            )
        )
    end0 = lengths[0]
    end1 = end0 + lengths[1]

    def masked(scores, block, chunk):
        start = (p.y * 8 + block * 4 + p.z) * BLOCK + chunk * 128
        query = start + lax.broadcasted_iota(jnp.int32, (128, 192), 0)
        key = start - WINDOW + lax.broadcasted_iota(jnp.int32, (128, 192), 1)
        seen = (key <= query) & (key > query - WINDOW) & (key >= 0)
        for end in (end0, end1):
            seen = seen & ((key >= end) | (query < end))
        return jnp.where(seen, scores, masked_score)

    def probabilities(query, keys, block, chunk):
        scores = lax.dot_general(query, keys, TURNED, preferred_element_type=f32) * SCALE
        scores = masked(scores, block, chunk)
        expo = jnp.exp(scores - jnp.max(scores, axis=-1, keepdims=True))
        return expo / jnp.sum(expo, axis=-1, keepdims=True)

    def attend(block, chunk):
        x, core = block * 2 + chunk // 2, chunk % 2
        r = pl.multiple_of(chunk * 128, 128)
        for head in range(2):
            lane = head * 128
            query = gg[x, core, :, lane : lane + 128]
            keys = kv[block, pl.ds(r, 192), lane : lane + 128]
            values = kv[block, pl.ds(r, 192), lane + 256 : lane + 384]
            probs = probabilities(query, keys, block, chunk).astype(bf16)
            out = jnp.dot(probs, values, preferred_element_type=f32)
            gg[x, core, :, lane + 256 : lane + 384] = out.astype(bf16)

    def inner(i, _):
        attend(i // 3, i % 3 + 1)
        return 0

    e_cot.forward(1)
    e_cot.share()
    g_gu.start2()
    g_d.start2()
    lax.fori_loop(0, 6, inner, 0)
    e_cot.share_next()
    for copy in tails:
        copy.wait_recv()

    def first_chunk(i, _):
        attend(i, 0)
        return 0

    lax.fori_loop(0, 2, first_chunk, 0)
    mixed = gg.at[:, :, :, pl.ds(256, 256)]
    g_o.done()
    xr_spill.wait()

    def partial_of(left, right, width, start=0):
        def partial(n, core):
            return lax.dot_general(
                left[:, core, :, start : start + width].reshape(512, width),
                right[n].reshape(WIDE, width),
                TURNED,
                preferred_element_type=f32,
            )

        return partial

    def group_reduce(k, partial):
        span = pl.ds(5 * PIECES * k, 5 * PIECES)
        return GroupReduce(
            p, partial, (send_c, recv_c, tmp.at[pl.ds(0, 4)], snd, rcv, own), (group_send.at[span], group_recv.at[span])
        )

    r_branch = group_reduce(0, partial_of(gg, wo, 256, 256))
    r_branch.run(pass_on=False)
    r_branch.pass_range(0, 3)
    g_gu.start3()
    r_branch.pass_range(3, 4)
    g_d.start3()
    load_hid.wait()
    r_branch.finish()

    def resid_rows(i, _):
        r = pl.ds(i * 16, 16)
        total = hid_pair[p.xl, r].astype(f32) + own[r]
        resid[r] = total
        nm[p.x, p.c, r] = unit_scale(total).astype(bf16)
        return 0

    lax.fori_loop(0, OWNED // 16, resid_rows, 0)
    g_nm = GroupGather(links, p, nm)
    g_nm.start()
    q_spill = links.local(gg.at[:, :, :, pl.ds(0, 512)], qm_o)
    g_gu.done()
    own_cot.wait()
    for k in range(2):
        e_cot.done(k)
    q_spill.wait()
    g_d.done()
    g_nm.ready(0)

    def feed(k, _):
        @pl.when(k == 1)
        def _():
            g_nm.forward()
            g_nm.share_near()
            g_nm.ready(1)

        @pl.when(k == 2)
        def _():
            g_nm.ready(2)

        @pl.when(k == 3)
        def _():
            g_nm.share_far()
            g_nm.ready(3)

        t = (p.x + jnp.where(k == 0, 0, jnp.where(k == 1, 3, k - 1))) % 4
        part = jnp.dot(nm[t].reshape(256, 2048), gu[...].reshape(2048, 1408), preferred_element_type=f32)
        back = jnp.dot(cot[t].reshape(256, 2048), d[...].reshape(2048, 768), preferred_element_type=f32)
        tail = part[:, 1280:]
        flipped = pltpu.roll(tail, 64, 1)
        lane = lax.broadcasted_iota(jnp.int32, (256, 128), 1)
        for lanes, gate, up in (
            (slice(0, 640), part[:, :640], part[:, 640:1280]),
            (slice(640, 768), tail, flipped),
        ):
            sig = 1 / (1 + jnp.exp(-gate))
            silu = gate * sig
            grad_act = back[:, lanes]
            act[t, :, :, lanes] = (silu * up).astype(bf16).reshape(2, OWNED, -1)
            grad_gate = grad_act * up * sig * (1 + gate * (1 - sig))
            grad_up = grad_act * silu
            if lanes.start == 0:
                gg[t, :, :, :640] = grad_gate.astype(bf16).reshape(2, OWNED, 640)
                gg[t, :, :, 640:1280] = grad_up.astype(bf16).reshape(2, OWNED, 640)
            else:
                both = jnp.where(lane < 64, grad_gate, pltpu.roll(grad_up, 64, 1))
                gg[t, :, :, 1280:] = both.astype(bf16).reshape(2, OWNED, 128)
        return 0

    lax.fori_loop(0, 4, feed, 0)

    r_branch.sent()
    links.settle()
    r_mlp = group_reduce(1, partial_of(gg, gu, 1408))
    r_mlp.run(pass_on=False)

    def grads_into(out, left, right, width, reduce=None):
        def body(n, _):
            lanes = pl.ds(pl.multiple_of(n * 256, 256), 256)
            part = lax.dot_general(
                left[:, :, :, lanes].reshape(1024, 256),
                right[...].reshape(1024, width),
                LEFT_TURNED,
                preferred_element_type=f32,
            )
            out[n // 2, n % 2] = part.astype(bf16).reshape(4, 64, width)
            if reduce is not None:

                @pl.when(n % 2 == 0)
                def _():
                    reduce.pass_on(n // 2)

            return 0

        lax.fori_loop(0, 8, body, 0)

    grads_into(gu, nm, gg, 1408, r_mlp)
    w_gu = WeightReduce(links, p, gu, in_gu, in2_gu, fin_gu, 768)
    w_gu.start0()
    signal(ready.at[0], (facing, beside))
    load_qm = links.local(qm_o, gg.at[:, :, :, pl.ds(0, 512)])
    r_mlp.finish()

    def grad_rows(i, _):
        r = pl.ds(i * 16, 16)
        grad = cot[p.x, p.c, r].astype(f32) + norm_back(own[r], resid[r])
        gb[p.x, p.c, r] = grad.astype(bf16)
        return 0

    lax.fori_loop(0, OWNED // 16, grad_rows, 0)
    g_branch = GroupGather(links, p, gb)
    g_branch.start()
    r_mlp.sent()
    g_branch.ready(0)

    def block_reduce(k, partial, moving, extra=None):
        span = pl.ds(5 * PIECES * k, 5 * PIECES)
        sems = (group_send.at[span], group_recv.at[span])
        return BlockReduce(p, partial, (send_c, recv_c, tmp.at[pl.ds(0, 4)], moving), sems, extra)

    r_out = block_reduce(2, partial_of(act, d, 768), nm, resid)
    r_out.run(launch=False, pass_on=False)
    g_branch.forward()
    w_gu.start1()
    grads_into(d, cot, act, 768)
    signal(ready.at[1], (facing, beside, sibling))
    w_d = WeightReduce(links, p, d, in_d, in2_d, fin_d, 384)
    w_d.start0()
    g_branch.share_near()

    def grad_mixed(t):
        out = jnp.dot(gb[t].reshape(256, 2048), wo[...].reshape(2048, 256), preferred_element_type=f32)
        gg[t, :, :, 512:768] = out.astype(bf16).reshape(2, OWNED, 256)

    first = jnp.where(p.z == 0, 1, 0)
    tails = []

    def attend_back(block):
        tmp[...] = jnp.zeros_like(tmp)

        def chunk_body(chunk, _):
            x, core = block * 2 + chunk // 2, chunk % 2
            r = pl.multiple_of(chunk * 128, 128)
            rows = pl.ds(r, 192)
            for head in range(2):
                lane = head * 128
                query = gg[x, core, :, lane : lane + 128]
                grad = gg[x, core, :, lane + 512 : lane + 640]
                keys = kv[block, rows, lane : lane + 128]
                values = kv[block, rows, lane + 256 : lane + 384]
                probs = probabilities(query, keys, block, chunk)
                probs_low = probs.astype(bf16)
                grad_probs = lax.dot_general(grad, values, TURNED, preferred_element_type=f32)
                inner = jnp.sum(probs * grad_probs, axis=-1, keepdims=True)
                grad_scores = (probs * (grad_probs - inner)).astype(bf16)
                grad_query = jnp.dot(grad_scores, keys, preferred_element_type=f32) * SCALE
                act[x, core, :, lane : lane + 128] = grad_query.astype(bf16)
                grad_keys = lax.dot_general(grad_scores, query, LEFT_TURNED, preferred_element_type=f32)
                grad_values = lax.dot_general(probs_low, grad, LEFT_TURNED, preferred_element_type=f32)
                for start, value in ((lane, grad_keys * SCALE), (lane + 256, grad_values)):
                    tmp[chunk, :, start : start + 128] += value[:128]
                    tmp[chunk + 1, 0:64, start : start + 128] += value[128:]
            return 0

        chunk_body(0, 0)
        tail_out[block] = tmp[0, 0:WINDOW].astype(bf16)
        to_y = jnp.where(block == 0, (p.y + 4 - first) % 4, p.y)
        slot = jnp.where(block == 0, first, 1 - first)
        tails.append(links.send(tail_out.at[block], tail_in.at[slot], p.at(y=to_y, z=(p.z + 3) % 4)))
        lax.fori_loop(1, 4, chunk_body, 0)
        last_kv[block] = tmp[4, 0:WINDOW]

        def store(i, _):
            x, core = block * 2 + i // 2, i % 2
            act[x, core, 0:64, 256:] = tmp[i, WINDOW:].astype(bf16)
            act[x, core, 64:128, 256:] = tmp[i + 1, 0:WINDOW].astype(bf16)
            return 0

        lax.fori_loop(0, 4, store, 0)

    pl.semaphore_wait(ready.at[0], 2)
    r_out.launch()
    load_qm.wait()
    g_branch.ready(1)
    g_branch.ready(2)

    grad_mixed(2 * p.xh)
    grad_mixed(2 * p.xh + 1)

    attend_back(p.xh)
    g_branch.share_far()
    r_out.pass_range(0, 1)
    w_gu.start2()
    g_branch.ready(3)
    grad_mixed(2 * (1 - p.xh))
    grad_mixed(2 * (1 - p.xh) + 1)
    attend_back(1 - p.xh)
    r_out.pass_range(1, 2)
    w_gu.start3()
    grads_into(wo, gb, mixed, 256)
    own[...] = gb[2 * p.xh, p.c].astype(f32)
    resid[...] = gb[2 * p.xh + 1, p.c].astype(f32)
    g_branch.sent()
    load_xr = links.local(xr_o, gb)
    for copy in tails:
        copy.wait_recv()
    for block in range(2):
        whole = last_kv[block] + tail_in[block].astype(f32)
        act[2 * block + 1, 1, pl.ds(64, 64), 256:] = whole.astype(bf16)
    w_d.start1()
    w_o = WeightReduce(links, p, wo, in_o, in2_o, fin_o, 128)
    w_o.start0()
    w_gu.start4()
    r_out.pass_range(2, 3)
    r_out.crossed()
    pl.semaphore_wait(ready.at[1], 3)
    again = [links.local(ref, raw) for ref, raw in raws[:3]]
    r_attn = block_reduce(3, partial_of(act, wq, 768), cot)
    r_attn.run(pass_on=False)
    r_out.pass_range(3, 4)
    w_d.start2()
    w_o.start1()
    load_xr.wait()
    grads_into(wq, gb, act, 768)
    w_d.start3()
    w_q = WeightReduce(links, p, wq, in_q, in2_q, fin_q, 384)
    w_q.start0()
    r_attn.pass_range(0, 2)
    w_o.start2()
    r_out.finish()
    r_out.sent()

    def result_rows(i, _):
        tile, r = i // 8, pl.ds((i % 8) * 16, 16)
        nm[2 + tile, 0, r] = r_out.total(tile, r).astype(bf16)
        return 0

    lax.fori_loop(0, 16, result_rows, 0)
    b_out = BlockOut(links, p, nm.at[pl.ds(2, 2), 0], result_o)
    w_d.start4()
    w_q.start1()
    r_attn.pass_range(2, 3)
    w_o.start3()
    r_attn.pass_range(3, 4)
    w_q.start2()
    w_o.start4()
    w_q.start3()
    w_q.start4()
    r_attn.finish()

    for item in (w_gu, w_d, w_q, w_o):
        item.done()

    part_attn, part_mlp = jnp.zeros((64, 1), f32), jnp.zeros((64, 1), f32)
    for copy in again:
        copy.wait()
    for k in range(2):
        for i, raw in enumerate((raw_q, raw_k, raw_v)):
            part_attn += row_dots(raw[:, 256 * k : 256 * k + 256], fin_q[k, :, 256 * i : 256 * i + 256])
        for i, raw in enumerate((raw_g, raw_u)):
            start = 688 * k
            part_mlp += row_dots(raw[:, start : start + 640], fin_gu[k, :, 640 * i : 640 * i + 640])
            tail = slice(1280 + 64 * i, 1328 + 64 * i)
            part_mlp += row_dots(raw[:, start + 640 : start + 688], fin_gu[k, :, tail])
    lane = lax.broadcasted_iota(jnp.int32, (64, 128), 1)
    sums[...] = jnp.where(lane == 0, part_attn, jnp.where(lane == 1, part_mlp, 0.0))
    others = (sibling, beside, p.at(x=2 * p.xh + 1 - p.xl, c=1 - p.c))
    shared = [links.send(sums, sums_in.at[k], device) for k, device in enumerate(others)]
    stored = [
        links.local(fin, out)
        for fin, out in ((fin_gu, fin_gu_o), (fin_d, fin_d_o), (fin_q, fin_q_o), (fin_o, fin_o_o))
    ]
    def input_rows(i, _):
        tile, r = i // 8, pl.ds((i % 8) * 16, 16)
        values = hid_pair[tile, r].astype(f32)
        base = jnp.where(tile == 0, own[r], resid[r])
        hid_pair[tile, r] = (base + norm_back(r_attn.total(tile, r), values)).astype(bf16)
        return 0

    lax.fori_loop(0, 16, input_rows, 0)
    b_in = BlockOut(links, p, hid_pair, grad_o)
    for copy in shared:
        copy.wait_recv()
    links.settle(shared)
    sums[...] = (sums[...] + sums_in[0]) + (sums_in[1] + sums_in[2])
    stored.append(links.local(sums, sums_o))
    for copy in stored:
        copy.wait()
    b_out.done()
    b_in.done()
    r_attn.crossed()
    r_attn.sent()
    links.settle()


def block_call(lengths, gain_attn, gain_mlp, weights, hid, cot):
    sds = jax.ShapeDtypeStruct
    group = (4, 2, OWNED)
    vm = pltpu.VMEM
    outs = pl.pallas_call(
        block_kernel,
        out_shape=(
            sds((2, 2, OWNED, 2048), bf16),
            sds((2, 2, OWNED, 2048), bf16),
            sds((2, 64, 1408), bf16),
            sds((2, 64, 768), bf16),
            sds((2, 64, 768), bf16),
            sds((2, 64, 256), bf16),
            sds((64, 128), f32),
            sds(group + (2048,), bf16),
            sds(group + (512,), bf16),
        ),
        in_specs=[pl.BlockSpec(memory_space=pltpu.SMEM)] + [pl.BlockSpec(memory_space=pltpu.VMEM)] * 2 + [ANY] * 9,
        out_specs=[ANY] * 9,
        scratch_shapes=[
            vm((64, 1376), bf16),
            vm((64, 1376), bf16),
            vm((64, 1376), bf16),
            vm((2, 64, 1408), bf16),
            vm((2, 64, 768), bf16),
            vm((2, 64, 768), bf16),
            vm((2, 64, 256), bf16),
            vm((64, 128), f32),
            vm((3, 64, 128), f32),
            vm((4, 2, 4, 64, 768), bf16),
            vm((4, 2, 4, 64, 256), bf16),
            vm((4, 2, 4, 64, 1408), bf16),
            vm((4, 2, 4, 64, 768), bf16),
            vm(group + (2048,), bf16),
            vm(group + (2048,), bf16),
            vm(group + (768,), bf16),
            vm(group + (1408,), bf16),
            vm((2, BLOCK + WINDOW, 512), bf16),
            vm((OWNED, 2048), f32),
            vm((2, OWNED, 2048), bf16),
            vm((OWNED, 2048), f32),
            vm(group + (2048,), bf16),
            vm((2, WINDOW, 512), f32),
            vm((2, WINDOW, 512), bf16),
            vm((2, WINDOW, 512), bf16),
            vm((6, 4, 64, 1408), bf16),
            vm((6, 4, 64, 768), bf16),
            vm((6, 4, 64, 768), bf16),
            vm((6, 4, 64, 256), bf16),
            vm((6, 64, 1408), bf16),
            vm((6, 64, 768), bf16),
            vm((6, 64, 768), bf16),
            vm((6, 64, 256), bf16),
            vm((2, 4, OWNED, WIDE), bf16),
            vm((PIECES, 6, 64, WIDE), bf16),
            vm((5, OWNED, WIDE), f32),
            vm((PIECES, 4, OWNED, WIDE), bf16),
            vm((PIECES, 6, 64, WIDE), bf16),
            pltpu.SemaphoreType.DMA((220,)),
            pltpu.SemaphoreType.DMA((220,)),
            pltpu.SemaphoreType.DMA((32,)),
            pltpu.SemaphoreType.DMA((20 * PIECES,)),
            pltpu.SemaphoreType.DMA((20 * PIECES,)),
            pltpu.SemaphoreType.REGULAR((2,)),
        ],
        compiler_params=pltpu.CompilerParams(
            collective_id=0, has_side_effects=True, vmem_limit_bytes=60 * 2**20
        ),
        name="block",
    )(lengths, gain_attn, gain_mlp, *weights, hid.reshape(2, 2, OWNED, 2048), cot.reshape(2, 2, OWNED, 2048))
    return outs[:7]


def per_device(
    hidden_in,
    norm_gain_attn,
    w_query,
    w_key,
    w_value,
    w_out,
    norm_gain_mlp,
    w_gate,
    w_up,
    w_down,
    lengths,
    cotangent,
):
    outs = block_call(
        lengths,
        norm_gain_attn,
        norm_gain_mlp,
        (w_query, w_key, w_value, w_out.T, w_gate, w_up, w_down.T),
        hidden_in,
        cotangent,
    )
    return final_call(*outs, norm_gain_attn, norm_gain_mlp)


def solution(mesh):
    mesh = Mesh(mesh.devices.reshape(4, 2, 4, 2, 2), AXES)
    seq, head = ("y", "xh", "z"), ("xl", "c")
    rows, cols, flat, turned = P(seq, None), P(seq, head), P(seq), P(head, seq)
    return jax.shard_map(
        per_device,
        mesh=mesh,
        in_specs=(rows, flat, cols, cols, cols, turned, flat, cols, cols, turned, P(), rows),
        out_specs=(rows, rows, flat, cols, cols, cols, turned, flat, cols, cols, turned),
        check_vma=False,
    )
```

```python
import jax
import jax.numpy as jnp
from jax import lax
from jax.experimental import pallas as pl
from jax.experimental.pallas import tpu as pltpu
from jax.sharding import Mesh, PartitionSpec as P

HEAD_DIM = 128
WINDOW = 64
BLOCK = 512
OWNED = 128
PIECES = 4
WIDE = 2048 // PIECES
AXES = ("y", "xh", "z", "xl", "c")

epsilon = 1e-05
masked_score = -1e30
f32 = jnp.float32
bf16 = jnp.bfloat16


MESH = pl.DeviceIdType.MESH
SCALE = HEAD_DIM ** (-0.5)
ANY = pl.BlockSpec(memory_space=pl.ANY)
TURNED = (((1,), (1,)), ((), ()))
LEFT_TURNED = (((0,), (0,)), ((), ()))


class Place:
    def __init__(self):
        self.y, self.z, self.c = lax.axis_index("y"), lax.axis_index("z"), lax.axis_index("c")
        self.xh, self.xl = lax.axis_index("xh"), lax.axis_index("xl")
        self.x = self.xh * 2 + self.xl
        self.q = self.xl * 2 + self.c

    def at(self, y=None, x=None, z=None, c=None):
        y = self.y if y is None else y
        x = self.x if x is None else x
        z = self.z if z is None else z
        c = self.c if c is None else c
        return (y, x // 2, z, x % 2, c)


class Links:
    def __init__(self, send_sems, recv_sems, local_sems):
        self.send_sems, self.recv_sems, self.local_sems = send_sems, recv_sems, local_sems
        self.count, self.local_count, self.started = 0, 0, []

    def send(self, src, dst, device):
        copy = self.prepare(src, dst, device)
        copy.start()
        return copy

    def prepare(self, src, dst, device):
        copy = pltpu.make_async_remote_copy(
            src_ref=src,
            dst_ref=dst,
            send_sem=self.send_sems.at[self.count],
            recv_sem=self.recv_sems.at[self.count],
            device_id=device,
            device_id_type=MESH,
        )
        self.count += 1
        self.started.append(copy)
        return copy

    def local(self, src, dst):
        copy = pltpu.make_async_copy(src, dst, self.local_sems.at[self.local_count])
        self.local_count += 1
        copy.start()
        return copy

    def settle(self, copies=None):
        copies = self.started if copies is None else copies
        for copy in copies:
            copy.wait_send()
        self.started = [copy for copy in self.started if not any(copy is other for other in copies)]


class WeightGather:
    def __init__(self, links, place, pack, whole, cut, direct=False):
        self.links, self.place, self.whole, self.direct = links, place, whole, direct
        cols = whole.shape[-1]
        self.parts = (pl.ds(0, cut), pl.ds(cut, cols - cut))
        self.swap = links.send(
            pack(1 - place.xh), whole.at[place.y, place.xh, place.z], place.at(x=(place.x + 2) % 4)
        )
        self.mine = links.local(pack(place.xh), whole.at[place.y, place.xh, place.z])

    def send(self, ref, device):
        return self.links.send(ref, ref, device)

    def near(self, view_z, view_y):
        p = self.place
        first, second = self.parts
        zs = (p.at(z=(p.z + 1) % 4), p.at(z=(p.z + 3) % 4))
        ys = (p.at(y=(p.y + 1) % 4), p.at(y=(p.y + 3) % 4))
        (ref_z, axis_z), (ref_y, axis_y) = view_z, view_y
        to = {"z": zs, "y": ys}
        self.got = [
            self.send(ref_z, to[axis_z][0]),
            self.send(ref_y, to[axis_y][0]),
            self.send(ref_z, to[axis_z][1]),
            self.send(ref_y, to[axis_y][1]),
        ]

    def wait(self):
        for copy in self.got:
            copy.wait_recv()

    def start0(self):
        p, w = self.place, self.whole
        first, second = self.parts
        self.swap.wait_recv()
        self.mine.wait()
        self.near(
            (w.at[p.y, :, p.z, :, first], "z"),
            (w.at[p.y, :, p.z, :, second], "y"),
        )
        if self.direct:
            self.got += [
                self.send(w.at[p.y, :, p.z, :, first], p.at(z=(p.z + 2) % 4)),
                self.send(w.at[p.y, :, p.z, :, second], p.at(y=(p.y + 2) % 4)),
            ]

    def start1(self):
        if self.direct:
            return
        p, w = self.place, self.whole
        first, second = self.parts
        self.wait()
        zn, zp, yn, yp = (p.z + 1) % 4, (p.z + 3) % 4, (p.y + 1) % 4, (p.y + 3) % 4
        self.got = [
            self.send(w.at[p.y, 0, zp, :, first], p.at(z=zn)),
            self.send(w.at[yp, 0, p.z, :, second], p.at(y=yn)),
            self.send(w.at[p.y, 1, zn, :, first], p.at(z=zp)),
            self.send(w.at[yn, 1, p.z, :, second], p.at(y=yp)),
        ]

    def start2(self):
        p, w = self.place, self.whole
        first, second = self.parts
        self.wait()
        self.near(
            (w.at[:, :, p.z, :, second], "z"),
            (w.at[p.y, :, :, :, first], "y"),
        )

    def start3(self):
        p, w = self.place, self.whole
        first, second = self.parts
        self.wait()
        zn, zp, yn, yp = (p.z + 1) % 4, (p.z + 3) % 4, (p.y + 1) % 4, (p.y + 3) % 4
        self.got = [
            self.send(w.at[yp, 0, :, :, first], p.at(y=yn)),
            self.send(w.at[:, 0, zp, :, second], p.at(z=zn)),
            self.send(w.at[yn, 1, :, :, first], p.at(y=yp)),
            self.send(w.at[:, 1, zn, :, second], p.at(z=zp)),
        ]

    def done(self):
        self.wait()


def greet(place):
    p = place
    barrier = pltpu.get_barrier_semaphore()
    partners = (
        p.at(z=(p.z + 1) % 4),
        p.at(z=(p.z + 3) % 4),
        p.at(y=(p.y + 1) % 4),
        p.at(y=(p.y + 3) % 4),
        p.at(x=(p.x + 1) % 4),
        p.at(x=(p.x + 3) % 4),
        p.at(x=(p.x + 2) % 4),
        p.at(c=1 - p.c),
        p.at(y=(p.y + 2) % 4),
        p.at(z=(p.z + 2) % 4),
        p.at(x=2 * p.xh + 1 - p.xl, c=1 - p.c),
    )
    for device in partners:
        pl.semaphore_signal(barrier, inc=1, device_id=device, device_id_type=MESH)

    @pl.when(p.z == 3)
    def _():
        pl.semaphore_signal(barrier, inc=1, device_id=p.at(y=(p.y + 1) % 4, z=0 * p.z), device_id_type=MESH)

    @pl.when(p.z == 0)
    def _():
        pl.semaphore_signal(barrier, inc=1, device_id=p.at(y=(p.y + 3) % 4, z=0 * p.z + 3), device_id_type=MESH)

    pl.semaphore_wait(barrier, 11 + jnp.where((p.z == 3) | (p.z == 0), 1, 0))


def unit_scale(values):
    return values * lax.rsqrt(jnp.mean(values * values, axis=-1, keepdims=True) + epsilon)


class WeightReduce:
    def __init__(self, links, place, total, first_in, second_in, out, cut):
        self.links, self.place, self.total, self.out = links, place, total, out
        self.copies = []
        self.one, self.two = first_in, second_in
        cols = total.shape[-1]
        self.cols = cols
        self.parts = (pl.ds(0, cut), pl.ds(cut, cols - cut))
        p = place
        self.yn, self.yp, self.yf = (p.y + 1) % 4, (p.y + 3) % 4, (p.y + 2) % 4
        self.zn, self.zp, self.zf = (p.z + 1) % 4, (p.z + 3) % 4, (p.z + 2) % 4
        self.next_y, self.prev_y = p.at(y=self.yn), p.at(y=self.yp)
        self.next_z, self.prev_z = p.at(z=self.zn), p.at(z=self.zp)

    def send(self, src, dst, device):
        copy = self.links.send(src, dst, device)
        self.copies.append(copy)
        return copy

    def start0(self):
        a, b = self.parts
        t, one, send = self.total, self.one, self.send
        self.far = [
            send(t.at[self.yf, 0, :, :, a], one.at[0, :, :, a], self.next_y),
            send(t.at[:, 0, self.zf, :, b], one.at[0, :, :, b], self.next_z),
            send(t.at[self.yf, 1, :, :, a], one.at[2, :, :, a], self.prev_y),
            send(t.at[:, 1, self.zf, :, b], one.at[2, :, :, b], self.prev_z),
        ]
        self.near = [
            send(t.at[self.yn, 1, :, :, a], one.at[1, :, :, a], self.next_y),
            send(t.at[:, 1, self.zn, :, b], one.at[1, :, :, b], self.next_z),
            send(t.at[self.yp, 0, :, :, a], one.at[3, :, :, a], self.prev_y),
            send(t.at[:, 0, self.zp, :, b], one.at[3, :, :, b], self.prev_z),
        ]

    def add(self, target, sources, rows):
        def body(i, _):
            ref = target(i)
            value = ref[...].astype(f32)
            for source in sources:
                value = value + source(i)[...].astype(f32)
            ref[...] = value.astype(bf16)
            return 0

        lax.fori_loop(0, rows, body, 0)

    def start1(self):
        a, b = self.parts
        t, one, send = self.total, self.one, self.send
        yn, yp, zn, zp = self.yn, self.yp, self.zn, self.zp
        self.sums = []
        self.far[0].wait_recv()
        self.add(lambda i: t.at[yn, 0, i, :, a], [lambda i: one.at[0, i, :, a]], 4)
        self.sums.append(send(t.at[yn, 0, :, :, a], one.at[4, :, :, a], self.next_y))
        self.far[1].wait_recv()
        self.add(lambda i: t.at[i, 0, zn, :, b], [lambda i: one.at[0, i, :, b]], 4)
        self.sums.append(send(t.at[:, 0, zn, :, b], one.at[4, :, :, b], self.next_z))
        self.far[2].wait_recv()
        self.add(lambda i: t.at[yp, 1, i, :, a], [lambda i: one.at[2, i, :, a]], 4)
        self.sums.append(send(t.at[yp, 1, :, :, a], one.at[5, :, :, a], self.prev_y))
        self.far[3].wait_recv()
        self.add(lambda i: t.at[i, 1, zp, :, b], [lambda i: one.at[2, i, :, b]], 4)
        self.sums.append(send(t.at[:, 1, zp, :, b], one.at[5, :, :, b], self.prev_z))

    def start2(self):
        a, b = self.parts
        t, one, two, send = self.total, self.one, self.two, self.send
        p = self.place
        for copy in self.near + self.sums:
            copy.wait_recv()
        self.add(lambda i: t.at[p.y, 0, i, :, a], [lambda i: one.at[3, i, :, a], lambda i: one.at[4, i, :, a]], 4)
        self.add(lambda i: t.at[p.y, 1, i, :, a], [lambda i: one.at[1, i, :, a], lambda i: one.at[5, i, :, a]], 4)
        self.add(lambda i: t.at[i, 0, p.z, :, b], [lambda i: one.at[3, i, :, b], lambda i: one.at[4, i, :, b]], 4)
        self.add(lambda i: t.at[i, 1, p.z, :, b], [lambda i: one.at[1, i, :, b], lambda i: one.at[5, i, :, b]], 4)
        sends = (
            (t.at[p.y, :, self.zn, :, a], 0, a, self.next_z),
            (t.at[self.yn, :, p.z, :, b], 0, b, self.next_y),
            (t.at[p.y, :, self.zp, :, a], 2, a, self.prev_z),
            (t.at[self.yp, :, p.z, :, b], 2, b, self.prev_y),
            (t.at[p.y, :, self.zf, :, a], 4, a, p.at(z=self.zf)),
            (t.at[self.yf, :, p.z, :, b], 4, b, p.at(y=self.yf)),
        )
        self.sums = [send(src, two.at[pl.ds(slot, 2), :, lanes], device) for src, slot, lanes, device in sends]

    def plus(self, target, *sources):
        value = target[...].astype(f32)
        for source in sources:
            value = value + source[...].astype(f32)
        target[...] = value.astype(bf16)

    def start3(self):
        p, two = self.place, self.two
        for copy in self.sums:
            copy.wait_recv()
        for half in range(2):
            self.plus(two.at[half], two.at[2 + half], two.at[4 + half], self.total.at[p.y, half, p.z])
        self.swap = self.links.send(two.at[1 - p.xh], self.out.at[p.xh], p.at(x=(p.x + 2) % 4))
        self.mine = self.links.local(two.at[p.xh], self.out.at[p.xh])

    def sent(self):
        self.links.settle(self.copies)

    def done(self):
        self.swap.wait_recv()
        self.mine.wait()


class GroupReduce:
    def __init__(self, place, partial, bufs, sems):
        self.place, self.partial = place, partial
        self.send_c, self.recv_c, self.tmp, self.snd, self.rcv, self.own = bufs
        self.send_sems, self.recv_sems = sems

    def copy(self, src, dst, index, device):
        return pltpu.make_async_remote_copy(
            src_ref=src,
            dst_ref=dst,
            send_sem=self.send_sems.at[index],
            recv_sem=self.recv_sems.at[index],
            device_id=device,
            device_id_type=MESH,
        )

    def crossing(self, n):
        return self.copy(self.send_c.at[n % 2], self.recv_c.at[n], n, self.place.at(c=1 - self.place.c))

    def to_next(self, n):
        pair = pl.ds(0, 2)
        return self.copy(
            self.snd.at[n, pair], self.rcv.at[n, pair], PIECES + n, self.place.at(x=(self.place.x + 1) % 4)
        )

    def to_prev(self, n):
        pair = pl.ds(2, 2)
        return self.copy(
            self.snd.at[n, pair], self.rcv.at[n, pair], 2 * PIECES + n, self.place.at(x=(self.place.x + 3) % 4)
        )

    def sum_next(self, n):
        return self.copy(
            self.snd.at[n, 4], self.rcv.at[n, 4], 3 * PIECES + n, self.place.at(x=(self.place.x + 1) % 4)
        )

    def sum_prev(self, n):
        return self.copy(
            self.snd.at[n, 5], self.rcv.at[n, 5], 4 * PIECES + n, self.place.at(x=(self.place.x + 3) % 4)
        )

    def sibling_part(self, n):
        part = self.partial(n, 1 - self.place.c)

        @pl.when(n >= 2)
        def _():
            self.crossing(n - 2).wait_send()

        self.send_c[n % 2] = part.astype(bf16).reshape(4, OWNED, WIDE)
        self.crossing(n).start()

    def own_part(self, n, launch):
        p, tmp, snd = self.place, self.tmp, self.snd
        part = self.partial(n, p.c).reshape(4, OWNED, WIDE)
        self.crossing(n).wait_recv()
        tmp[...] = part + self.recv_c[n].astype(f32)
        far, nxt, prev = (p.x + 2) % 4, (p.x + 1) % 4, (p.x + 3) % 4
        low, high = pl.ds(0, 64), pl.ds(64, 64)
        snd[n, 0] = tmp[far, low].astype(bf16)
        snd[n, 1] = tmp[nxt, high].astype(bf16)
        if launch:
            self.to_next(n).start()
        snd[n, 2] = tmp[far, high].astype(bf16)
        snd[n, 3] = tmp[prev, low].astype(bf16)
        if launch:
            self.to_prev(n).start()
        snd[n, 4] = tmp[nxt, low].astype(bf16)
        snd[n, 5] = tmp[prev, high].astype(bf16)
        self.own[:, pl.ds(pl.multiple_of(n * WIDE, WIDE), WIDE)] = tmp[p.x]

    def pass_on(self, n):
        snd, rcv = self.snd, self.rcv
        self.to_next(n).wait_recv()
        snd[n, 4] = (snd[n, 4].astype(f32) + rcv[n, 0].astype(f32)).astype(bf16)
        self.sum_next(n).start()
        self.to_prev(n).wait_recv()
        snd[n, 5] = (snd[n, 5].astype(f32) + rcv[n, 2].astype(f32)).astype(bf16)
        self.sum_prev(n).start()

    def run(self, launch=True, pass_on=True, hooks=()):
        def body(i, _):
            @pl.when(i < PIECES)
            def _():
                self.sibling_part(i)

            @pl.when((i >= 1) & (i < PIECES + 1))
            def _():
                self.own_part(i - 1, launch)

            if pass_on:

                @pl.when(i >= 2)
                def _():
                    self.pass_on(i - 2)

            for step, hook in hooks:
                pl.when(i == step)(hook)
            return 0

        lax.fori_loop(0, PIECES + 2 if pass_on else PIECES + 1, body, 0)

    def launch(self):
        def body(n, _):
            self.to_next(n).start()
            self.to_prev(n).start()
            return 0

        lax.fori_loop(0, PIECES, body, 0)

    def pass_range(self, start, stop):
        def body(n, _):
            self.pass_on(n)
            return 0

        lax.fori_loop(start, stop, body, 0)

    def finish(self):
        def body(n, _):
            lanes = pl.ds(pl.multiple_of(n * WIDE, WIDE), WIDE)
            low, high = pl.ds(0, 64), pl.ds(64, 64)
            rcv, own = self.rcv, self.own
            self.sum_next(n).wait_recv()
            own[low, lanes] = own[low, lanes] + rcv[n, 3].astype(f32) + rcv[n, 4].astype(f32)
            self.sum_prev(n).wait_recv()
            own[high, lanes] = own[high, lanes] + rcv[n, 1].astype(f32) + rcv[n, 5].astype(f32)
            return 0

        lax.fori_loop(0, PIECES, body, 0)

    def sent(self):
        def body(n, _):
            for copy in (self.to_next, self.to_prev, self.sum_next, self.sum_prev):
                copy(n).wait_send()
            return 0

        self.crossing(PIECES - 2).wait_send()
        self.crossing(PIECES - 1).wait_send()

        lax.fori_loop(0, PIECES, body, 0)


class GroupGather:
    def __init__(self, links, place, whole):
        self.links, self.place, self.whole = links, place, whole
        self.low, self.high = pl.ds(0, 64), pl.ds(64, 64)

    def send(self, ref, device):
        return self.links.send(ref, ref, device)

    def start(self):
        p, w = self.place, self.whole
        self.nxt, self.prev, self.far = (p.x + 1) % 4, (p.x + 3) % 4, (p.x + 2) % 4
        self.to_next, self.to_prev = p.at(x=self.nxt), p.at(x=self.prev)
        self.sibling = p.at(c=1 - p.c)
        low, high = w.at[p.x, p.c, self.low], w.at[p.x, p.c, self.high]
        self.first = [self.send(low, self.to_next), self.send(high, self.to_prev)]
        self.second = [self.send(high, self.to_next), self.send(low, self.to_prev)]
        tiles = (p.x, self.prev, self.nxt, self.far)
        self.paired = [self.later(w.at[x, p.c], self.sibling) for x in tiles]
        self.paired[0].start()
        self.third = [
            self.later(w.at[self.prev, p.c, self.low], self.to_next),
            self.later(w.at[self.nxt, p.c, self.high], self.to_prev),
        ]

    def later(self, ref, device):
        return self.links.prepare(ref, ref, device)

    def forward(self):
        for k in range(2):
            self.first[k].wait_recv()
            self.third[k].start()

    def share_near(self):
        for k in range(2):
            self.second[k].wait_recv()
            self.paired[1 + k].start()

    def share_far(self):
        for copy in self.third:
            copy.wait_recv()
        self.paired[3].start()

    def sent(self):
        self.links.settle(self.first + self.second + self.third + self.paired)

    def ready(self, k):
        self.paired[k].wait_recv()


class BlockExchange:
    def __init__(self, links, place, block, whole):
        p = place
        self.place, self.links = p, links
        beside = p.at(x=2 * p.xh + 1 - p.xl)
        sibling = p.at(c=1 - p.c)
        self.near, self.next = 3 - p.x, 2 * (1 - p.xh) + p.xl
        halves = [pl.ds(0, 64), pl.ds(64, 64)]
        self.cross = [links.send(block.at[p.xl, p.c, h], whole.at[p.x, p.c, h], p.at(x=3 - p.x)) for h in halves]
        self.across = [
            links.prepare(whole.at[self.near, p.c, h], whole.at[self.near, p.c, h], beside) for h in halves
        ]
        self.paired = [
            links.prepare(whole.at[x, p.c], whole.at[x, p.c], sibling) for x in (self.near, self.next)
        ]

    def forward(self, k):
        self.cross[k].wait_recv()
        self.across[k].start()

    def share(self):
        self.paired[0].start()

    def share_next(self):
        for copy in self.across:
            copy.wait_recv()
        self.paired[1].start()

    def done(self, k):
        self.paired[k].wait_recv()


class BlockReduce(GroupReduce):
    def __init__(self, place, partial, bufs, sems, extra=None):
        self.place, self.partial, self.extra = place, partial, extra
        self.send_c, self.recv_c, self.tmp, self.moving = bufs
        self.send_sems, self.recv_sems = sems
        self.facing, self.beside = place.at(x=3 - place.x), place.at(x=2 * place.xh + 1 - place.xl)

    def part(self, which, n):
        lanes = pl.ds(pl.multiple_of(n * WIDE, WIDE), WIDE)
        return self.moving.at[pl.ds(2 * (which // 2), 2), which % 2, :, lanes]

    def over(self, n):
        return self.copy(self.part(0, n), self.part(1, n), PIECES + n, self.facing)

    def across(self, n):
        return self.copy(self.part(2, n), self.part(3, n), 2 * PIECES + n, self.beside)

    def own_part(self, n, launch):
        p, tmp = self.place, self.tmp
        part = self.partial(n, p.c).reshape(4, OWNED, WIDE)
        self.crossing(n).wait_recv()
        tmp[...] = part + self.recv_c[n].astype(f32)
        if self.extra is not None:
            lanes = pl.ds(pl.multiple_of(n * WIDE, WIDE), WIDE)
            tmp[p.x] += self.extra[:, lanes]
        self.part(0, n)[...] = tmp[pl.ds(2 * (1 - p.xh), 2)].astype(bf16)
        if launch:
            self.over(n).start()
        self.part(2, n)[...] = tmp[pl.ds(2 * p.xh, 2)].astype(bf16)

    def pass_on(self, n):
        self.over(n).wait_recv()
        mine = self.part(2, n)
        mine[...] = (mine[...].astype(f32) + self.part(1, n)[...].astype(f32)).astype(bf16)
        self.across(n).start()

    def launch(self):
        def body(n, _):
            self.over(n).start()
            return 0

        lax.fori_loop(0, PIECES, body, 0)

    def finish(self):
        def body(n, _):
            self.across(n).wait_recv()
            return 0

        lax.fori_loop(0, PIECES, body, 0)

    def total(self, tile, rows):
        return self.moving[2 + tile, 0, rows].astype(f32) + self.moving[2 + tile, 1, rows].astype(f32)

    def crossed(self):
        self.crossing(PIECES - 2).wait_send()
        self.crossing(PIECES - 1).wait_send()

    def sent(self):
        def body(n, _):
            self.over(n).wait_send()
            self.across(n).wait_send()
            return 0

        lax.fori_loop(0, PIECES, body, 0)


class BlockOut:
    def __init__(self, links, place, rows, out):
        mine = out.at[:, place.c]
        self.local = links.local(rows, mine)
        self.paired = links.send(rows, mine, place.at(c=1 - place.c))

    def done(self):
        self.paired.wait_recv()
        self.local.wait()


def norm_back(e, values):
    r = lax.rsqrt(jnp.mean(values * values, axis=-1, keepdims=True) + epsilon)
    return r * e - values * r**3 * jnp.mean(e * values, axis=-1, keepdims=True)


def column(gain):
    row = gain[...].astype(f32).reshape(1, 64)
    places = [lax.broadcasted_iota(jnp.int32, (64, 64), k) for k in range(2)]
    return jnp.sum(jnp.where(places[0] == places[1], row, 0.0), axis=1, keepdims=True)


def pack_attn(gain, query, key, value, pack):
    for i, ref in enumerate((query, key, value)):
        scaled = (ref[...].astype(f32) * gain).astype(bf16)
        for k in range(2):
            pack(k)[:, 256 * i : 256 * i + 256] = scaled[:, 256 * k : 256 * k + 256]


def pack_out(out, pack):
    for k in range(2):
        pack(k)[...] = out[:, 256 * k : 256 * k + 256]


def pack_ff(gain, gate, up, down, pack_gu, pack_d):
    zeros = jnp.zeros((64, 16), f32)
    for k in range(2):
        start = 688 * k
        tails = []
        for i, ref in enumerate((gate, up)):
            part = ref[:, start : start + 640].astype(f32) * gain
            pack_gu(k)[:, 640 * i : 640 * i + 640] = part.astype(bf16)
            tails += [ref[:, start + 640 : start + 688].astype(f32) * gain, zeros]
        pack_gu(k)[:, 1280:] = jnp.concatenate(tails, axis=1).astype(bf16)
        part = down[:, start : start + 688].astype(f32)
        pack_d(k)[...] = jnp.concatenate([part, jnp.zeros((64, 80), f32)], axis=1).astype(bf16)


def row_dots(weight, grads):
    return jnp.sum(weight.astype(f32) * grads.astype(f32), axis=1, keepdims=True)


def final_kernel(
    result_in, input_in, fin_gu, fin_d, fin_q, fin_o, sums, gain_attn, gain_mlp,
    result, input_grad, g_attn, query, key, value, out, g_mlp, gate, up, down,
    hold, sems,
):
    parts = [(k, i, j) for i in range(2) for j in range(2) for k in range(2)]
    inputs, outputs = (result_in, input_in), (result, input_grad)
    loads = [
        pltpu.make_async_copy(inputs[k].at[i, j], hold.at[k, i, j], sems.at[n]) for n, (k, i, j) in enumerate(parts)
    ]
    stores = [
        pltpu.make_async_copy(hold.at[k, i, j], outputs[k].at[i, j], sems.at[8 + n])
        for n, (k, i, j) in enumerate(parts)
    ]
    for copy in loads:
        copy.start()
    attn, mlp = column(gain_attn), column(gain_mlp)
    for load, store in zip(loads, stores):
        load.wait()
        store.start()
    for i, ref in enumerate((query, key, value)):
        for k in range(2):
            ref[:, 256 * k : 256 * k + 256] = fin_q[k, :, 256 * i : 256 * i + 256].astype(f32) * attn
    for k in range(2):
        out[:, 256 * k : 256 * k + 256] = fin_o[k].astype(f32)
        down[:, 688 * k : 688 * k + 688] = fin_d[k, :, :688].astype(f32)
        tail = fin_gu[k, :, 1280:].astype(f32) * mlp
        for i, ref in enumerate((gate, up)):
            ref[:, 688 * k : 688 * k + 640] = fin_gu[k, :, 640 * i : 640 * i + 640].astype(f32) * mlp
            ref[:, 688 * k + 640 : 688 * k + 688] = tail[:, 64 * i : 64 * i + 48]
    turned = sums[...].T
    g_attn[...] = turned[0:1]
    g_mlp[...] = turned[1:2]
    for copy in stores:
        copy.wait()


def final_call(result, input_grad, fin_gu, fin_d, fin_q, fin_o, sums, gain_attn, gain_mlp):
    sds = jax.ShapeDtypeStruct
    vmem = pl.BlockSpec(memory_space=pltpu.VMEM)
    whole = (2, 2, OWNED, 2048)
    outs = pl.pallas_call(
        final_kernel,
        out_shape=(
            sds(whole, bf16),
            sds(whole, bf16),
            sds((1, 64), f32),
            sds((64, 512), f32),
            sds((64, 512), f32),
            sds((64, 512), f32),
            sds((64, 512), f32),
            sds((1, 64), f32),
            sds((64, 1376), f32),
            sds((64, 1376), f32),
            sds((64, 1376), f32),
        ),
        in_specs=[ANY] * 2 + [vmem] * 7,
        out_specs=[ANY] * 2 + [vmem] * 9,
        scratch_shapes=[pltpu.VMEM((2,) + whole, bf16), pltpu.SemaphoreType.DMA((16,))],
        compiler_params=pltpu.CompilerParams(vmem_limit_bytes=62 * 2**20),
        name="final",
    )(result, input_grad, fin_gu, fin_d, fin_q, fin_o, sums, gain_attn, gain_mlp)
    result, input_grad, g_attn, query, key, value, out, g_mlp, gate, up, down = outs
    return (
        result.reshape(BLOCK, 2048),
        input_grad.reshape(BLOCK, 2048),
        g_attn.reshape(64),
        query,
        key,
        value,
        out.T,
        g_mlp.reshape(64),
        gate,
        up,
        down.T,
    )


def block_kernel(
    lengths, gain_attn, gain_mlp, w_query, w_key, w_value, w_out, w_gate, w_up, w_down, hid, cot_in,
    result_o, grad_o, fin_gu_o, fin_d_o, fin_q_o, fin_o_o, sums_o, xr_o, qm_o,
    raw_g, raw_u, raw_d,
    fin_gu, fin_d, fin_q, fin_o, sums, sums_in,
    wq, wo, gu, d, nm, cot, act, gg, kv, resid, hid_pair, own, gb,
    last_kv, tail_out, tail_in, in_gu, in_d, in_q, in_o, in2_gu, in2_d, in2_q, in2_o,
    send_c, snd, tmp, recv_c, rcv,
    send_sems, recv_sems, local_sems, group_send, group_recv, ready,
):
    p = Place()
    links = Links(send_sems, recv_sems, local_sems)
    sibling = p.at(c=1 - p.c)
    facing, beside = p.at(x=3 - p.x), p.at(x=2 * p.xh + 1 - p.xl)

    def signal(semaphore, devices):
        for device in devices:
            pl.semaphore_signal(semaphore, inc=1, device_id=device, device_id_type=MESH)

    hidg, xr = gb, nm

    own_pair = pl.ds(2 * p.xh, 2)
    own_hidden = links.local(hid, hidg.at[own_pair])
    load_hid = links.local(hid.at[:, p.c], hid_pair)
    own_cot = links.local(cot_in, cot.at[own_pair])
    raw_q, raw_k, raw_v, raw_o = (snd.at[0, k] for k in range(4))
    half = lambda k: pl.ds(64 * k, 64)
    pk_q, pk_d = (lambda k: act.at[0, 0, half(k)]), (lambda k: act.at[0, 1, half(k)])
    pk_o, pk_gu = (lambda k: act.at[1, 0, half(k), pl.ds(0, 256)]), (lambda k: gg.at[0, 0, half(k)])
    raws = ((w_query, raw_q), (w_key, raw_k), (w_value, raw_v), (w_out, raw_o), (w_gate, raw_g), (w_up, raw_u), (w_down, raw_d))
    loads = [links.local(ref, raw) for ref, raw in raws]
    greet(p)
    scale_attn, scale_mlp = column(gain_attn), column(gain_mlp)
    for copy in loads[:4]:
        copy.wait()
    pack_attn(scale_attn, raw_q, raw_k, raw_v, pk_q)
    pack_out(raw_o, pk_o)
    g_q = WeightGather(links, p, pk_q, wq, 384, direct=True)
    g_o = WeightGather(links, p, pk_o, wo, 128, direct=True)
    e_hid = BlockExchange(links, p, hid, hidg)
    for copy in loads[4:]:
        copy.wait()
    pack_ff(scale_mlp, raw_g, raw_u, raw_d, pk_gu, pk_d)
    g_q.start0()
    g_o.start0()
    def norm_rows(tile, core):
        def body(i, _):
            r = pl.ds(i * 32, 32)
            xr[tile, core, r] = unit_scale(hidg[tile, core, r].astype(f32)).astype(bf16)
            return 0

        lax.fori_loop(0, 4, body, 0)

    def norm_own(i, _):
        norm_rows(2 * p.xh + i // 2, i % 2)
        return 0

    own_hidden.wait()
    lax.fori_loop(0, 4, norm_own, 0)
    g_q.start2()
    e_hid.forward(0)
    g_gu = WeightGather(links, p, pk_gu, gu, 768)
    g_d = WeightGather(links, p, pk_d, d, 384)
    e_hid.forward(1)
    e_hid.share()
    e_cot = BlockExchange(links, p, cot_in, cot)
    norm_rows(e_hid.near, p.c)
    g_q.start3()
    g_o.start2()
    g_gu.start0()
    g_d.start0()
    e_hid.done(0)
    norm_rows(e_hid.near, 1 - p.c)
    g_q.done()

    links.settle([g_q.swap, g_o.swap, g_gu.swap, g_d.swap])

    def project(t):
        w = wq[...].reshape(2048, 768)
        out = jnp.dot(xr[t].reshape(256, 2048), w, preferred_element_type=f32).astype(bf16)
        gg[t, :, :, 0:256] = out[:, :256].reshape(2, OWNED, 256)
        kv[t // 2, pl.ds((t % 2) * 256 + WINDOW, 256)] = out[:, 256:]

    def project_three(i, _):
        project(jnp.where(i < 2, 2 * p.xh + i, e_hid.near))
        return 0

    lax.fori_loop(0, 3, project_three, 0)
    g_o.start3()
    e_hid.share_next()
    norm_rows(e_hid.next, p.c)
    e_cot.forward(0)
    e_hid.done(1)
    norm_rows(e_hid.next, 1 - p.c)
    xr_spill = links.local(xr, xr_o)
    project(e_hid.next)

    tails = []
    last = jnp.where(p.z == 3, 1, 0)
    for block in range(2):
        to_y = p.y if block == 0 else (p.y + last) % 4
        slot = last if block == 0 else 1 - last
        tails.append(
            links.send(
                kv.at[block, pl.ds(BLOCK, WINDOW)],
                kv.at[slot, pl.ds(0, WINDOW)],
                p.at(y=to_y, z=(p.z + 1) % 4),
            )
        )
    end0 = lengths[0]
    end1 = end0 + lengths[1]

    def masked(scores, block, chunk):
        start = (p.y * 8 + block * 4 + p.z) * BLOCK + chunk * 128
        query = start + lax.broadcasted_iota(jnp.int32, (128, 192), 0)
        key = start - WINDOW + lax.broadcasted_iota(jnp.int32, (128, 192), 1)
        seen = (key <= query) & (key > query - WINDOW) & (key >= 0)
        for end in (end0, end1):
            seen = seen & ((key >= end) | (query < end))
        return jnp.where(seen, scores, masked_score)

    def probabilities(query, keys, block, chunk):
        scores = lax.dot_general(query, keys, TURNED, preferred_element_type=f32) * SCALE
        scores = masked(scores, block, chunk)
        expo = jnp.exp(scores - jnp.max(scores, axis=-1, keepdims=True))
        return expo / jnp.sum(expo, axis=-1, keepdims=True)

    def attend(block, chunk):
        x, core = block * 2 + chunk // 2, chunk % 2
        r = pl.multiple_of(chunk * 128, 128)
        for head in range(2):
            lane = head * 128
            query = gg[x, core, :, lane : lane + 128]
            keys = kv[block, pl.ds(r, 192), lane : lane + 128]
            values = kv[block, pl.ds(r, 192), lane + 256 : lane + 384]
            probs = probabilities(query, keys, block, chunk).astype(bf16)
            out = jnp.dot(probs, values, preferred_element_type=f32)
            gg[x, core, :, lane + 256 : lane + 384] = out.astype(bf16)

    def inner(i, _):
        attend(i // 3, i % 3 + 1)
        return 0

    e_cot.forward(1)
    e_cot.share()
    g_gu.start1()
    g_d.start1()
    lax.fori_loop(0, 6, inner, 0)
    g_d.start2()
    e_cot.share_next()
    for copy in tails:
        copy.wait_recv()

    def first_chunk(i, _):
        attend(i, 0)
        return 0

    lax.fori_loop(0, 2, first_chunk, 0)
    mixed = gg.at[:, :, :, pl.ds(256, 256)]
    g_gu.start2()
    g_o.done()
    xr_spill.wait()

    def partial_of(left, right, width, start=0):
        def partial(n, core):
            return lax.dot_general(
                left[:, core, :, start : start + width].reshape(512, width),
                right[n].reshape(WIDE, width),
                TURNED,
                preferred_element_type=f32,
            )

        return partial

    def group_reduce(k, partial):
        span = pl.ds(5 * PIECES * k, 5 * PIECES)
        return GroupReduce(
            p, partial, (send_c, recv_c, tmp.at[pl.ds(0, 4)], snd, rcv, own), (group_send.at[span], group_recv.at[span])
        )

    r_branch = group_reduce(0, partial_of(gg, wo, 256, 256))
    r_branch.run(pass_on=False)
    r_branch.pass_range(0, 3)
    g_d.start3()
    r_branch.pass_range(3, 4)
    load_hid.wait()
    r_branch.finish()

    def resid_rows(i, _):
        r = pl.ds(i * 16, 16)
        total = hid_pair[p.xl, r].astype(f32) + own[r]
        resid[r] = total
        nm[p.x, p.c, r] = unit_scale(total).astype(bf16)
        return 0

    lax.fori_loop(0, OWNED // 16, resid_rows, 0)
    g_nm = GroupGather(links, p, nm)
    g_nm.start()
    g_gu.start3()
    q_spill = links.local(gg.at[:, :, :, pl.ds(0, 512)], qm_o)
    own_cot.wait()
    for k in range(2):
        e_cot.done(k)
    g_d.done()

    def grad_activated(t, _):
        out = jnp.dot(cot[t].reshape(256, 2048), d[...].reshape(2048, 768), preferred_element_type=f32)
        act[t] = out.astype(bf16).reshape(2, OWNED, 768)
        return 0

    lax.fori_loop(0, 4, grad_activated, 0)
    q_spill.wait()
    g_nm.forward()
    g_gu.done()
    g_nm.ready(0)

    def feed(k, _):
        @pl.when(k == 1)
        def _():
            g_nm.share_near()
            g_nm.ready(1)

        @pl.when(k == 2)
        def _():
            g_nm.ready(2)

        @pl.when(k == 3)
        def _():
            g_nm.share_far()
            g_nm.ready(3)

        t = (p.x + jnp.where(k == 0, 0, jnp.where(k == 1, 3, k - 1))) % 4
        part = jnp.dot(nm[t].reshape(256, 2048), gu[...].reshape(2048, 1408), preferred_element_type=f32)
        back = act[t].reshape(256, 768).astype(f32)
        tail = part[:, 1280:]
        flipped = pltpu.roll(tail, 64, 1)
        lane = lax.broadcasted_iota(jnp.int32, (256, 128), 1)
        for lanes, gate, up in (
            (slice(0, 640), part[:, :640], part[:, 640:1280]),
            (slice(640, 768), tail, flipped),
        ):
            sig = 1 / (1 + jnp.exp(-gate))
            silu = gate * sig
            grad_act = back[:, lanes]
            act[t, :, :, lanes] = (silu * up).astype(bf16).reshape(2, OWNED, -1)
            grad_gate = grad_act * up * sig * (1 + gate * (1 - sig))
            grad_up = grad_act * silu
            if lanes.start == 0:
                gg[t, :, :, :640] = grad_gate.astype(bf16).reshape(2, OWNED, 640)
                gg[t, :, :, 640:1280] = grad_up.astype(bf16).reshape(2, OWNED, 640)
            else:
                both = jnp.where(lane < 64, grad_gate, pltpu.roll(grad_up, 64, 1))
                gg[t, :, :, 1280:] = both.astype(bf16).reshape(2, OWNED, 128)
        return 0

    lax.fori_loop(0, 4, feed, 0)

    r_branch.sent()
    links.settle()
    r_mlp = group_reduce(1, partial_of(gg, gu, 1408))
    r_mlp.run(pass_on=False)

    def grads_into(out, left, right, width, reduce=None):
        def body(n, _):
            lanes = pl.ds(pl.multiple_of(n * 256, 256), 256)
            part = lax.dot_general(
                left[:, :, :, lanes].reshape(1024, 256),
                right[...].reshape(1024, width),
                LEFT_TURNED,
                preferred_element_type=f32,
            )
            out[n // 2, n % 2] = part.astype(bf16).reshape(4, 64, width)
            if reduce is not None:

                @pl.when(n % 2 == 0)
                def _():
                    reduce.pass_on(n // 2)

            return 0

        lax.fori_loop(0, 8, body, 0)

    grads_into(gu, nm, gg, 1408, r_mlp)
    w_gu = WeightReduce(links, p, gu, in_gu, in2_gu, fin_gu, 768)
    w_gu.start0()
    signal(ready.at[0], (facing, beside))
    load_qm = links.local(qm_o, gg.at[:, :, :, pl.ds(0, 512)])
    r_mlp.finish()

    def grad_rows(i, _):
        r = pl.ds(i * 16, 16)
        grad = cot[p.x, p.c, r].astype(f32) + norm_back(own[r], resid[r])
        gb[p.x, p.c, r] = grad.astype(bf16)
        return 0

    lax.fori_loop(0, OWNED // 16, grad_rows, 0)
    g_branch = GroupGather(links, p, gb)
    g_branch.start()
    r_mlp.sent()
    g_branch.ready(0)

    def block_reduce(k, partial, moving, extra=None):
        span = pl.ds(5 * PIECES * k, 5 * PIECES)
        sems = (group_send.at[span], group_recv.at[span])
        return BlockReduce(p, partial, (send_c, recv_c, tmp.at[pl.ds(0, 4)], moving), sems, extra)

    r_out = block_reduce(2, partial_of(act, d, 768), nm, resid)
    r_out.run(launch=False, pass_on=False)
    g_branch.forward()
    w_gu.start1()
    grads_into(d, cot, act, 768)
    signal(ready.at[1], (facing, beside, sibling))
    w_d = WeightReduce(links, p, d, in_d, in2_d, fin_d, 384)
    w_d.start0()
    g_branch.share_near()

    def grad_mixed(t):
        out = jnp.dot(gb[t].reshape(256, 2048), wo[...].reshape(2048, 256), preferred_element_type=f32)
        gg[t, :, :, 512:768] = out.astype(bf16).reshape(2, OWNED, 256)

    first = jnp.where(p.z == 0, 1, 0)
    tails = []

    def attend_back(block):
        tmp[...] = jnp.zeros_like(tmp)

        def chunk_body(chunk, _):
            x, core = block * 2 + chunk // 2, chunk % 2
            r = pl.multiple_of(chunk * 128, 128)
            rows = pl.ds(r, 192)
            for head in range(2):
                lane = head * 128
                query = gg[x, core, :, lane : lane + 128]
                grad = gg[x, core, :, lane + 512 : lane + 640]
                keys = kv[block, rows, lane : lane + 128]
                values = kv[block, rows, lane + 256 : lane + 384]
                probs = probabilities(query, keys, block, chunk)
                probs_low = probs.astype(bf16)
                grad_probs = lax.dot_general(grad, values, TURNED, preferred_element_type=f32)
                inner = jnp.sum(probs * grad_probs, axis=-1, keepdims=True)
                grad_scores = (probs * (grad_probs - inner)).astype(bf16)
                grad_query = jnp.dot(grad_scores, keys, preferred_element_type=f32) * SCALE
                act[x, core, :, lane : lane + 128] = grad_query.astype(bf16)
                grad_keys = lax.dot_general(grad_scores, query, LEFT_TURNED, preferred_element_type=f32)
                grad_values = lax.dot_general(probs_low, grad, LEFT_TURNED, preferred_element_type=f32)
                for start, value in ((lane, grad_keys * SCALE), (lane + 256, grad_values)):
                    tmp[chunk, :, start : start + 128] += value[:128]
                    tmp[chunk + 1, 0:64, start : start + 128] += value[128:]
            return 0

        chunk_body(0, 0)
        tail_out[block] = tmp[0, 0:WINDOW].astype(bf16)
        to_y = jnp.where(block == 0, (p.y + 4 - first) % 4, p.y)
        slot = jnp.where(block == 0, first, 1 - first)
        tails.append(links.send(tail_out.at[block], tail_in.at[slot], p.at(y=to_y, z=(p.z + 3) % 4)))
        lax.fori_loop(1, 4, chunk_body, 0)
        last_kv[block] = tmp[4, 0:WINDOW]

        def store(i, _):
            x, core = block * 2 + i // 2, i % 2
            act[x, core, 0:64, 256:] = tmp[i, WINDOW:].astype(bf16)
            act[x, core, 64:128, 256:] = tmp[i + 1, 0:WINDOW].astype(bf16)
            return 0

        lax.fori_loop(0, 4, store, 0)

    pl.semaphore_wait(ready.at[0], 2)
    r_out.launch()
    load_qm.wait()
    g_branch.ready(1)
    g_branch.ready(2)

    grad_mixed(2 * p.xh)
    grad_mixed(2 * p.xh + 1)

    attend_back(p.xh)
    g_branch.share_far()
    r_out.pass_range(0, 1)
    w_gu.start2()
    g_branch.ready(3)
    grad_mixed(2 * (1 - p.xh))
    grad_mixed(2 * (1 - p.xh) + 1)
    attend_back(1 - p.xh)
    r_out.pass_range(1, 2)
    grads_into(wo, gb, mixed, 256)
    own[...] = gb[2 * p.xh, p.c].astype(f32)
    resid[...] = gb[2 * p.xh + 1, p.c].astype(f32)
    g_branch.sent()
    load_xr = links.local(xr_o, gb)
    for copy in tails:
        copy.wait_recv()
    for block in range(2):
        whole = last_kv[block] + tail_in[block].astype(f32)
        act[2 * block + 1, 1, pl.ds(64, 64), 256:] = whole.astype(bf16)
    w_d.start1()
    w_o = WeightReduce(links, p, wo, in_o, in2_o, fin_o, 128)
    w_o.start0()
    w_gu.start3()
    r_out.pass_range(2, 3)
    r_out.crossed()
    pl.semaphore_wait(ready.at[1], 3)
    again = [links.local(ref, raw) for ref, raw in raws[:3]]
    r_attn = block_reduce(3, partial_of(act, wq, 768), cot)
    r_attn.run(pass_on=False)
    r_out.pass_range(3, 4)
    w_d.start2()
    w_o.start1()
    load_xr.wait()
    grads_into(wq, gb, act, 768)
    w_q = WeightReduce(links, p, wq, in_q, in2_q, fin_q, 384)
    w_q.start0()
    r_attn.pass_range(0, 2)
    w_o.start2()
    r_out.finish()
    r_out.sent()

    def result_rows(i, _):
        tile, r = i // 8, pl.ds((i % 8) * 16, 16)
        nm[2 + tile, 0, r] = r_out.total(tile, r).astype(bf16)
        return 0

    lax.fori_loop(0, 16, result_rows, 0)
    b_out = BlockOut(links, p, nm.at[pl.ds(2, 2), 0], result_o)
    w_d.start3()
    w_q.start1()
    r_attn.pass_range(2, 3)
    w_o.start3()
    w_q.start2()
    r_attn.pass_range(3, 4)
    w_q.start3()
    r_attn.finish()

    for item in (w_gu, w_d, w_q, w_o):
        item.done()

    part_attn, part_mlp = jnp.zeros((64, 1), f32), jnp.zeros((64, 1), f32)
    for copy in again:
        copy.wait()
    for k in range(2):
        for i, raw in enumerate((raw_q, raw_k, raw_v)):
            part_attn += row_dots(raw[:, 256 * k : 256 * k + 256], fin_q[k, :, 256 * i : 256 * i + 256])
        for i, raw in enumerate((raw_g, raw_u)):
            start = 688 * k
            part_mlp += row_dots(raw[:, start : start + 640], fin_gu[k, :, 640 * i : 640 * i + 640])
            tail = slice(1280 + 64 * i, 1328 + 64 * i)
            part_mlp += row_dots(raw[:, start + 640 : start + 688], fin_gu[k, :, tail])
    lane = lax.broadcasted_iota(jnp.int32, (64, 128), 1)
    sums[...] = jnp.where(lane == 0, part_attn, jnp.where(lane == 1, part_mlp, 0.0))
    others = (sibling, beside, p.at(x=2 * p.xh + 1 - p.xl, c=1 - p.c))
    shared = [links.send(sums, sums_in.at[k], device) for k, device in enumerate(others)]
    stored = [
        links.local(fin, out)
        for fin, out in ((fin_gu, fin_gu_o), (fin_d, fin_d_o), (fin_q, fin_q_o), (fin_o, fin_o_o))
    ]
    def input_rows(i, _):
        tile, r = i // 8, pl.ds((i % 8) * 16, 16)
        values = hid_pair[tile, r].astype(f32)
        base = jnp.where(tile == 0, own[r], resid[r])
        hid_pair[tile, r] = (base + norm_back(r_attn.total(tile, r), values)).astype(bf16)
        return 0

    lax.fori_loop(0, 16, input_rows, 0)
    b_in = BlockOut(links, p, hid_pair, grad_o)
    for copy in shared:
        copy.wait_recv()
    links.settle(shared)
    sums[...] = (sums[...] + sums_in[0]) + (sums_in[1] + sums_in[2])
    stored.append(links.local(sums, sums_o))
    for copy in stored:
        copy.wait()
    b_out.done()
    b_in.done()
    r_attn.crossed()
    r_attn.sent()
    links.settle()


def block_call(lengths, gain_attn, gain_mlp, weights, hid, cot):
    sds = jax.ShapeDtypeStruct
    group = (4, 2, OWNED)
    vm = pltpu.VMEM
    outs = pl.pallas_call(
        block_kernel,
        out_shape=(
            sds((2, 2, OWNED, 2048), bf16),
            sds((2, 2, OWNED, 2048), bf16),
            sds((2, 64, 1408), bf16),
            sds((2, 64, 768), bf16),
            sds((2, 64, 768), bf16),
            sds((2, 64, 256), bf16),
            sds((64, 128), f32),
            sds(group + (2048,), bf16),
            sds(group + (512,), bf16),
        ),
        in_specs=[pl.BlockSpec(memory_space=pltpu.SMEM)] + [pl.BlockSpec(memory_space=pltpu.VMEM)] * 2 + [ANY] * 9,
        out_specs=[ANY] * 9,
        scratch_shapes=[
            vm((64, 1376), bf16),
            vm((64, 1376), bf16),
            vm((64, 1376), bf16),
            vm((2, 64, 1408), bf16),
            vm((2, 64, 768), bf16),
            vm((2, 64, 768), bf16),
            vm((2, 64, 256), bf16),
            vm((64, 128), f32),
            vm((3, 64, 128), f32),
            vm((4, 2, 4, 64, 768), bf16),
            vm((4, 2, 4, 64, 256), bf16),
            vm((4, 2, 4, 64, 1408), bf16),
            vm((4, 2, 4, 64, 768), bf16),
            vm(group + (2048,), bf16),
            vm(group + (2048,), bf16),
            vm(group + (768,), bf16),
            vm(group + (1408,), bf16),
            vm((2, BLOCK + WINDOW, 512), bf16),
            vm((OWNED, 2048), f32),
            vm((2, OWNED, 2048), bf16),
            vm((OWNED, 2048), f32),
            vm(group + (2048,), bf16),
            vm((2, WINDOW, 512), f32),
            vm((2, WINDOW, 512), bf16),
            vm((2, WINDOW, 512), bf16),
            vm((6, 4, 64, 1408), bf16),
            vm((6, 4, 64, 768), bf16),
            vm((6, 4, 64, 768), bf16),
            vm((6, 4, 64, 256), bf16),
            vm((6, 64, 1408), bf16),
            vm((6, 64, 768), bf16),
            vm((6, 64, 768), bf16),
            vm((6, 64, 256), bf16),
            vm((2, 4, OWNED, WIDE), bf16),
            vm((PIECES, 6, 64, WIDE), bf16),
            vm((5, OWNED, WIDE), f32),
            vm((PIECES, 4, OWNED, WIDE), bf16),
            vm((PIECES, 6, 64, WIDE), bf16),
            pltpu.SemaphoreType.DMA((220,)),
            pltpu.SemaphoreType.DMA((220,)),
            pltpu.SemaphoreType.DMA((32,)),
            pltpu.SemaphoreType.DMA((20 * PIECES,)),
            pltpu.SemaphoreType.DMA((20 * PIECES,)),
            pltpu.SemaphoreType.REGULAR((2,)),
        ],
        compiler_params=pltpu.CompilerParams(
            collective_id=0, has_side_effects=True, vmem_limit_bytes=60 * 2**20
        ),
        name="block",
    )(lengths, gain_attn, gain_mlp, *weights, hid.reshape(2, 2, OWNED, 2048), cot.reshape(2, 2, OWNED, 2048))
    return outs[:7]


def per_device(
    hidden_in,
    norm_gain_attn,
    w_query,
    w_key,
    w_value,
    w_out,
    norm_gain_mlp,
    w_gate,
    w_up,
    w_down,
    lengths,
    cotangent,
):
    outs = block_call(
        lengths,
        norm_gain_attn,
        norm_gain_mlp,
        (w_query, w_key, w_value, w_out.T, w_gate, w_up, w_down.T),
        hidden_in,
        cotangent,
    )
    return final_call(*outs, norm_gain_attn, norm_gain_mlp)


def solution(mesh):
    mesh = Mesh(mesh.devices.reshape(4, 2, 4, 2, 2), AXES)
    seq, head = ("y", "xh", "z"), ("xl", "c")
    rows, cols, flat, turned = P(seq, None), P(seq, head), P(seq), P(head, seq)
    return jax.shard_map(
        per_device,
        mesh=mesh,
        in_specs=(rows, flat, cols, cols, cols, turned, flat, cols, cols, turned, P(), rows),
        out_specs=(rows, rows, flat, cols, cols, cols, turned, flat, cols, cols, turned),
        check_vma=False,
    )
```

```python
import jax
import jax.numpy as jnp
from jax import lax
from jax.experimental import pallas as pl
from jax.experimental.pallas import tpu as pltpu
from jax.sharding import Mesh, PartitionSpec as P

HEAD_DIM = 128
WINDOW = 64
BLOCK = 512
OWNED = 128
PIECES = 4
WIDE = 2048 // PIECES
AXES = ("y", "xh", "z", "xl", "c")

epsilon = 1e-05
masked_score = -1e30
f32 = jnp.float32
bf16 = jnp.bfloat16


MESH = pl.DeviceIdType.MESH
SCALE = HEAD_DIM ** (-0.5)
ANY = pl.BlockSpec(memory_space=pl.ANY)
TURNED = (((1,), (1,)), ((), ()))
LEFT_TURNED = (((0,), (0,)), ((), ()))


class Place:
    def __init__(self):
        self.y, self.z, self.c = lax.axis_index("y"), lax.axis_index("z"), lax.axis_index("c")
        self.xh, self.xl = lax.axis_index("xh"), lax.axis_index("xl")
        self.x = self.xh * 2 + self.xl
        self.q = self.xl * 2 + self.c

    def at(self, y=None, x=None, z=None, c=None):
        y = self.y if y is None else y
        x = self.x if x is None else x
        z = self.z if z is None else z
        c = self.c if c is None else c
        return (y, x // 2, z, x % 2, c)


class Links:
    def __init__(self, send_sems, recv_sems, local_sems):
        self.send_sems, self.recv_sems, self.local_sems = send_sems, recv_sems, local_sems
        self.count, self.local_count, self.started = 0, 0, []

    def send(self, src, dst, device):
        copy = self.prepare(src, dst, device)
        copy.start()
        return copy

    def prepare(self, src, dst, device):
        copy = pltpu.make_async_remote_copy(
            src_ref=src,
            dst_ref=dst,
            send_sem=self.send_sems.at[self.count],
            recv_sem=self.recv_sems.at[self.count],
            device_id=device,
            device_id_type=MESH,
        )
        self.count += 1
        self.started.append(copy)
        return copy

    def local(self, src, dst):
        copy = pltpu.make_async_copy(src, dst, self.local_sems.at[self.local_count])
        self.local_count += 1
        copy.start()
        return copy

    def settle(self, copies=None):
        copies = self.started if copies is None else copies
        for copy in copies:
            copy.wait_send()
        self.started = [copy for copy in self.started if not any(copy is other for other in copies)]


class WeightGather:
    def __init__(self, links, place, pack, whole, cut, direct=False):
        self.links, self.place, self.whole, self.direct = links, place, whole, direct
        cols = whole.shape[-1]
        self.parts = (pl.ds(0, cut), pl.ds(cut, cols - cut))
        self.swap = links.send(
            pack(1 - place.xh), whole.at[place.y, place.xh, place.z], place.at(x=(place.x + 2) % 4)
        )
        self.mine = links.local(pack(place.xh), whole.at[place.y, place.xh, place.z])
        if direct:
            self.got = self.spread(pack(place.xh), place.xh)
            self.early = list(self.got)

    def spread(self, ref, half):
        p, w = self.place, self.whole
        devices = [
            (p.at(z=(p.z + k) % 4), p.at(y=(p.y + k) % 4)) for k in (1, 3, 2)
        ]
        copies = []
        for along_z, along_y in devices:
            for lanes, device in zip(self.parts, (along_z, along_y)):
                copies.append(self.links.send(ref.at[:, lanes], w.at[p.y, half, p.z, :, lanes], device))
        return copies

    def send(self, ref, device):
        return self.links.send(ref, ref, device)

    def near(self, view_z, view_y):
        p = self.place
        first, second = self.parts
        zs = (p.at(z=(p.z + 1) % 4), p.at(z=(p.z + 3) % 4))
        ys = (p.at(y=(p.y + 1) % 4), p.at(y=(p.y + 3) % 4))
        (ref_z, axis_z), (ref_y, axis_y) = view_z, view_y
        to = {"z": zs, "y": ys}
        self.got = [
            self.send(ref_z, to[axis_z][0]),
            self.send(ref_y, to[axis_y][0]),
            self.send(ref_z, to[axis_z][1]),
            self.send(ref_y, to[axis_y][1]),
        ]

    def wait(self):
        for copy in self.got:
            copy.wait_recv()

    def start0(self):
        p, w = self.place, self.whole
        first, second = self.parts
        self.swap.wait_recv()
        self.mine.wait()
        if self.direct:
            self.got += self.spread(w.at[p.y, 1 - p.xh, p.z], 1 - p.xh)
            return
        self.near(
            (w.at[p.y, :, p.z, :, first], "z"),
            (w.at[p.y, :, p.z, :, second], "y"),
        )

    def start1(self):
        if self.direct:
            return
        p, w = self.place, self.whole
        first, second = self.parts
        self.wait()
        zn, zp, yn, yp = (p.z + 1) % 4, (p.z + 3) % 4, (p.y + 1) % 4, (p.y + 3) % 4
        self.got = [
            self.send(w.at[p.y, 0, zp, :, first], p.at(z=zn)),
            self.send(w.at[yp, 0, p.z, :, second], p.at(y=yn)),
            self.send(w.at[p.y, 1, zn, :, first], p.at(z=zp)),
            self.send(w.at[yn, 1, p.z, :, second], p.at(y=yp)),
        ]

    def start2(self):
        p, w = self.place, self.whole
        first, second = self.parts
        self.wait()
        self.near(
            (w.at[:, :, p.z, :, second], "z"),
            (w.at[p.y, :, :, :, first], "y"),
        )

    def start3(self):
        p, w = self.place, self.whole
        first, second = self.parts
        self.wait()
        zn, zp, yn, yp = (p.z + 1) % 4, (p.z + 3) % 4, (p.y + 1) % 4, (p.y + 3) % 4
        self.got = [
            self.send(w.at[yp, 0, :, :, first], p.at(y=yn)),
            self.send(w.at[:, 0, zp, :, second], p.at(z=zn)),
            self.send(w.at[yn, 1, :, :, first], p.at(y=yp)),
            self.send(w.at[:, 1, zn, :, second], p.at(z=zp)),
        ]

    def done(self):
        self.wait()


def greet(place):
    p = place
    barrier = pltpu.get_barrier_semaphore()
    partners = (
        p.at(z=(p.z + 1) % 4),
        p.at(z=(p.z + 3) % 4),
        p.at(y=(p.y + 1) % 4),
        p.at(y=(p.y + 3) % 4),
        p.at(x=(p.x + 1) % 4),
        p.at(x=(p.x + 3) % 4),
        p.at(x=(p.x + 2) % 4),
        p.at(c=1 - p.c),
        p.at(y=(p.y + 2) % 4),
        p.at(z=(p.z + 2) % 4),
        p.at(x=2 * p.xh + 1 - p.xl, c=1 - p.c),
    )
    for device in partners:
        pl.semaphore_signal(barrier, inc=1, device_id=device, device_id_type=MESH)

    @pl.when(p.z == 3)
    def _():
        pl.semaphore_signal(barrier, inc=1, device_id=p.at(y=(p.y + 1) % 4, z=0 * p.z), device_id_type=MESH)

    @pl.when(p.z == 0)
    def _():
        pl.semaphore_signal(barrier, inc=1, device_id=p.at(y=(p.y + 3) % 4, z=0 * p.z + 3), device_id_type=MESH)

    pl.semaphore_wait(barrier, 11 + jnp.where((p.z == 3) | (p.z == 0), 1, 0))


def unit_scale(values):
    return values * lax.rsqrt(jnp.mean(values * values, axis=-1, keepdims=True) + epsilon)


class WeightReduce:
    def __init__(self, links, place, total, first_in, second_in, out, cut):
        self.links, self.place, self.total, self.out = links, place, total, out
        self.copies = []
        self.one, self.two = first_in, second_in
        cols = total.shape[-1]
        self.cols = cols
        self.parts = (pl.ds(0, cut), pl.ds(cut, cols - cut))
        p = place
        self.yn, self.yp, self.yf = (p.y + 1) % 4, (p.y + 3) % 4, (p.y + 2) % 4
        self.zn, self.zp, self.zf = (p.z + 1) % 4, (p.z + 3) % 4, (p.z + 2) % 4
        self.next_y, self.prev_y = p.at(y=self.yn), p.at(y=self.yp)
        self.next_z, self.prev_z = p.at(z=self.zn), p.at(z=self.zp)

    def send(self, src, dst, device):
        copy = self.links.send(src, dst, device)
        self.copies.append(copy)
        return copy

    def start0(self):
        a, b = self.parts
        t, one, send = self.total, self.one, self.send
        self.far = [
            send(t.at[self.yf, 0, :, :, a], one.at[0, :, :, a], self.next_y),
            send(t.at[:, 0, self.zf, :, b], one.at[0, :, :, b], self.next_z),
            send(t.at[self.yf, 1, :, :, a], one.at[2, :, :, a], self.prev_y),
            send(t.at[:, 1, self.zf, :, b], one.at[2, :, :, b], self.prev_z),
        ]
        self.near = [
            send(t.at[self.yn, 1, :, :, a], one.at[1, :, :, a], self.next_y),
            send(t.at[:, 1, self.zn, :, b], one.at[1, :, :, b], self.next_z),
            send(t.at[self.yp, 0, :, :, a], one.at[3, :, :, a], self.prev_y),
            send(t.at[:, 0, self.zp, :, b], one.at[3, :, :, b], self.prev_z),
        ]

    def add(self, target, sources, rows):
        def body(i, _):
            ref = target(i)
            value = ref[...].astype(f32)
            for source in sources:
                value = value + source(i)[...].astype(f32)
            ref[...] = value.astype(bf16)
            return 0

        lax.fori_loop(0, rows, body, 0)

    def start1(self):
        a, b = self.parts
        t, one, send = self.total, self.one, self.send
        yn, yp, zn, zp = self.yn, self.yp, self.zn, self.zp
        self.sums = []
        self.far[0].wait_recv()
        self.add(lambda i: t.at[yn, 0, i, :, a], [lambda i: one.at[0, i, :, a]], 4)
        self.sums.append(send(t.at[yn, 0, :, :, a], one.at[4, :, :, a], self.next_y))
        self.far[1].wait_recv()
        self.add(lambda i: t.at[i, 0, zn, :, b], [lambda i: one.at[0, i, :, b]], 4)
        self.sums.append(send(t.at[:, 0, zn, :, b], one.at[4, :, :, b], self.next_z))
        self.far[2].wait_recv()
        self.add(lambda i: t.at[yp, 1, i, :, a], [lambda i: one.at[2, i, :, a]], 4)
        self.sums.append(send(t.at[yp, 1, :, :, a], one.at[5, :, :, a], self.prev_y))
        self.far[3].wait_recv()
        self.add(lambda i: t.at[i, 1, zp, :, b], [lambda i: one.at[2, i, :, b]], 4)
        self.sums.append(send(t.at[:, 1, zp, :, b], one.at[5, :, :, b], self.prev_z))

    def start2(self):
        a, b = self.parts
        t, one, two, send = self.total, self.one, self.two, self.send
        p = self.place
        for copy in self.near + self.sums:
            copy.wait_recv()
        self.add(lambda i: t.at[p.y, 0, i, :, a], [lambda i: one.at[3, i, :, a], lambda i: one.at[4, i, :, a]], 4)
        self.add(lambda i: t.at[p.y, 1, i, :, a], [lambda i: one.at[1, i, :, a], lambda i: one.at[5, i, :, a]], 4)
        self.add(lambda i: t.at[i, 0, p.z, :, b], [lambda i: one.at[3, i, :, b], lambda i: one.at[4, i, :, b]], 4)
        self.add(lambda i: t.at[i, 1, p.z, :, b], [lambda i: one.at[1, i, :, b], lambda i: one.at[5, i, :, b]], 4)
        sends = (
            (t.at[p.y, :, self.zn, :, a], 0, a, self.next_z),
            (t.at[self.yn, :, p.z, :, b], 0, b, self.next_y),
            (t.at[p.y, :, self.zp, :, a], 2, a, self.prev_z),
            (t.at[self.yp, :, p.z, :, b], 2, b, self.prev_y),
            (t.at[p.y, :, self.zf, :, a], 4, a, p.at(z=self.zf)),
            (t.at[self.yf, :, p.z, :, b], 4, b, p.at(y=self.yf)),
        )
        self.sums = [send(src, two.at[pl.ds(slot, 2), :, lanes], device) for src, slot, lanes, device in sends]

    def plus(self, target, *sources):
        value = target[...].astype(f32)
        for source in sources:
            value = value + source[...].astype(f32)
        target[...] = value.astype(bf16)

    def start3(self):
        p, two = self.place, self.two
        for copy in self.sums:
            copy.wait_recv()
        for half in range(2):
            self.plus(two.at[half], two.at[2 + half], two.at[4 + half], self.total.at[p.y, half, p.z])
        self.swap = self.links.send(two.at[1 - p.xh], self.out.at[p.xh], p.at(x=(p.x + 2) % 4))
        self.mine = self.links.local(two.at[p.xh], self.out.at[p.xh])

    def sent(self):
        self.links.settle(self.copies)

    def done(self):
        self.swap.wait_recv()
        self.mine.wait()


class GroupReduce:
    def __init__(self, place, partial, bufs, sems):
        self.place, self.partial = place, partial
        self.send_c, self.recv_c, self.tmp, self.snd, self.rcv, self.own = bufs
        self.send_sems, self.recv_sems = sems

    def copy(self, src, dst, index, device):
        return pltpu.make_async_remote_copy(
            src_ref=src,
            dst_ref=dst,
            send_sem=self.send_sems.at[index],
            recv_sem=self.recv_sems.at[index],
            device_id=device,
            device_id_type=MESH,
        )

    def crossing(self, n):
        return self.copy(self.send_c.at[n % 2], self.recv_c.at[n], n, self.place.at(c=1 - self.place.c))

    def to_next(self, n):
        pair = pl.ds(0, 2)
        return self.copy(
            self.snd.at[n, pair], self.rcv.at[n, pair], PIECES + n, self.place.at(x=(self.place.x + 1) % 4)
        )

    def to_prev(self, n):
        pair = pl.ds(2, 2)
        return self.copy(
            self.snd.at[n, pair], self.rcv.at[n, pair], 2 * PIECES + n, self.place.at(x=(self.place.x + 3) % 4)
        )

    def sum_next(self, n):
        return self.copy(
            self.snd.at[n, 4], self.rcv.at[n, 4], 3 * PIECES + n, self.place.at(x=(self.place.x + 1) % 4)
        )

    def sum_prev(self, n):
        return self.copy(
            self.snd.at[n, 5], self.rcv.at[n, 5], 4 * PIECES + n, self.place.at(x=(self.place.x + 3) % 4)
        )

    def sibling_part(self, n):
        part = self.partial(n, 1 - self.place.c)

        @pl.when(n >= 2)
        def _():
            self.crossing(n - 2).wait_send()

        self.send_c[n % 2] = part.astype(bf16).reshape(4, OWNED, WIDE)
        self.crossing(n).start()

    def own_part(self, n, launch):
        p, tmp, snd = self.place, self.tmp, self.snd
        part = self.partial(n, p.c).reshape(4, OWNED, WIDE)
        self.crossing(n).wait_recv()
        tmp[...] = part + self.recv_c[n].astype(f32)
        far, nxt, prev = (p.x + 2) % 4, (p.x + 1) % 4, (p.x + 3) % 4
        low, high = pl.ds(0, 64), pl.ds(64, 64)
        snd[n, 0] = tmp[far, low].astype(bf16)
        snd[n, 1] = tmp[nxt, high].astype(bf16)
        if launch:
            self.to_next(n).start()
        snd[n, 2] = tmp[far, high].astype(bf16)
        snd[n, 3] = tmp[prev, low].astype(bf16)
        if launch:
            self.to_prev(n).start()
        snd[n, 4] = tmp[nxt, low].astype(bf16)
        snd[n, 5] = tmp[prev, high].astype(bf16)
        self.own[:, pl.ds(pl.multiple_of(n * WIDE, WIDE), WIDE)] = tmp[p.x]

    def pass_on(self, n):
        snd, rcv = self.snd, self.rcv
        self.to_next(n).wait_recv()
        snd[n, 4] = (snd[n, 4].astype(f32) + rcv[n, 0].astype(f32)).astype(bf16)
        self.sum_next(n).start()
        self.to_prev(n).wait_recv()
        snd[n, 5] = (snd[n, 5].astype(f32) + rcv[n, 2].astype(f32)).astype(bf16)
        self.sum_prev(n).start()

    def run(self, launch=True, pass_on=True, hooks=()):
        def body(i, _):
            @pl.when(i < PIECES)
            def _():
                self.sibling_part(i)

            @pl.when((i >= 1) & (i < PIECES + 1))
            def _():
                self.own_part(i - 1, launch)

            if pass_on:

                @pl.when(i >= 2)
                def _():
                    self.pass_on(i - 2)

            for step, hook in hooks:
                pl.when(i == step)(hook)
            return 0

        lax.fori_loop(0, PIECES + 2 if pass_on else PIECES + 1, body, 0)

    def launch(self):
        def body(n, _):
            self.to_next(n).start()
            self.to_prev(n).start()
            return 0

        lax.fori_loop(0, PIECES, body, 0)

    def pass_range(self, start, stop):
        def body(n, _):
            self.pass_on(n)
            return 0

        lax.fori_loop(start, stop, body, 0)

    def finish(self):
        def body(n, _):
            lanes = pl.ds(pl.multiple_of(n * WIDE, WIDE), WIDE)
            low, high = pl.ds(0, 64), pl.ds(64, 64)
            rcv, own = self.rcv, self.own
            self.sum_next(n).wait_recv()
            own[low, lanes] = own[low, lanes] + rcv[n, 3].astype(f32) + rcv[n, 4].astype(f32)
            self.sum_prev(n).wait_recv()
            own[high, lanes] = own[high, lanes] + rcv[n, 1].astype(f32) + rcv[n, 5].astype(f32)
            return 0

        lax.fori_loop(0, PIECES, body, 0)

    def sent(self):
        def body(n, _):
            for copy in (self.to_next, self.to_prev, self.sum_next, self.sum_prev):
                copy(n).wait_send()
            return 0

        self.crossing(PIECES - 2).wait_send()
        self.crossing(PIECES - 1).wait_send()

        lax.fori_loop(0, PIECES, body, 0)


class GroupGather:
    def __init__(self, links, place, whole):
        self.links, self.place, self.whole = links, place, whole
        self.low, self.high = pl.ds(0, 64), pl.ds(64, 64)

    def send(self, ref, device):
        return self.links.send(ref, ref, device)

    def start(self):
        p, w = self.place, self.whole
        self.nxt, self.prev, self.far = (p.x + 1) % 4, (p.x + 3) % 4, (p.x + 2) % 4
        self.to_next, self.to_prev = p.at(x=self.nxt), p.at(x=self.prev)
        self.sibling = p.at(c=1 - p.c)
        low, high = w.at[p.x, p.c, self.low], w.at[p.x, p.c, self.high]
        self.first = [self.send(low, self.to_next), self.send(high, self.to_prev)]
        self.second = [self.send(high, self.to_next), self.send(low, self.to_prev)]
        tiles = (p.x, self.prev, self.nxt, self.far)
        self.paired = [self.later(w.at[x, p.c], self.sibling) for x in tiles]
        self.paired[0].start()
        self.third = [
            self.later(w.at[self.prev, p.c, self.low], self.to_next),
            self.later(w.at[self.nxt, p.c, self.high], self.to_prev),
        ]

    def later(self, ref, device):
        return self.links.prepare(ref, ref, device)

    def forward(self):
        for k in range(2):
            self.first[k].wait_recv()
            self.third[k].start()

    def share_near(self):
        for k in range(2):
            self.second[k].wait_recv()
            self.paired[1 + k].start()

    def share_far(self):
        for copy in self.third:
            copy.wait_recv()
        self.paired[3].start()

    def sent(self):
        self.links.settle(self.first + self.second + self.third + self.paired)

    def ready(self, k):
        self.paired[k].wait_recv()


class BlockExchange:
    def __init__(self, links, place, block, whole):
        p = place
        self.place, self.links = p, links
        beside = p.at(x=2 * p.xh + 1 - p.xl)
        sibling = p.at(c=1 - p.c)
        self.near, self.next = 3 - p.x, 2 * (1 - p.xh) + p.xl
        halves = [pl.ds(0, 64), pl.ds(64, 64)]
        self.cross = [links.send(block.at[p.xl, p.c, h], whole.at[p.x, p.c, h], p.at(x=3 - p.x)) for h in halves]
        self.across = [
            links.prepare(whole.at[self.near, p.c, h], whole.at[self.near, p.c, h], beside) for h in halves
        ]
        self.paired = [
            links.prepare(whole.at[x, p.c], whole.at[x, p.c], sibling) for x in (self.near, self.next)
        ]

    def forward(self, k):
        self.cross[k].wait_recv()
        self.across[k].start()

    def share(self):
        self.paired[0].start()

    def share_next(self):
        for copy in self.across:
            copy.wait_recv()
        self.paired[1].start()

    def done(self, k):
        self.paired[k].wait_recv()


class BlockReduce(GroupReduce):
    def __init__(self, place, partial, bufs, sems, extra=None):
        self.place, self.partial, self.extra = place, partial, extra
        self.send_c, self.recv_c, self.tmp, self.moving = bufs
        self.send_sems, self.recv_sems = sems
        self.facing, self.beside = place.at(x=3 - place.x), place.at(x=2 * place.xh + 1 - place.xl)

    def part(self, which, n):
        lanes = pl.ds(pl.multiple_of(n * WIDE, WIDE), WIDE)
        return self.moving.at[pl.ds(2 * (which // 2), 2), which % 2, :, lanes]

    def over(self, n):
        return self.copy(self.part(0, n), self.part(1, n), PIECES + n, self.facing)

    def across(self, n):
        return self.copy(self.part(2, n), self.part(3, n), 2 * PIECES + n, self.beside)

    def own_part(self, n, launch):
        p, tmp = self.place, self.tmp
        part = self.partial(n, p.c).reshape(4, OWNED, WIDE)
        self.crossing(n).wait_recv()
        tmp[...] = part + self.recv_c[n].astype(f32)
        if self.extra is not None:
            lanes = pl.ds(pl.multiple_of(n * WIDE, WIDE), WIDE)
            tmp[p.x] += self.extra[:, lanes]
        self.part(0, n)[...] = tmp[pl.ds(2 * (1 - p.xh), 2)].astype(bf16)
        if launch:
            self.over(n).start()
        self.part(2, n)[...] = tmp[pl.ds(2 * p.xh, 2)].astype(bf16)

    def pass_on(self, n):
        self.over(n).wait_recv()
        mine = self.part(2, n)
        mine[...] = (mine[...].astype(f32) + self.part(1, n)[...].astype(f32)).astype(bf16)
        self.across(n).start()

    def launch(self):
        def body(n, _):
            self.over(n).start()
            return 0

        lax.fori_loop(0, PIECES, body, 0)

    def finish(self):
        def body(n, _):
            self.across(n).wait_recv()
            return 0

        lax.fori_loop(0, PIECES, body, 0)

    def total(self, tile, rows):
        return self.moving[2 + tile, 0, rows].astype(f32) + self.moving[2 + tile, 1, rows].astype(f32)

    def crossed(self):
        self.crossing(PIECES - 2).wait_send()
        self.crossing(PIECES - 1).wait_send()

    def sent(self):
        def body(n, _):
            self.over(n).wait_send()
            self.across(n).wait_send()
            return 0

        lax.fori_loop(0, PIECES, body, 0)


class BlockOut:
    def __init__(self, links, place, rows, out):
        mine = out.at[:, place.c]
        self.local = links.local(rows, mine)
        self.paired = links.send(rows, mine, place.at(c=1 - place.c))

    def done(self):
        self.paired.wait_recv()
        self.local.wait()


def norm_back(e, values):
    r = lax.rsqrt(jnp.mean(values * values, axis=-1, keepdims=True) + epsilon)
    return r * e - values * r**3 * jnp.mean(e * values, axis=-1, keepdims=True)


def column(gain):
    row = gain[...].astype(f32).reshape(1, 64)
    places = [lax.broadcasted_iota(jnp.int32, (64, 64), k) for k in range(2)]
    return jnp.sum(jnp.where(places[0] == places[1], row, 0.0), axis=1, keepdims=True)


def pack_attn(gain, query, key, value, pack):
    for i, ref in enumerate((query, key, value)):
        scaled = (ref[...].astype(f32) * gain).astype(bf16)
        for k in range(2):
            pack(k)[:, 256 * i : 256 * i + 256] = scaled[:, 256 * k : 256 * k + 256]


def pack_out(out, pack):
    for k in range(2):
        pack(k)[...] = out[:, 256 * k : 256 * k + 256]


def pack_ff(gain, gate, up, down, pack_gu, pack_d):
    zeros = jnp.zeros((64, 16), f32)
    for k in range(2):
        start = 688 * k
        tails = []
        for i, ref in enumerate((gate, up)):
            part = ref[:, start : start + 640].astype(f32) * gain
            pack_gu(k)[:, 640 * i : 640 * i + 640] = part.astype(bf16)
            tails += [ref[:, start + 640 : start + 688].astype(f32) * gain, zeros]
        pack_gu(k)[:, 1280:] = jnp.concatenate(tails, axis=1).astype(bf16)
        part = down[:, start : start + 688].astype(f32)
        pack_d(k)[...] = jnp.concatenate([part, jnp.zeros((64, 80), f32)], axis=1).astype(bf16)


def row_dots(weight, grads):
    return jnp.sum(weight.astype(f32) * grads.astype(f32), axis=1, keepdims=True)


def final_kernel(
    result_in, input_in, fin_gu_in, fin_d_in, fin_q_in, fin_o_in, sums_in, gain_attn, gain_mlp,
    result, input_grad, g_attn_out, query_out, key_out, value_out, out_out, g_mlp_out, gate_out, up_out, down_out,
    hold, fin_gu, fin_d, fin_q, fin_o, sums, g_attn, query, key, value, out, g_mlp, gate, up, down, sems, small_sems,
):
    parts = [(k, i, j) for i in range(2) for j in range(2) for k in range(2)]
    inputs, outputs = (result_in, input_in), (result, input_grad)
    small = ((fin_q_in, fin_q), (fin_o_in, fin_o), (fin_d_in, fin_d), (fin_gu_in, fin_gu), (sums_in, sums))
    fetched = [pltpu.make_async_copy(ref, here, small_sems.at[n]) for n, (ref, here) in enumerate(small)]
    loads = [
        pltpu.make_async_copy(inputs[k].at[i, j], hold.at[k, i, j], sems.at[n]) for n, (k, i, j) in enumerate(parts)
    ]
    stores = [
        pltpu.make_async_copy(hold.at[k, i, j], outputs[k].at[i, j], sems.at[8 + n])
        for n, (k, i, j) in enumerate(parts)
    ]
    finished = [
        pltpu.make_async_copy(here, ref, small_sems.at[5 + n])
        for n, (here, ref) in enumerate(
            (
                (query, query_out),
                (key, key_out),
                (value, value_out),
                (out, out_out),
                (down, down_out),
                (gate, gate_out),
                (up, up_out),
                (g_attn, g_attn_out),
                (g_mlp, g_mlp_out),
            )
        )
    ]
    for copy in fetched + loads:
        copy.start()
    attn, mlp = column(gain_attn), column(gain_mlp)

    def hand_over(start):
        for n in (start, start + 1):
            loads[n].wait()
            stores[n].start()

    fetched[0].wait()
    for i, ref in enumerate((query, key, value)):
        for k in range(2):
            ref[:, 256 * k : 256 * k + 256] = fin_q[k, :, 256 * i : 256 * i + 256].astype(f32) * attn
        finished[i].start()
    fetched[1].wait()
    for k in range(2):
        out[:, 256 * k : 256 * k + 256] = fin_o[k].astype(f32)
    finished[3].start()
    hand_over(0)
    fetched[2].wait()
    for k in range(2):
        down[:, 688 * k : 688 * k + 688] = fin_d[k, :, :688].astype(f32)
    finished[4].start()
    hand_over(2)
    fetched[3].wait()
    for i, ref in enumerate((gate, up)):
        for k in range(2):
            ref[:, 688 * k : 688 * k + 640] = fin_gu[k, :, 640 * i : 640 * i + 640].astype(f32) * mlp
            tail = fin_gu[k, :, 1280:].astype(f32) * mlp
            ref[:, 688 * k + 640 : 688 * k + 688] = tail[:, 64 * i : 64 * i + 48]
        finished[5 + i].start()
    hand_over(4)
    fetched[4].wait()
    turned = sums[...].T
    g_attn[...] = turned[0:1]
    g_mlp[...] = turned[1:2]
    for copy in finished[7:]:
        copy.start()
    hand_over(6)
    for copy in stores + finished:
        copy.wait()


def final_call(result, input_grad, fin_gu, fin_d, fin_q, fin_o, sums, gain_attn, gain_mlp):
    sds, vm = jax.ShapeDtypeStruct, pltpu.VMEM
    vmem = pl.BlockSpec(memory_space=pltpu.VMEM)
    whole = (2, 2, OWNED, 2048)
    grads = ((1, 64), (64, 512), (64, 512), (64, 512), (64, 512), (1, 64), (64, 1376), (64, 1376), (64, 1376))
    outs = pl.pallas_call(
        final_kernel,
        out_shape=(sds(whole, bf16), sds(whole, bf16)) + tuple(sds(shape, f32) for shape in grads),
        in_specs=[ANY] * 7 + [vmem] * 2,
        out_specs=[ANY] * 11,
        scratch_shapes=[vm((2,) + whole, bf16)]
        + [vm(ref.shape, ref.dtype) for ref in (fin_gu, fin_d, fin_q, fin_o, sums)]
        + [vm(shape, f32) for shape in grads]
        + [pltpu.SemaphoreType.DMA((16,)), pltpu.SemaphoreType.DMA((14,))],
        compiler_params=pltpu.CompilerParams(vmem_limit_bytes=62 * 2**20),
        name="final",
    )(result, input_grad, fin_gu, fin_d, fin_q, fin_o, sums, gain_attn, gain_mlp)
    result, input_grad, g_attn, query, key, value, out, g_mlp, gate, up, down = outs
    return (
        result.reshape(BLOCK, 2048),
        input_grad.reshape(BLOCK, 2048),
        g_attn.reshape(64),
        query,
        key,
        value,
        out.T,
        g_mlp.reshape(64),
        gate,
        up,
        down.T,
    )


def block_kernel(
    lengths, gain_attn, gain_mlp, w_query, w_key, w_value, w_out, w_gate, w_up, w_down, hid, cot_in,
    result_o, grad_o, fin_gu_o, fin_d_o, fin_q_o, fin_o_o, sums_o, xr_o, qm_o,
    raw_g, raw_u, raw_d,
    fin_gu, fin_d, fin_q, fin_o, sums, sums_in,
    wq, wo, gu, d, nm, cot, act, gg, kv, resid, hid_pair, own, gb,
    last_kv, tail_out, tail_in, in_gu, in_d, in_q, in_o, in2_gu, in2_d, in2_q, in2_o,
    send_c, snd, tmp, recv_c, rcv,
    send_sems, recv_sems, local_sems, group_send, group_recv, ready,
):
    p = Place()
    links = Links(send_sems, recv_sems, local_sems)
    sibling = p.at(c=1 - p.c)
    facing, beside = p.at(x=3 - p.x), p.at(x=2 * p.xh + 1 - p.xl)

    def signal(semaphore, devices):
        for device in devices:
            pl.semaphore_signal(semaphore, inc=1, device_id=device, device_id_type=MESH)

    hidg, xr = gb, nm

    own_pair = pl.ds(2 * p.xh, 2)
    own_hidden = links.local(hid, hidg.at[own_pair])
    load_hid = links.local(hid.at[:, p.c], hid_pair)
    own_cot = links.local(cot_in, cot.at[own_pair])
    raw_q, raw_k, raw_v, raw_o = (snd.at[0, k] for k in range(4))
    half = lambda k: pl.ds(64 * k, 64)
    pk_q, pk_d = (lambda k: act.at[0, 0, half(k)]), (lambda k: act.at[0, 1, half(k)])
    pk_o, pk_gu = (lambda k: act.at[1, 0, half(k), pl.ds(0, 256)]), (lambda k: gg.at[0, 0, half(k)])
    raws = ((w_query, raw_q), (w_key, raw_k), (w_value, raw_v), (w_out, raw_o), (w_gate, raw_g), (w_up, raw_u), (w_down, raw_d))
    loads = [links.local(ref, raw) for ref, raw in raws]
    greet(p)
    scale_attn, scale_mlp = column(gain_attn), column(gain_mlp)
    for copy in loads[:4]:
        copy.wait()
    pack_attn(scale_attn, raw_q, raw_k, raw_v, pk_q)
    pack_out(raw_o, pk_o)
    g_q = WeightGather(links, p, pk_q, wq, 384, direct=True)
    g_o = WeightGather(links, p, pk_o, wo, 128, direct=True)
    e_hid = BlockExchange(links, p, hid, hidg)
    for copy in loads[4:]:
        copy.wait()
    pack_ff(scale_mlp, raw_g, raw_u, raw_d, pk_gu, pk_d)
    g_q.start0()
    g_o.start0()
    def norm_rows(tile, core):
        def body(i, _):
            r = pl.ds(i * 32, 32)
            xr[tile, core, r] = unit_scale(hidg[tile, core, r].astype(f32)).astype(bf16)
            return 0

        lax.fori_loop(0, 4, body, 0)

    def norm_own(i, _):
        norm_rows(2 * p.xh + i // 2, i % 2)
        return 0

    own_hidden.wait()
    lax.fori_loop(0, 4, norm_own, 0)
    g_q.start2()
    e_hid.forward(0)
    g_gu = WeightGather(links, p, pk_gu, gu, 768)
    g_d = WeightGather(links, p, pk_d, d, 384)
    e_hid.forward(1)
    e_hid.share()
    e_cot = BlockExchange(links, p, cot_in, cot)
    norm_rows(e_hid.near, p.c)
    g_q.start3()
    g_o.start2()
    g_gu.start0()
    g_d.start0()
    e_hid.done(0)
    norm_rows(e_hid.near, 1 - p.c)
    g_q.done()

    links.settle([g_q.swap, g_o.swap, g_gu.swap, g_d.swap] + g_q.early + g_o.early)

    def project(t):
        w = wq[...].reshape(2048, 768)
        out = jnp.dot(xr[t].reshape(256, 2048), w, preferred_element_type=f32).astype(bf16)
        gg[t, :, :, 0:256] = out[:, :256].reshape(2, OWNED, 256)
        kv[t // 2, pl.ds((t % 2) * 256 + WINDOW, 256)] = out[:, 256:]

    def project_three(i, _):
        project(jnp.where(i < 2, 2 * p.xh + i, e_hid.near))
        return 0

    lax.fori_loop(0, 3, project_three, 0)
    g_o.start3()
    e_hid.share_next()
    norm_rows(e_hid.next, p.c)
    e_cot.forward(0)
    e_hid.done(1)
    norm_rows(e_hid.next, 1 - p.c)
    xr_spill = links.local(xr, xr_o)
    project(e_hid.next)

    tails = []
    last = jnp.where(p.z == 3, 1, 0)
    for block in range(2):
        to_y = p.y if block == 0 else (p.y + last) % 4
        slot = last if block == 0 else 1 - last
        tails.append(
            links.send(
                kv.at[block, pl.ds(BLOCK, WINDOW)],
                kv.at[slot, pl.ds(0, WINDOW)],
                p.at(y=to_y, z=(p.z + 1) % 4),
            )
        )
    end0 = lengths[0]
    end1 = end0 + lengths[1]

    def masked(scores, block, chunk):
        start = (p.y * 8 + block * 4 + p.z) * BLOCK + chunk * 128
        query = start + lax.broadcasted_iota(jnp.int32, (128, 192), 0)
        key = start - WINDOW + lax.broadcasted_iota(jnp.int32, (128, 192), 1)
        seen = (key <= query) & (key > query - WINDOW) & (key >= 0)
        for end in (end0, end1):
            seen = seen & ((key >= end) | (query < end))
        return jnp.where(seen, scores, masked_score)

    def probabilities(query, keys, block, chunk):
        scores = lax.dot_general(query, keys, TURNED, preferred_element_type=f32) * SCALE
        scores = masked(scores, block, chunk)
        expo = jnp.exp(scores - jnp.max(scores, axis=-1, keepdims=True))
        return expo / jnp.sum(expo, axis=-1, keepdims=True)

    def attend(block, chunk):
        x, core = block * 2 + chunk // 2, chunk % 2
        r = pl.multiple_of(chunk * 128, 128)
        for head in range(2):
            lane = head * 128
            query = gg[x, core, :, lane : lane + 128]
            keys = kv[block, pl.ds(r, 192), lane : lane + 128]
            values = kv[block, pl.ds(r, 192), lane + 256 : lane + 384]
            probs = probabilities(query, keys, block, chunk).astype(bf16)
            out = jnp.dot(probs, values, preferred_element_type=f32)
            gg[x, core, :, lane + 256 : lane + 384] = out.astype(bf16)

    def inner(i, _):
        for chunk in range(1, 4):
            attend(i, chunk)
        return 0

    e_cot.forward(1)
    e_cot.share()
    g_gu.start1()
    g_d.start1()
    lax.fori_loop(0, 2, inner, 0)
    g_d.start2()
    for copy in tails:
        copy.wait_recv()

    def first_chunk(i, _):
        attend(i, 0)
        return 0

    lax.fori_loop(0, 2, first_chunk, 0)
    mixed = gg.at[:, :, :, pl.ds(256, 256)]
    g_gu.start2()
    g_o.done()
    xr_spill.wait()

    def partial_of(left, right, width, start=0):
        def partial(n, core):
            return lax.dot_general(
                left[:, core, :, start : start + width].reshape(512, width),
                right[n].reshape(WIDE, width),
                TURNED,
                preferred_element_type=f32,
            )

        return partial

    def group_reduce(k, partial):
        span = pl.ds(5 * PIECES * k, 5 * PIECES)
        return GroupReduce(
            p, partial, (send_c, recv_c, tmp.at[pl.ds(0, 4)], snd, rcv, own), (group_send.at[span], group_recv.at[span])
        )

    r_branch = group_reduce(0, partial_of(gg, wo, 256, 256))
    r_branch.run(pass_on=False)
    e_cot.share_next()
    r_branch.pass_range(0, 3)
    g_d.start3()
    r_branch.pass_range(3, 4)
    load_hid.wait()
    r_branch.finish()

    def resid_rows(i, _):
        r = pl.ds(i * 16, 16)
        total = hid_pair[p.xl, r].astype(f32) + own[r]
        resid[r] = total
        nm[p.x, p.c, r] = unit_scale(total).astype(bf16)
        return 0

    lax.fori_loop(0, OWNED // 16, resid_rows, 0)
    g_nm = GroupGather(links, p, nm)
    g_nm.start()
    g_gu.start3()
    q_spill = links.local(gg.at[:, :, :, pl.ds(0, 512)], qm_o)
    own_cot.wait()
    for k in range(2):
        e_cot.done(k)
    g_d.done()

    def grad_activated(t, _):
        out = jnp.dot(cot[t].reshape(256, 2048), d[...].reshape(2048, 768), preferred_element_type=f32)
        act[t] = out.astype(bf16).reshape(2, OWNED, 768)
        return 0

    lax.fori_loop(0, 4, grad_activated, 0)
    q_spill.wait()
    g_nm.forward()
    g_gu.done()
    g_nm.ready(0)

    def feed(k, _):
        @pl.when(k == 1)
        def _():
            g_nm.share_near()
            g_nm.ready(1)

        @pl.when(k == 2)
        def _():
            g_nm.ready(2)

        @pl.when(k == 3)
        def _():
            g_nm.share_far()
            g_nm.ready(3)

        t = (p.x + jnp.where(k == 0, 0, jnp.where(k == 1, 3, k - 1))) % 4
        part = jnp.dot(nm[t].reshape(256, 2048), gu[...].reshape(2048, 1408), preferred_element_type=f32)
        back = act[t].reshape(256, 768).astype(f32)
        tail = part[:, 1280:]
        flipped = pltpu.roll(tail, 64, 1)
        lane = lax.broadcasted_iota(jnp.int32, (256, 128), 1)
        for lanes, gate, up in (
            (slice(0, 640), part[:, :640], part[:, 640:1280]),
            (slice(640, 768), tail, flipped),
        ):
            sig = 1 / (1 + jnp.exp(-gate))
            silu = gate * sig
            grad_act = back[:, lanes]
            act[t, :, :, lanes] = (silu * up).astype(bf16).reshape(2, OWNED, -1)
            grad_gate = grad_act * up * sig * (1 + gate * (1 - sig))
            grad_up = grad_act * silu
            if lanes.start == 0:
                gg[t, :, :, :640] = grad_gate.astype(bf16).reshape(2, OWNED, 640)
                gg[t, :, :, 640:1280] = grad_up.astype(bf16).reshape(2, OWNED, 640)
            else:
                both = jnp.where(lane < 64, grad_gate, pltpu.roll(grad_up, 64, 1))
                gg[t, :, :, 1280:] = both.astype(bf16).reshape(2, OWNED, 128)
        return 0

    lax.fori_loop(0, 4, feed, 0)

    r_branch.sent()
    links.settle()
    r_mlp = group_reduce(1, partial_of(gg, gu, 1408))
    r_mlp.run(pass_on=False)

    def grads_into(out, left, right, width, reduce=None):
        def body(n, _):
            lanes = pl.ds(pl.multiple_of(n * 256, 256), 256)
            part = lax.dot_general(
                left[:, :, :, lanes].reshape(1024, 256),
                right[...].reshape(1024, width),
                LEFT_TURNED,
                preferred_element_type=f32,
            )
            out[n // 2, n % 2] = part.astype(bf16).reshape(4, 64, width)
            if reduce is not None:

                @pl.when(n % 2 == 0)
                def _():
                    reduce.pass_on(n // 2)

            return 0

        lax.fori_loop(0, 8, body, 0)

    grads_into(gu, nm, gg, 1408, r_mlp)
    w_gu = WeightReduce(links, p, gu, in_gu, in2_gu, fin_gu, 768)
    w_gu.start0()
    signal(ready.at[0], (facing, beside))
    load_qm = links.local(qm_o, gg.at[:, :, :, pl.ds(0, 512)])
    r_mlp.finish()

    def grad_rows(i, _):
        r = pl.ds(i * 16, 16)
        grad = cot[p.x, p.c, r].astype(f32) + norm_back(own[r], resid[r])
        gb[p.x, p.c, r] = grad.astype(bf16)
        return 0

    lax.fori_loop(0, OWNED // 16, grad_rows, 0)
    g_branch = GroupGather(links, p, gb)
    g_branch.start()
    r_mlp.sent()
    g_branch.ready(0)

    def block_reduce(k, partial, moving, extra=None):
        span = pl.ds(5 * PIECES * k, 5 * PIECES)
        sems = (group_send.at[span], group_recv.at[span])
        return BlockReduce(p, partial, (send_c, recv_c, tmp.at[pl.ds(0, 4)], moving), sems, extra)

    r_out = block_reduce(2, partial_of(act, d, 768), nm, resid)
    r_out.run(launch=False, pass_on=False)
    g_branch.forward()
    w_gu.start1()
    grads_into(d, cot, act, 768)
    signal(ready.at[1], (facing, beside, sibling))
    w_d = WeightReduce(links, p, d, in_d, in2_d, fin_d, 384)
    w_d.start0()
    g_branch.share_near()

    def grad_mixed(t):
        out = jnp.dot(gb[t].reshape(256, 2048), wo[...].reshape(2048, 256), preferred_element_type=f32)
        gg[t, :, :, 512:768] = out.astype(bf16).reshape(2, OWNED, 256)

    first = jnp.where(p.z == 0, 1, 0)
    tails = []

    def attend_back(block):
        tmp[...] = jnp.zeros_like(tmp)

        def chunk_body(chunk, _):
            x, core = block * 2 + chunk // 2, chunk % 2
            r = pl.multiple_of(chunk * 128, 128)
            rows = pl.ds(r, 192)
            for head in range(2):
                lane = head * 128
                query = gg[x, core, :, lane : lane + 128]
                grad = gg[x, core, :, lane + 512 : lane + 640]
                keys = kv[block, rows, lane : lane + 128]
                values = kv[block, rows, lane + 256 : lane + 384]
                probs = probabilities(query, keys, block, chunk)
                probs_low = probs.astype(bf16)
                grad_probs = lax.dot_general(grad, values, TURNED, preferred_element_type=f32)
                inner = jnp.sum(probs * grad_probs, axis=-1, keepdims=True)
                grad_scores = (probs * (grad_probs - inner)).astype(bf16)
                grad_query = jnp.dot(grad_scores, keys, preferred_element_type=f32) * SCALE
                act[x, core, :, lane : lane + 128] = grad_query.astype(bf16)
                grad_keys = lax.dot_general(grad_scores, query, LEFT_TURNED, preferred_element_type=f32)
                grad_values = lax.dot_general(probs_low, grad, LEFT_TURNED, preferred_element_type=f32)
                for start, value in ((lane, grad_keys * SCALE), (lane + 256, grad_values)):
                    tmp[chunk, :, start : start + 128] += value[:128]
                    tmp[chunk + 1, 0:64, start : start + 128] += value[128:]
            return 0

        chunk_body(0, 0)
        tail_out[block] = tmp[0, 0:WINDOW].astype(bf16)
        to_y = jnp.where(block == 0, (p.y + 4 - first) % 4, p.y)
        slot = jnp.where(block == 0, first, 1 - first)
        tails.append(links.send(tail_out.at[block], tail_in.at[slot], p.at(y=to_y, z=(p.z + 3) % 4)))
        lax.fori_loop(1, 4, chunk_body, 0)
        last_kv[block] = tmp[4, 0:WINDOW]

        def store(i, _):
            x, core = block * 2 + i // 2, i % 2
            act[x, core, 0:64, 256:] = tmp[i, WINDOW:].astype(bf16)
            act[x, core, 64:128, 256:] = tmp[i + 1, 0:WINDOW].astype(bf16)
            return 0

        lax.fori_loop(0, 4, store, 0)

    pl.semaphore_wait(ready.at[0], 2)
    r_out.launch()
    load_qm.wait()
    g_branch.ready(1)
    g_branch.ready(2)

    grad_mixed(2 * p.xh)
    grad_mixed(2 * p.xh + 1)

    attend_back(p.xh)
    g_branch.share_far()
    r_out.pass_range(0, 1)
    w_gu.start2()
    g_branch.ready(3)
    grad_mixed(2 * (1 - p.xh))
    grad_mixed(2 * (1 - p.xh) + 1)
    attend_back(1 - p.xh)
    r_out.pass_range(1, 2)
    grads_into(wo, gb, mixed, 256)
    own[...] = gb[2 * p.xh, p.c].astype(f32)
    resid[...] = gb[2 * p.xh + 1, p.c].astype(f32)
    g_branch.sent()
    load_xr = links.local(xr_o, gb)
    for copy in tails:
        copy.wait_recv()
    for block in range(2):
        whole = last_kv[block] + tail_in[block].astype(f32)
        act[2 * block + 1, 1, pl.ds(64, 64), 256:] = whole.astype(bf16)
    w_d.start1()
    w_o = WeightReduce(links, p, wo, in_o, in2_o, fin_o, 128)
    w_o.start0()
    w_gu.start3()
    r_out.pass_range(2, 3)
    r_out.crossed()
    pl.semaphore_wait(ready.at[1], 3)
    again = [links.local(ref, raw) for ref, raw in raws[:3]]
    r_attn = block_reduce(3, partial_of(act, wq, 768), cot)
    r_attn.run(pass_on=False)
    r_out.pass_range(3, 4)
    w_d.start2()
    w_o.start1()
    load_xr.wait()
    grads_into(wq, gb, act, 768)
    w_q = WeightReduce(links, p, wq, in_q, in2_q, fin_q, 384)
    w_q.start0()
    r_attn.pass_range(0, 2)
    w_o.start2()
    r_out.finish()
    r_out.sent()

    def result_rows(i, _):
        tile, r = i // 8, pl.ds((i % 8) * 16, 16)
        nm[2 + tile, 0, r] = r_out.total(tile, r).astype(bf16)
        return 0

    lax.fori_loop(0, 16, result_rows, 0)
    b_out = BlockOut(links, p, nm.at[pl.ds(2, 2), 0], result_o)
    w_d.start3()
    w_q.start1()
    r_attn.pass_range(2, 3)
    w_o.start3()
    w_q.start2()
    r_attn.pass_range(3, 4)
    w_q.start3()
    r_attn.finish()

    for item in (w_gu, w_d, w_q, w_o):
        item.done()

    part_attn, part_mlp = jnp.zeros((64, 1), f32), jnp.zeros((64, 1), f32)
    for copy in again:
        copy.wait()
    for k in range(2):
        for i, raw in enumerate((raw_q, raw_k, raw_v)):
            part_attn += row_dots(raw[:, 256 * k : 256 * k + 256], fin_q[k, :, 256 * i : 256 * i + 256])
        for i, raw in enumerate((raw_g, raw_u)):
            start = 688 * k
            part_mlp += row_dots(raw[:, start : start + 640], fin_gu[k, :, 640 * i : 640 * i + 640])
            tail = slice(1280 + 64 * i, 1328 + 64 * i)
            part_mlp += row_dots(raw[:, start + 640 : start + 688], fin_gu[k, :, tail])
    lane = lax.broadcasted_iota(jnp.int32, (64, 128), 1)
    sums[...] = jnp.where(lane == 0, part_attn, jnp.where(lane == 1, part_mlp, 0.0))
    others = (sibling, beside, p.at(x=2 * p.xh + 1 - p.xl, c=1 - p.c))
    shared = [links.send(sums, sums_in.at[k], device) for k, device in enumerate(others)]
    stored = [
        links.local(fin, out)
        for fin, out in ((fin_gu, fin_gu_o), (fin_d, fin_d_o), (fin_q, fin_q_o), (fin_o, fin_o_o))
    ]
    def input_rows(i, _):
        tile, r = i // 8, pl.ds((i % 8) * 16, 16)
        values = hid_pair[tile, r].astype(f32)
        base = jnp.where(tile == 0, own[r], resid[r])
        hid_pair[tile, r] = (base + norm_back(r_attn.total(tile, r), values)).astype(bf16)
        return 0

    lax.fori_loop(0, 16, input_rows, 0)
    b_in = BlockOut(links, p, hid_pair, grad_o)
    for copy in shared:
        copy.wait_recv()
    links.settle(shared)
    sums[...] = (sums[...] + sums_in[0]) + (sums_in[1] + sums_in[2])
    stored.append(links.local(sums, sums_o))
    for copy in stored:
        copy.wait()
    b_out.done()
    b_in.done()
    r_attn.crossed()
    r_attn.sent()
    links.settle()


def block_call(lengths, gain_attn, gain_mlp, weights, hid, cot):
    sds = jax.ShapeDtypeStruct
    group = (4, 2, OWNED)
    vm = pltpu.VMEM
    outs = pl.pallas_call(
        block_kernel,
        out_shape=(
            sds((2, 2, OWNED, 2048), bf16),
            sds((2, 2, OWNED, 2048), bf16),
            sds((2, 64, 1408), bf16),
            sds((2, 64, 768), bf16),
            sds((2, 64, 768), bf16),
            sds((2, 64, 256), bf16),
            sds((64, 128), f32),
            sds(group + (2048,), bf16),
            sds(group + (512,), bf16),
        ),
        in_specs=[pl.BlockSpec(memory_space=pltpu.SMEM)] + [pl.BlockSpec(memory_space=pltpu.VMEM)] * 2 + [ANY] * 9,
        out_specs=[ANY] * 9,
        scratch_shapes=[
            vm((64, 1376), bf16),
            vm((64, 1376), bf16),
            vm((64, 1376), bf16),
            vm((2, 64, 1408), bf16),
            vm((2, 64, 768), bf16),
            vm((2, 64, 768), bf16),
            vm((2, 64, 256), bf16),
            vm((64, 128), f32),
            vm((3, 64, 128), f32),
            vm((4, 2, 4, 64, 768), bf16),
            vm((4, 2, 4, 64, 256), bf16),
            vm((4, 2, 4, 64, 1408), bf16),
            vm((4, 2, 4, 64, 768), bf16),
            vm(group + (2048,), bf16),
            vm(group + (2048,), bf16),
            vm(group + (768,), bf16),
            vm(group + (1408,), bf16),
            vm((2, BLOCK + WINDOW, 512), bf16),
            vm((OWNED, 2048), f32),
            vm((2, OWNED, 2048), bf16),
            vm((OWNED, 2048), f32),
            vm(group + (2048,), bf16),
            vm((2, WINDOW, 512), f32),
            vm((2, WINDOW, 512), bf16),
            vm((2, WINDOW, 512), bf16),
            vm((6, 4, 64, 1408), bf16),
            vm((6, 4, 64, 768), bf16),
            vm((6, 4, 64, 768), bf16),
            vm((6, 4, 64, 256), bf16),
            vm((6, 64, 1408), bf16),
            vm((6, 64, 768), bf16),
            vm((6, 64, 768), bf16),
            vm((6, 64, 256), bf16),
            vm((2, 4, OWNED, WIDE), bf16),
            vm((PIECES, 6, 64, WIDE), bf16),
            vm((5, OWNED, WIDE), f32),
            vm((PIECES, 4, OWNED, WIDE), bf16),
            vm((PIECES, 6, 64, WIDE), bf16),
            pltpu.SemaphoreType.DMA((220,)),
            pltpu.SemaphoreType.DMA((220,)),
            pltpu.SemaphoreType.DMA((32,)),
            pltpu.SemaphoreType.DMA((20 * PIECES,)),
            pltpu.SemaphoreType.DMA((20 * PIECES,)),
            pltpu.SemaphoreType.REGULAR((2,)),
        ],
        compiler_params=pltpu.CompilerParams(
            collective_id=0, has_side_effects=True, vmem_limit_bytes=60 * 2**20
        ),
        name="block",
    )(lengths, gain_attn, gain_mlp, *weights, hid.reshape(2, 2, OWNED, 2048), cot.reshape(2, 2, OWNED, 2048))
    return outs[:7]


def per_device(
    hidden_in,
    norm_gain_attn,
    w_query,
    w_key,
    w_value,
    w_out,
    norm_gain_mlp,
    w_gate,
    w_up,
    w_down,
    lengths,
    cotangent,
):
    outs = block_call(
        lengths,
        norm_gain_attn,
        norm_gain_mlp,
        (w_query, w_key, w_value, w_out.T, w_gate, w_up, w_down.T),
        hidden_in,
        cotangent,
    )
    return final_call(*outs, norm_gain_attn, norm_gain_mlp)


def solution(mesh):
    mesh = Mesh(mesh.devices.reshape(4, 2, 4, 2, 2), AXES)
    seq, head = ("y", "xh", "z"), ("xl", "c")
    rows, cols, flat, turned = P(seq, None), P(seq, head), P(seq), P(head, seq)
    return jax.shard_map(
        per_device,
        mesh=mesh,
        in_specs=(rows, flat, cols, cols, cols, turned, flat, cols, cols, turned, P(), rows),
        out_specs=(rows, rows, flat, cols, cols, cols, turned, flat, cols, cols, turned),
        check_vma=False,
    )
```
